32 devices in a mesh: section: 2 (over x), dp: 16 (over z, y, core).
Axes of the slice: x: 2, y: 2, z: 4, core: 2. Of those that a mesh axis runs over, the one named last changes fastest.
Arguments:
- block_in: bfloat16 [2, 32, 256, 768], P('section', 'dp'), may hold values from -6 to 6
- cotangent: bfloat16 [32, 256, 768], P('dp'), may hold values from -6 to 6
- lengths: int32 [32], P('dp'), may hold values from 63 to 256, as said below
- sources: int32 [32], P('dp'), may hold values from 0 to 2
- loss_weight: int32 [3], replicated, may hold values from 1 to 3
- gains: bfloat16 [2, 3, 768], P('section', None, 'dp'), may hold values from 0.5 to 1.5
- qkv_weight: bfloat16 [2, 768, 2304], P('section', 'dp'), may hold values from -0.21875 to 0.21875
- out_weight: bfloat16 [2, 768, 768], P('section', 'dp'), may hold values from -2.5 to 2.5
- cross_weight: bfloat16 [2, 768, 1536], P('section', 'dp'), may hold values from -2.5 to 2.5
- in_weight: bfloat16 [2, 768, 4096], P('section', 'dp'), may hold values from -0.21875 to 0.21875
- down_weight: bfloat16 [2, 2048, 768], P('section', 'dp'), may hold values from -0.125 to 0.125
Outputs:
- block_out: bfloat16 [2, 32, 256, 768], P('section', 'dp')
- input_grad: float32 [2, 32, 256, 768], P('section', 'dp')
- gains_grad: float32 [2, 3, 768], P('section', None, 'dp')
- qkv_grad: float32 [2, 768, 2304], P('section', 'dp')
- out_grad: float32 [2, 768, 768], P('section', 'dp')
- cross_grad: float32 [2, 768, 1536], P('section', 'dp')
- in_grad: float32 [2, 768, 4096], P('section', 'dp')
- down_grad: float32 [2, 2048, 768], P('section', 'dp')
The draws below stay inside these ranges and needn't reach their ends.
Inputs may be any that keep to these rules, and one draw needn't show every extreme that they name: `lengths`: in every draw some table has exactly 256 tokens.
All inputs are finite; a program needn't handle non-finite values.
Results may differ from the reference program's by a relative error of at most 0.015.
Values may be sent and summed in bfloat16 or wider, within the bound.
A program may use at most 384 MiB of HBM per device.

```python
import math
import jax
import jax.numpy as jnp
from jax import lax

D = 768
FF = 2048
HEADS = 12
HEAD_DIM = 64
SEQ = 256
TAB_DEV = 2
TABLES = 32


def draw_lengths(key, part):
    key = jax.random.fold_in(key, 11)
    first_key, second_key = jax.random.split(key)
    device = jnp.arange(TABLES, dtype=jnp.int32) // TAB_DEV
    groups = TABLES // TAB_DEV
    lowest = SEQ // 3
    upper = lowest + (SEQ - lowest) * device // max(groups - 1, 1)
    lower = upper * 3 // 4
    offset = jax.random.randint(first_key, (TABLES,), 0, 1 << 20, dtype=jnp.int32)
    drawn = lower + offset % (upper - lower + 1)
    chosen = TABLES - TAB_DEV + jax.random.randint(second_key, (), 0, TAB_DEV, dtype=jnp.int32)
    return jnp.where(jnp.arange(TABLES, dtype=jnp.int32) == chosen, SEQ, drawn).astype(jnp.int32)


def draw_cross_weight(key, part):
    key = jax.random.fold_in(key, 7)
    base = jnp.clip(jax.random.normal(key, (2, D, 2 * D), jnp.float32), -6.0, 6.0) * D ** (-0.5)
    slot = lax.broadcasted_iota(jnp.int32, (2, D, 2 * D), 0)
    column = lax.broadcasted_iota(jnp.int32, (2, D, 2 * D), 2)
    factor = jnp.where((slot == 1) & (column >= D), math.sqrt(SEQ / 2.0), 1.0)
    return (base * factor).astype(jnp.bfloat16)


def plant(array, own_key, low, largest):
    extent = array.shape
    spot = [jax.random.randint(jax.random.fold_in(own_key, axis), (), 0, extent[axis]) for axis in range(len(extent))]
    array = array.at[tuple(spot)].set(low)
    longest = extent.index(max(extent))
    spot[longest] = (spot[longest] + 1) % extent[longest]
    return array.at[tuple(spot)].set(largest)


def level_of(own_key, shape, shards, smallest, top_value):
    def one(dim, parts):
        draws = jax.random.uniform(jax.random.fold_in(jax.random.fold_in(own_key, 6), dim), (parts,), jnp.float32, smallest / len(shards), top_value / len(shards))
        return jnp.repeat(jnp.exp(draws), shape[dim] // parts).reshape((-1,) + (1,) * (len(shape) - dim - 1))

    level = one(*shards[0])
    for cut in shards[1:]:
        level = level * one(*cut)
    return level


def gaussian(stream_key, extent, deviation, limit, pieces=(), kind=jnp.bfloat16):
    gain = level_of(stream_key, extent, pieces, -0.22, 0.18) if pieces else 1.0
    array = jax.random.normal(stream_key, extent, jnp.float32) * deviation * gain
    return jnp.minimum(jnp.maximum(array, -limit), limit).astype(kind)


def setup_inputs(seed: int = 0) -> dict:
    seeds = jax.random.split(jax.random.key(seed), 12)
    return {
        "block_in": gaussian(seeds[0], (2, TABLES, SEQ, D), 1.0, 6.0, ((0, 2), (1, 16))),
        "cotangent": gaussian(seeds[1], (TABLES, SEQ, D), 1.0, 6.0, ((0, 16),)),
        "lengths": draw_lengths(jax.random.fold_in(seeds[11], 71), 0),
        "sources": plant(jax.random.randint(seeds[3], (TABLES,), 0, 3), jax.random.fold_in(seeds[3], 1), 0, 2).astype(jnp.int32),
        "loss_weight": jax.random.randint(seeds[4], (3,), 1, 4).astype(jnp.int32),
        "gains": jnp.clip(1.0 + 0.1 * jax.random.normal(seeds[5], (2, 3, D), jnp.float32), 0.5, 1.5).astype(jnp.bfloat16),
        "qkv_weight": gaussian(seeds[6], (2, D, 3 * D), D ** -0.5, 0.21875, ((0, 2), (1, 16))),
        "out_weight": gaussian(seeds[7], (2, D, D), (max(1, 2 * D // SEQ)) ** -0.5, 2.5, ((0, 2), (1, 16))),
        "cross_weight": draw_cross_weight(jax.random.fold_in(seeds[11], 71), 0),
        "in_weight": gaussian(seeds[9], (2, D, 2 * FF), D ** -0.5, 0.21875, ((0, 2), (1, 16))),
        "down_weight": gaussian(seeds[10], (2, FF, D), FF ** -0.5, 0.125, ((0, 2), (1, 16))),
    }


EPS = 1e-06
NEG = -1000000000.0

@jax.custom_vjp
def low(v):
    return lax.optimization_barrier(v.astype(jnp.bfloat16)).astype(jnp.float32)

@jax.custom_vjp
def low_back(v):
    return v

def low_keep(v):
    return (low(v), None)

def low_pass(kept, grad):
    return (grad,)

def back_keep(v):
    return (v, None)

def back_low(kept, grad):
    return (low(grad),)
low.defvjp(low_keep, low_pass)
low_back.defvjp(back_keep, back_low)

def matmul(a, b):
    return jnp.dot(a, b, precision=lax.Precision.HIGHEST)

def rms_norm(h, norm_gain):
    return h * lax.rsqrt(lax.optimization_barrier(jnp.mean(h * h, axis=-1, keepdims=True)) + EPS) * norm_gain

def attend(q, k, v, key_mask):
    rows_query = q.shape[0]
    heads_q = q.reshape(rows_query, HEADS, -1)
    heads_k = k.reshape(k.shape[0], HEADS, -1)
    heads_v = v.reshape(v.shape[0], HEADS, -1)
    scores = jnp.einsum('qhd,khd->hqk', heads_q, heads_k, precision=lax.Precision.HIGHEST) * HEAD_DIM ** (-0.5)
    scores = low_back(scores)
    if key_mask is not None:
        scores = jnp.where(key_mask[None], scores, NEG)
    weights = low(jax.nn.softmax(scores, axis=-1))
    output = jnp.einsum('hqk,khd->qhd', weights, heads_v, precision=lax.Precision.HIGHEST).reshape(rows_query, -1)
    return low(low_back(output))

def attn_branch(h, norm_gain, w_qkv, w_out, key_mask):
    normed = low(rms_norm(h, norm_gain))
    joined = low(low_back(matmul(normed, w_qkv)))
    q, k, v = jnp.split(joined, 3, axis=1)
    return low_back(matmul(attend(q, k, v, key_mask), w_out))

def mlp_branch(h, norm_gain, w_in, w_down):
    normed = low(rms_norm(h, norm_gain))
    joined = low_back(matmul(normed, w_in))
    gate, upper = jnp.split(joined, 2, axis=1)
    hidden = low(jax.nn.gelu(gate, approximate=True) * upper)
    return low_back(matmul(hidden, w_down))

def pair_loss(gains, w_qkv, w_out, w_cross, w_in, w_down, plot, table, weight_cot, length, factor):
    h = plot
    h = h + attn_branch(h, gains[0, 0], w_qkv[0], w_out[0], None)
    h = h + mlp_branch(h, gains[0, 1], w_in[0], w_down[0])
    memory = low(rms_norm(h, gains[0, 2]))
    key_value = low(low_back(matmul(memory, w_cross[0])))
    mem_keys, mem_values = jnp.split(key_value, 2, axis=1)
    position = jnp.arange(table.shape[0], dtype=jnp.int32)
    is_valid = position < length
    key_mask = (position[None, :] <= position[:, None]) & is_valid[None, :]
    y = table
    y = y + attn_branch(y, gains[1, 0], w_qkv[1], w_out[1], key_mask)
    normed = low(rms_norm(y, gains[1, 1]))
    w_query, w_back = jnp.split(w_cross[1], 2, axis=1)
    queries = low(low_back(matmul(normed, w_query)))
    y = y + low_back(matmul(attend(queries, mem_keys, mem_values, None), w_back))
    y = y + mlp_branch(y, gains[1, 2], w_in[1], w_down[1])
    loss = factor * jnp.sum(jnp.where(is_valid[:, None], weight_cot * y, 0.0))
    return (loss, (memory, y))

def reference(block_in, cotangent, lengths, sources, loss_weight, gains, qkv_weight, out_weight, cross_weight, in_weight, down_weight):
    weights = tuple((w.astype(jnp.float32) for w in (gains, qkv_weight, out_weight, cross_weight, in_weight, down_weight)))
    onehot = (sources[:, None] == jnp.arange(3, dtype=jnp.int32)[None, :]).astype(jnp.float32)
    counts = lax.optimization_barrier(jnp.sum(onehot * lengths[:, None].astype(jnp.float32), axis=0))
    own_count = lax.optimization_barrier(jnp.sum(onehot * counts[None, :], axis=1))
    own_weight = lax.optimization_barrier(jnp.sum(onehot * loss_weight[None, :].astype(jnp.float32), axis=1))
    scale = own_weight * (TABLES * SEQ / 3.0) / own_count

    def step(totals, item):
        plot, table, weight_cot, length, factor = item

        def loss_of(*primals):
            return pair_loss(*primals, weight_cot, length, factor)
        loss, back, extra = jax.vjp(loss_of, *weights, plot, table, has_aux=True)
        grads = back(jnp.ones_like(loss))
        totals = tuple((a + b for a, b in zip(totals, grads[:6])))
        return (totals, (extra[0].astype(jnp.bfloat16), extra[1].astype(jnp.bfloat16), grads[6], grads[7]))
    start = tuple((jnp.zeros_like(w) for w in weights))
    items = (block_in[0].astype(jnp.float32), block_in[1].astype(jnp.float32), cotangent.astype(jnp.float32), lengths, scale)
    totals, (memory, decoded, plot_grad, table_grad) = lax.scan(step, start, items)
    block_out = jnp.stack([memory, decoded])
    input_grad = jnp.stack([plot_grad, table_grad]).astype(jnp.float32)
    return (block_out, input_grad, totals[0], totals[1], totals[2], totals[3], totals[4], totals[5])
```

```python
from functools import partial

import jax
import jax.numpy as jnp
from jax import lax
from jax.experimental import pallas as pl
from jax.experimental.pallas import tpu as pltpu
from jax.sharding import PartitionSpec as P

HEADS = 12
HEAD_DIM = 64


EPS = 1e-06
NEG = -1000000000.0


def shifted(block, axis, distance):
    devices = range(lax.axis_size(axis))
    route = [(i - distance, i) for i in devices if i - distance in devices]
    return lax.ppermute(block, axis, route)


def product(a, b):
    return jnp.dot(a, b, preferred_element_type=jnp.float32)


def split_heads(v):
    return v.reshape(v.shape[0], HEADS, -1)


def norm_forward(h, norm_gain):
    inv_root = lax.rsqrt(jnp.mean(h * h, axis=-1, keepdims=True) + EPS)
    return (h * inv_root * norm_gain.astype(jnp.float32), inv_root)


def norm_back(d_normed, h, inv_root, norm_gain):
    scaled = h * inv_root
    d_gain = jnp.sum(d_normed * scaled, axis=0)
    inner = d_normed * norm_gain.astype(jnp.float32)
    d_input = inv_root * (inner - scaled * jnp.mean(inner * scaled, axis=-1, keepdims=True))
    return (d_input, d_gain)


def score_block(q, k, key_mask):
    scores = jnp.einsum(
        "qhd,khd->hqk", split_heads(q), split_heads(k), preferred_element_type=jnp.float32
    ) * HEAD_DIM ** (-0.5)
    if key_mask is not None:
        scores = jnp.where(key_mask[None], scores, NEG)
    return scores


def attend_forward(q, k, v, key_mask):
    scores = score_block(q, k, key_mask)
    highest = jnp.max(scores, axis=-1, keepdims=True)
    expo = jnp.exp(scores - highest)
    total = jnp.sum(expo, axis=-1, keepdims=True)
    weights = (expo / total).astype(jnp.bfloat16)
    output = jnp.einsum("hqk,khd->qhd", weights, split_heads(v), preferred_element_type=jnp.float32)
    return (output.reshape(q.shape[0], -1), highest + jnp.log(total))


def attend_back(q, k, v, key_mask, log_total, d_out):
    scores = score_block(q, k, key_mask)
    probs = jnp.exp(scores - log_total)
    heads_dout = split_heads(d_out)
    d_value = jnp.einsum(
        "hqk,qhd->khd", probs.astype(jnp.bfloat16), heads_dout, preferred_element_type=jnp.float32
    )
    d_probs = jnp.einsum(
        "qhd,khd->hqk", heads_dout, split_heads(v), preferred_element_type=jnp.float32
    )
    centre = jnp.sum(probs * d_probs, axis=-1, keepdims=True)
    d_scores = (probs * (d_probs - centre)).astype(jnp.bfloat16)
    d_query = jnp.einsum(
        "hqk,khd->qhd", d_scores, split_heads(k), preferred_element_type=jnp.float32
    ) * HEAD_DIM ** (-0.5)
    d_key = jnp.einsum(
        "hqk,qhd->khd", d_scores, split_heads(q), preferred_element_type=jnp.float32
    ) * HEAD_DIM ** (-0.5)
    rows_query = q.shape[0]
    rows_key = k.shape[0]
    return (
        d_query.reshape(rows_query, -1),
        d_key.reshape(rows_key, -1),
        d_value.reshape(rows_key, -1),
    )


def attention_forward(h, norm_gain, w_qkv, w_out, key_mask):
    normed, inv_root = norm_forward(h, norm_gain)
    normed_low = normed.astype(jnp.bfloat16)
    joined = product(normed_low, w_qkv).astype(jnp.bfloat16)
    q, k, v = jnp.split(joined, 3, axis=1)
    output, log_total = attend_forward(q, k, v, key_mask)
    output_low = output.astype(jnp.bfloat16)
    return (normed_low, inv_root, joined, output_low, log_total, product(output_low, w_out))


def attention_back(d_h, h, saved, norm_gain, w_qkv, w_out, key_mask):
    normed_low, inv_root, joined, output_low, log_total, unused = saved
    d_low = d_h.astype(jnp.bfloat16)
    d_wout = product(output_low.T, d_low)
    d_output = product(d_low, w_out.T).astype(jnp.bfloat16)
    q, k, v = jnp.split(joined, 3, axis=1)
    d_query, d_key, d_value = attend_back(q, k, v, key_mask, log_total, d_output)
    d_joined = jnp.concatenate([d_query, d_key, d_value], axis=1).astype(jnp.bfloat16)
    d_wqkv = product(normed_low.T, d_joined)
    d_normed = product(d_joined, w_qkv.T)
    d_input, d_gain = norm_back(d_normed, h, inv_root, norm_gain)
    return (d_input, d_gain, d_wqkv, d_wout)


def mlp_forward(h, norm_gain, w_in, w_down):
    normed, inv_root = norm_forward(h, norm_gain)
    normed_low = normed.astype(jnp.bfloat16)
    joined = product(normed_low, w_in)
    gate, upper = jnp.split(joined, 2, axis=1)
    hidden_low = (jax.nn.gelu(gate, approximate=True) * upper).astype(jnp.bfloat16)
    return (normed_low, inv_root, joined, hidden_low, product(hidden_low, w_down))


def mlp_back(d_h, h, saved, norm_gain, w_in, w_down):
    normed_low, inv_root, joined, hidden_low, unused = saved
    d_low = d_h.astype(jnp.bfloat16)
    d_wdown = product(hidden_low.T, d_low)
    d_hidden = product(d_low, w_down.T)
    gate, upper = jnp.split(joined, 2, axis=1)
    active, active_back = jax.vjp(partial(jax.nn.gelu, approximate=True), gate)
    d_gate = active_back(d_hidden * upper)[0]
    d_upper = d_hidden * active
    d_joined = jnp.concatenate([d_gate, d_upper], axis=1).astype(jnp.bfloat16)
    d_win = product(normed_low.T, d_joined)
    d_normed = product(d_joined, w_in.T)
    d_input, d_gain = norm_back(d_normed, h, inv_root, norm_gain)
    return (d_input, d_gain, d_win, d_wdown)


def encoder_forward(weights, source):
    gains, w_qkv, w_out, w_cross, w_in, w_down = weights
    inputs = source.astype(jnp.float32)
    attn_saved = attention_forward(inputs, gains[0], w_qkv, w_out, None)
    middle = inputs + attn_saved[-1]
    mlp_saved = mlp_forward(middle, gains[1], w_in, w_down)
    final = middle + mlp_saved[-1]
    normed, inv_root = norm_forward(final, gains[2])
    memory = normed.astype(jnp.bfloat16)
    key_value = product(memory, w_cross).astype(jnp.bfloat16)
    return (inputs, attn_saved, middle, mlp_saved, final, inv_root, memory, key_value)


def encoder_front(weights, source):
    saved = encoder_forward(weights, source)
    return (saved[7], saved[6])


def encoder_back_saved(weights, saved, d_keyvalue):
    gains, w_qkv, w_out, w_cross, w_in, w_down = weights
    inputs, attn_saved, middle, mlp_saved, final, inv_root, memory, key_value = saved
    d_wcross = product(memory.T, d_keyvalue)
    d_memory = product(d_keyvalue, w_cross.T)
    d_final, gain_last = norm_back(d_memory, final, inv_root, gains[2])
    d_part, gain_mlp, d_win, d_wdown = mlp_back(d_final, middle, mlp_saved, gains[1], w_in, w_down)
    d_middle = d_final + d_part
    d_first, gain_attn, d_wqkv, d_wout = attention_back(
        d_middle, inputs, attn_saved, gains[0], w_qkv, w_out, None
    )
    grads = (jnp.stack([gain_attn, gain_mlp, gain_last]), d_wqkv, d_wout, d_wcross, d_win, d_wdown)
    return (d_middle + d_first, grads)


def encoder_back(weights, source, d_keyvalue):
    return encoder_back_saved(weights, encoder_forward(weights, source), d_keyvalue)


def decoder_pass(weights, source, key_value, weight_cot, length, factor):
    gains, w_qkv, w_out, w_cross, w_in, w_down = weights
    width = source.shape[1]
    inputs = source.astype(jnp.float32)
    position = jnp.arange(inputs.shape[0], dtype=jnp.int32)
    is_valid = position < length
    key_mask = (position[None, :] <= position[:, None]) & is_valid[None, :]
    attn_saved = attention_forward(inputs, gains[0], w_qkv, w_out, key_mask)
    middle = inputs + attn_saved[-1]
    normed, inv_root = norm_forward(middle, gains[1])
    normed_low = normed.astype(jnp.bfloat16)
    w_query = w_cross[:, :width]
    w_back = w_cross[:, width:]
    queries = product(normed_low, w_query).astype(jnp.bfloat16)
    mem_keys = key_value[:, :width]
    mem_values = key_value[:, width:]
    cross_out, cross_total = attend_forward(queries, mem_keys, mem_values, None)
    cross_low = cross_out.astype(jnp.bfloat16)
    after = middle + product(cross_low, w_back)
    mlp_saved = mlp_forward(after, gains[2], w_in, w_down)
    final = after + mlp_saved[-1]
    d_final = jnp.where(is_valid[:, None], weight_cot.astype(jnp.float32) * factor, 0.0)
    d_part, gain_mlp, d_win, d_wdown = mlp_back(d_final, after, mlp_saved, gains[2], w_in, w_down)
    d_after = d_final + d_part
    d_low = d_after.astype(jnp.bfloat16)
    d_wback = product(cross_low.T, d_low)
    d_cross = product(d_low, w_back.T).astype(jnp.bfloat16)
    d_query, d_key, d_value = attend_back(queries, mem_keys, mem_values, None, cross_total, d_cross)
    d_query_low = d_query.astype(jnp.bfloat16)
    d_wquery = product(normed_low.T, d_query_low)
    d_normed = product(d_query_low, w_query.T)
    d_norm_in, gain_cross = norm_back(d_normed, middle, inv_root, gains[1])
    d_middle = d_after + d_norm_in
    d_keyvalue = jnp.concatenate([d_key, d_value], axis=1).astype(jnp.bfloat16)
    d_first, gain_attn, d_wqkv, d_wout = attention_back(
        d_middle, inputs, attn_saved, gains[0], w_qkv, w_out, key_mask
    )
    grads = (
        jnp.stack([gain_attn, gain_cross, gain_mlp]),
        d_wqkv,
        d_wout,
        jnp.concatenate([d_wquery, d_wback], axis=1),
        d_win,
        d_wdown,
    )
    return (final.astype(jnp.bfloat16), d_middle + d_first, d_keyvalue, grads)


def on_section(flag, work, operands):

    def run_work(values):
        return work(*values)

    def skip_work(values):
        return jax.tree.map(jnp.zeros_like, work(*values))

    return lax.cond(flag, run_work, skip_work, operands)


MESH = pl.DeviceIdType.MESH


def ring_position(chip, chips):
    return jnp.where(chip % 2 == 0, chip // 2, chips - 1 - chip // 2)


def ring_chip(position, chips):
    position = lax.rem(position + 2 * chips, chips)
    return jnp.where(position < chips // 2, 2 * position, 2 * (chips - 1 - position) + 1)


def ring_hops(index, chips):
    long, short = chips // 2, chips - 1 - chips // 2
    return (long, short) if index % 2 == 0 else (short, long)


def entry_barrier(partners):
    barrier = pltpu.get_barrier_semaphore()
    for partner in partners:
        pl.semaphore_signal(barrier, inc=1, device_id=partner, device_id_type=MESH)
    pl.semaphore_wait(barrier, len(partners))


def remote(src, dst, send_sem, recv_sem, target):
    return pltpu.make_async_remote_copy(
        src_ref=src,
        dst_ref=dst,
        send_sem=send_sem,
        recv_sem=recv_sem,
        device_id=target,
        device_id_type=MESH,
    )


def gather_kernel(wide, count, *refs):
    shards, fulls = refs[:count], refs[count : 2 * count]
    own_sem, ring_send, ring_recv, twin_send, twin_recv = refs[2 * count :]
    chips = wide // 2
    section, me = lax.axis_index("section"), lax.axis_index("dp")
    chip, core = me // 2, lax.rem(me, 2)
    place = ring_position(chip, chips)
    ahead = (section, 2 * ring_chip(place + 1, chips) + core)
    behind = (section, 2 * ring_chip(place - 1, chips) + core)
    twin = (section, 2 * chip + 1 - core)
    entry_barrier((ahead, behind, twin))

    def rows_of(index, origin_chip, origin_core):
        rows = shards[index].shape[0]
        start = pl.multiple_of((2 * origin_chip + origin_core) * rows, 16)
        return fulls[index].at[pl.ds(start, rows)]

    def ring_copy(index, way, hop):
        origin = ring_chip(place - hop if way == 0 else place + hop, chips)
        target = rows_of(index, origin, core)
        source = shards[index] if hop == 0 else target
        return remote(
            source, target, ring_send.at[index, way, hop], ring_recv.at[index, way, hop], ahead if way == 0 else behind
        )

    def twin_copy(index, way, hop):
        slot = 0 if hop == 0 else 1 + way * (chips // 2) + hop - 1
        origin = ring_chip(place - hop if way == 0 else place + hop, chips)
        target = rows_of(index, origin, core)
        source = shards[index] if hop == 0 else target
        return remote(source, target, twin_send.at[index, slot], twin_recv.at[index, slot], twin)

    own = [pltpu.make_async_copy(shards[i], rows_of(i, chip, core), own_sem.at[i]) for i in range(count)]
    for i in range(count):
        for way in range(2):
            ring_copy(i, way, 0).start()
    for i in range(count):
        twin_copy(i, 0, 0).start()
        own[i].start()
    for hop in range(chips // 2):
        for i in range(count):
            for way in range(2):
                hops = ring_hops(i, chips)[way]
                if hop < hops:
                    ring_copy(i, way, hop).wait_recv()
                    if hop + 1 < hops:
                        ring_copy(i, way, hop + 1).start()
                    twin_copy(i, way, hop + 1).start()
    for i in range(count):
        own[i].wait()
        twin_copy(i, 0, 0).wait()
        for way in range(2):
            for hop in range(ring_hops(i, chips)[way]):
                twin_copy(i, way, hop + 1).wait()
                ring_copy(i, way, hop).wait_send()


def gather_weights(wide, shards):
    count, chips = len(shards), wide // 2
    return pl.pallas_call(
        partial(gather_kernel, wide, count),
        out_shape=[jax.ShapeDtypeStruct((wide * s.shape[0], s.shape[1]), s.dtype) for s in shards],
        in_specs=[pl.BlockSpec(memory_space=pl.ANY)] * count,
        out_specs=[pl.BlockSpec(memory_space=pl.ANY)] * count,
        scratch_shapes=[
            pltpu.SemaphoreType.DMA((count,)),
            pltpu.SemaphoreType.DMA((count, 2, chips // 2)),
            pltpu.SemaphoreType.DMA((count, 2, chips // 2)),
            pltpu.SemaphoreType.DMA((count, chips + 1)),
            pltpu.SemaphoreType.DMA((count, chips + 1)),
        ],
        name="gather_weights",
        compiler_params=pltpu.CompilerParams(collective_id=0, has_side_effects=True),
    )(*shards)


def reduce_kernel(wide, count, *refs):
    grads, outs = refs[:count], refs[count : 2 * count]
    blocks, twins, arrived = (refs[(2 + n) * count : (3 + n) * count] for n in range(3))
    load_sem, twin_send, twin_recv, ring_send, ring_recv = refs[5 * count :]
    chips = wide // 2
    section, me = lax.axis_index("section"), lax.axis_index("dp")
    chip, core = me // 2, lax.rem(me, 2)
    place = ring_position(chip, chips)
    ahead = (section, 2 * ring_chip(place + 1, chips) + core)
    behind = (section, 2 * ring_chip(place - 1, chips) + core)
    twin = (section, 2 * chip + 1 - core)
    entry_barrier((ahead, behind, twin))

    def offset_chip(way, distance):
        return ring_chip(place + distance if way == 0 else place - distance, chips)

    def rows_of(index, to_chip, to_core):
        rows = outs[index].shape[0]
        start = pl.multiple_of((2 * to_chip + to_core) * rows, 16)
        return grads[index].at[pl.ds(start, rows)]

    def twin_copy(index, way, distance):
        slot = 0 if distance == 0 else 1 + way * (chips // 2) + distance - 1
        return remote(
            rows_of(index, offset_chip(way, distance), 1 - core),
            twins[index].at[slot],
            twin_send.at[index, slot],
            twin_recv.at[index, slot],
            twin,
        )

    def load_copy(index, way, distance):
        slot = 0 if distance == 0 else 1 + way * (chips // 2) + distance - 1
        return pltpu.make_async_copy(
            rows_of(index, offset_chip(way, distance), core), blocks[index].at[slot], load_sem.at[index, slot]
        )

    def ring_copy(index, way, hop):
        distance = ring_hops(index, chips)[way] - hop
        slot = 1 + way * (chips // 2) + distance - 1
        return remote(
            blocks[index].at[slot],
            arrived[index].at[way, hop],
            ring_send.at[index, way, hop],
            ring_recv.at[index, way, hop],
            ahead if way == 0 else behind,
        )

    for hop in range(chips // 2 + 1):
        for i in range(count):
            for way in range(2):
                distance = ring_hops(i, chips)[way] - hop
                if distance > 0 or (distance == 0 and ring_hops(i, chips)[way] == chips // 2):
                    twin_copy(i, way, distance).start()
                    load_copy(i, way, distance).start()

    def summed(terms, out):
        @pl.loop(0, out.shape[0] // 16)
        def _(group):
            rows = pl.ds(pl.multiple_of(group * 16, 16), 16)
            total = terms[0][rows].astype(jnp.float32)
            for term in terms[1:]:
                total += term[rows].astype(jnp.float32)
            out[rows] = total.astype(out.dtype)

    for hop in range(chips // 2):
        for i in range(count):
            for way in range(2):
                hops = ring_hops(i, chips)[way]
                distance = hops - hop
                if distance <= 0:
                    continue
                slot = 1 + way * (chips // 2) + distance - 1
                load_copy(i, way, distance).wait()
                twin_copy(i, way, distance).wait_recv()
                terms = [blocks[i].at[slot], twins[i].at[slot]]
                if hop > 0:
                    ring_copy(i, way, hop - 1).wait_recv()
                    terms.append(arrived[i].at[way, hop - 1])
                summed(terms, blocks[i].at[slot])
                ring_copy(i, way, hop).start()
    for i in range(count):
        load_copy(i, 0, 0).wait()
        twin_copy(i, 0, 0).wait_recv()
        terms = [blocks[i].at[0], twins[i].at[0]]
        for way in range(2):
            hops = ring_hops(i, chips)[way]
            ring_copy(i, way, hops - 1).wait_recv()
            terms.append(arrived[i].at[way, hops - 1])
        summed(terms, outs[i])
    for i in range(count):
        twin_copy(i, 0, 0).wait_send()
        for way in range(2):
            for hop in range(ring_hops(i, chips)[way]):
                ring_copy(i, way, hop).wait_send()
                twin_copy(i, way, hop + 1).wait_send()


def reduce_grads(wide, grads):
    count, chips = len(grads), wide // 2
    shapes = [(g.shape[0] // wide, g.shape[1]) for g in grads]
    return pl.pallas_call(
        partial(reduce_kernel, wide, count),
        out_shape=[jax.ShapeDtypeStruct(s, jnp.float32) for s in shapes],
        in_specs=[pl.BlockSpec(memory_space=pl.ANY)] * count,
        out_specs=[pl.BlockSpec(memory_space=pltpu.VMEM)] * count,
        scratch_shapes=[pltpu.VMEM((chips + 1,) + s, jnp.bfloat16) for s in shapes]
        + [pltpu.VMEM((chips + 1,) + s, jnp.bfloat16) for s in shapes]
        + [pltpu.VMEM((2, chips // 2) + s, jnp.bfloat16) for s in shapes]
        + [
            pltpu.SemaphoreType.DMA((count, chips + 1)),
            pltpu.SemaphoreType.DMA((count, chips + 1)),
            pltpu.SemaphoreType.DMA((count, chips + 1)),
            pltpu.SemaphoreType.DMA((count, 2, chips // 2)),
            pltpu.SemaphoreType.DMA((count, 2, chips // 2)),
        ],
        name="reduce_grads",
        compiler_params=pltpu.CompilerParams(
            collective_id=1, has_side_effects=True, vmem_limit_bytes=60 * 2**20
        ),
    )(*grads)


def body(
    block_in,
    cotangent,
    lengths,
    sources,
    loss_weight,
    gains,
    qkv_weight,
    out_weight,
    cross_weight,
    in_weight,
    down_weight,
):
    is_encoder = lax.axis_index("section") == 0
    is_decoder = jnp.logical_not(is_encoder)
    wide = lax.axis_size("dp")
    tiled = all(w.shape[1] % 16 == 0 for w in (qkv_weight, out_weight, cross_weight, in_weight, down_weight))
    shards = tuple((w[0] for w in (qkv_weight, out_weight, cross_weight, in_weight, down_weight)))
    gains_full = lax.all_gather(gains[0], "dp", axis=1, tiled=True)
    if tiled:
        weights = (gains_full, *gather_weights(wide, shards))
    else:
        weights = (gains_full, *(lax.all_gather(s, "dp", axis=0, tiled=True) for s in shards))
    onehot = (sources[:, None] == jnp.arange(3, dtype=jnp.int32)[None, :]).astype(jnp.float32)
    counts = lax.psum(jnp.sum(onehot * lengths[:, None].astype(jnp.float32), axis=0), "dp")
    own_count = jnp.sum(onehot * counts[None, :], axis=1)
    own_weight = jnp.sum(onehot * loss_weight[None, :].astype(jnp.float32), axis=1)
    scale = own_weight * (lengths.shape[0] * wide * block_in.shape[2] / 3.0) / own_count

    def step(carry, item):
        source, weight_cot, length, factor = item
        key_value, memory = on_section(is_encoder, encoder_front, (weights, source))
        received = shifted(key_value, "section", 1)
        decoded, table_grad, d_keyvalue, dec_grads = on_section(
            is_decoder, decoder_pass, (weights, source, received, weight_cot, length, factor)
        )
        returned = shifted(d_keyvalue, "section", -1)
        plot_grad, enc_grads = on_section(is_encoder, encoder_back, (weights, source, returned))
        grads = tuple((a + b for a, b in zip(dec_grads, enc_grads)))
        carry = tuple((a + b for a, b in zip(carry, grads)))
        return (carry, (memory + decoded, plot_grad + table_grad))

    start = tuple((jnp.zeros(w.shape, jnp.float32) for w in weights))
    carry, (outputs, input_grads) = lax.scan(step, start, (block_in[0], cotangent, lengths, scale))
    gains_reduced = lax.psum_scatter(carry[0], "dp", scatter_dimension=1, tiled=True)
    if tiled:
        sums = reduce_grads(wide, tuple((g.astype(jnp.bfloat16) for g in carry[1:])))
    else:
        sums = tuple((lax.psum_scatter(g, "dp", scatter_dimension=0, tiled=True) for g in carry[1:]))
    reduced = (gains_reduced[None], *(g[None] for g in sums))
    return (
        outputs[None],
        input_grads[None],
        reduced[0],
        reduced[1],
        reduced[2],
        reduced[3],
        reduced[4],
        reduced[5],
    )


def solution(mesh):
    in_specs = (
        P("section", "dp", None, None),
        P("dp", None, None),
        P("dp"),
        P("dp"),
        P(),
        P("section", None, "dp"),
        P("section", "dp", None),
        P("section", "dp", None),
        P("section", "dp", None),
        P("section", "dp", None),
        P("section", "dp", None),
    )
    out_specs = (
        P("section", "dp", None, None),
        P("section", "dp", None, None),
        P("section", None, "dp"),
        P("section", "dp", None),
        P("section", "dp", None),
        P("section", "dp", None),
        P("section", "dp", None),
        P("section", "dp", None),
    )
    return jax.shard_map(body, mesh=mesh, in_specs=in_specs, out_specs=out_specs, check_vma=False)
```

```python
from functools import partial

import jax
import jax.numpy as jnp
from jax import lax
from jax.experimental import pallas as pl
from jax.experimental.pallas import tpu as pltpu
from jax.sharding import PartitionSpec as P

HEADS = 12
HEAD_DIM = 64


EPS = 1e-06
NEG = -1000000000.0


MESH = pl.DeviceIdType.MESH
VMEM_LIMIT = 62 * 2**20
F32, BF16 = jnp.float32, jnp.bfloat16
ANY = pl.BlockSpec(memory_space=pl.ANY)
SMEM = pl.BlockSpec(memory_space=pltpu.SMEM)
VMEM = pl.BlockSpec(memory_space=pltpu.VMEM)


def ring_position(chip, chips):
    return jnp.where(chip % 2 == 0, chip // 2, chips - 1 - chip // 2)


def ring_chip(position, chips):
    position = lax.rem(position + 2 * chips, chips)
    return jnp.where(position < chips // 2, 2 * position, 2 * (chips - 1 - position) + 1)


def ring_hops(long_way, chips):
    long, short = chips // 2, chips - 1 - chips // 2
    return (long, short) if long_way == 0 else (short, long)


def slot_of(way, distance, chips):
    return 0 if distance == 0 else 1 + way * (chips // 2) + distance - 1


def entry_barrier(partners):
    barrier = pltpu.get_barrier_semaphore()
    for partner in partners:
        pl.semaphore_signal(barrier, inc=1, device_id=partner, device_id_type=MESH)
    pl.semaphore_wait(barrier, len(partners))


def remote(src, dst, send_sem, recv_sem, target):
    return pltpu.make_async_remote_copy(
        src_ref=src,
        dst_ref=dst,
        send_sem=send_sem,
        recv_sem=recv_sem,
        device_id=target,
        device_id_type=MESH,
    )


class Place:
    def __init__(self, wide):
        self.chips = wide // 2
        self.section, self.me = lax.axis_index("section"), lax.axis_index("dp")
        self.chip, self.core = self.me // 2, lax.rem(self.me, 2)
        self.spot = ring_position(self.chip, self.chips)
        self.ahead = (self.section, 2 * ring_chip(self.spot + 1, self.chips) + self.core)
        self.behind = (self.section, 2 * ring_chip(self.spot - 1, self.chips) + self.core)
        self.twin = (self.section, 2 * self.chip + 1 - self.core)
        self.across = (1 - self.section, self.me)

    def next_of(self, way):
        return self.ahead if way == 0 else self.behind

    def chip_at(self, way, distance):
        return ring_chip(self.spot + distance if way == 0 else self.spot - distance, self.chips)


def block_rows(ref, rows, chip, core):
    return ref.at[pl.ds(pl.multiple_of((2 * chip + core) * rows, rows), rows)]


class Gather:
    def __init__(self, place, names, shards, fulls, rows, long_way, sems):
        self.place, self.names = place, names
        self.shards, self.fulls, self.rows, self.long_way = shards, fulls, rows, long_way
        self.own_sem, self.ring_send, self.ring_recv, self.twin_send, self.twin_recv = sems

    def hops(self, name, way):
        return ring_hops(self.long_way[name], self.place.chips)[way]

    def pieces(self, name, way, hop):
        at = self.place
        origin = at.chip_at(way, -hop)
        target = block_rows(self.fulls[name], self.rows[name], origin, at.core)
        own = self.shards.get(name)
        return (own if hop == 0 and own is not None else target), target

    def ring(self, name, way, hop):
        source, target = self.pieces(name, way, hop)
        i = self.names.index(name)
        return remote(
            source, target, self.ring_send.at[i, way, hop], self.ring_recv.at[i, way, hop], self.place.next_of(way)
        )

    def pair(self, name, way, hop):
        source, target = self.pieces(name, way, hop)
        i, slot = self.names.index(name), slot_of(way, hop, self.place.chips)
        return remote(source, target, self.twin_send.at[i, slot], self.twin_recv.at[i, slot], self.place.twin)

    def own(self, name):
        source, target = self.pieces(name, 0, 0)
        return pltpu.make_async_copy(source, target, self.own_sem.at[self.names.index(name)])

    def start(self, name):
        for way in range(2):
            self.ring(name, way, 0).start()
        self.pair(name, 0, 0).start()
        if name in self.shards:
            self.own(name).start()

    def step(self, name, hop):
        for way in range(2):
            hops = self.hops(name, way)
            if hop < hops:
                self.ring(name, way, hop).wait_recv()
                if hop + 1 < hops:
                    self.ring(name, way, hop + 1).start()
                self.pair(name, way, hop + 1).start()

    def complete(self, name):
        if name in self.shards:
            self.own(name).wait()
        self.pair(name, 0, 0).wait_recv()
        for way in range(2):
            for hop in range(self.hops(name, way)):
                self.pair(name, way, hop + 1).wait_recv()

    def drain(self):
        for name in self.names:
            if name not in self.all_names:
                continue
            self.pair(name, 0, 0).wait_send()
            for way in range(2):
                for hop in range(self.hops(name, way)):
                    self.pair(name, way, hop + 1).wait_send()
                    self.ring(name, way, hop).wait_send()


GATHER_NAMES = ("gains", "counts", "qkv", "out", "crossE", "crossD", "in", "down")
LONG_WAY = {"gains": 0, "counts": 1, "qkv": 0, "out": 1, "crossE": 0, "crossD": 1, "in": 1, "down": 0}


def gather_kernel(wide, *refs):
    ins, outs, sems = refs[:7], refs[7:15], refs[15:]
    shards = dict(zip(("gains", "counts", "qkv", "out", "cross", "in", "down"), ins))
    fulls = dict(zip(GATHER_NAMES, outs))
    rows = {n: outs[i].shape[0] // wide for i, n in enumerate(GATHER_NAMES)}
    at = Place(wide)
    across_send, across_recv = sems[5], sems[6]
    entry_barrier((at.ahead, at.behind, at.twin, at.across))
    passed = remote(
        shards["cross"],
        block_rows(fulls["crossE"], rows["crossE"], at.chip, at.core),
        across_send,
        across_recv,
        at.across,
    )

    def run(names, own):
        gather = Gather(at, GATHER_NAMES, own, fulls, rows, LONG_WAY, sems[:5])
        gather.all_names = names
        for name in names:
            if name == "crossE":
                passed.wait_recv()
            gather.start(name)
        for hop in range(at.chips // 2):
            for name in names:
                gather.step(name, hop)
        for name in names:
            gather.complete(name)
        gather.drain()

    @pl.when(at.section == 0)
    def _():
        passed.start()
        names = ("gains", "counts", "qkv", "out", "in", "down")
        run(names, {n: shards[n] for n in names})
        passed.wait_send()

    @pl.when(at.section == 1)
    def _():
        names = ("gains", "counts", "qkv", "out", "crossD", "in", "down", "crossE")
        own = {n: shards[n] for n in names if n in shards}
        own["crossD"] = shards["cross"]
        run(names, own)


def gather_sems(count, chips):
    return [
        pltpu.SemaphoreType.DMA((count,)),
        pltpu.SemaphoreType.DMA((count, 2, chips // 2)),
        pltpu.SemaphoreType.DMA((count, 2, chips // 2)),
        pltpu.SemaphoreType.DMA((count, chips + 1)),
        pltpu.SemaphoreType.DMA((count, chips + 1)),
        pltpu.SemaphoreType.DMA,
        pltpu.SemaphoreType.DMA,
    ]


def gather_weights(wide, gains, counts, qkv, out, cross, inner, down):
    shards = (gains, counts, qkv, out, cross, inner, down)
    fulls = (gains, counts, qkv, out, cross, cross, inner, down)
    return pl.pallas_call(
        partial(gather_kernel, wide),
        out_shape=[jax.ShapeDtypeStruct((wide * s.shape[0], s.shape[1]), s.dtype) for s in fulls],
        in_specs=[ANY] * len(shards),
        out_specs=[ANY] * len(fulls),
        scratch_shapes=gather_sems(len(fulls), wide // 2),
        name="gather_weights",
        compiler_params=pltpu.CompilerParams(collective_id=0, has_side_effects=True),
    )(*shards)


class Scatter:
    def __init__(self, place, names, grads, rows, long_way, blocks, twins, arrived, sems):
        self.place, self.names, self.grads, self.rows, self.long_way = place, names, grads, rows, long_way
        self.blocks, self.twins, self.arrived = blocks, twins, arrived
        self.load_sem, self.twin_send, self.twin_recv, self.ring_send, self.ring_recv = sems

    def hops(self, name, way):
        return ring_hops(self.long_way[name], self.place.chips)[way]

    def pair(self, name, way, distance):
        at, i = self.place, self.names.index(name)
        slot = slot_of(way, distance, at.chips)
        source = block_rows(self.grads[name], self.rows[name], at.chip_at(way, distance), 1 - at.core)
        return remote(source, self.twins[name].at[slot], self.twin_send.at[i, slot], self.twin_recv.at[i, slot], at.twin)

    def load(self, name, way, distance):
        at, i = self.place, self.names.index(name)
        slot = slot_of(way, distance, at.chips)
        source = block_rows(self.grads[name], self.rows[name], at.chip_at(way, distance), at.core)
        return pltpu.make_async_copy(source, self.blocks[name].at[slot], self.load_sem.at[i, slot])

    def ring(self, name, way, hop):
        at, i = self.place, self.names.index(name)
        slot = slot_of(way, self.hops(name, way) - hop, at.chips)
        return remote(
            self.blocks[name].at[slot],
            self.arrived[name].at[way, hop],
            self.ring_send.at[i, way, hop],
            self.ring_recv.at[i, way, hop],
            at.next_of(way),
        )

    def slots(self, name):
        found = []
        for hop in range(self.place.chips // 2 + 1):
            for way in range(2):
                distance = self.hops(name, way) - hop
                if distance > 0 or (distance == 0 and way == self.long_way[name]):
                    found.append((way, distance))
        return found

    def start(self, name):
        for way, distance in self.slots(name):
            self.pair(name, way, distance).start()
            self.load(name, way, distance).start()

    def add(self, terms, out):
        group = 16 if out.shape[0] % 16 == 0 else out.shape[0]

        @pl.loop(0, out.shape[0] // group)
        def _(n):
            rows = pl.ds(pl.multiple_of(n * group, group), group)
            total = terms[0][rows].astype(F32)
            for term in terms[1:]:
                total += term[rows].astype(F32)
            out[rows] = total.astype(out.dtype)

    def step(self, name, way, hop):
        distance = self.hops(name, way) - hop
        if distance <= 0:
            return
        slot = slot_of(way, distance, self.place.chips)
        self.load(name, way, distance).wait()
        self.pair(name, way, distance).wait_recv()
        terms = [self.blocks[name].at[slot], self.twins[name].at[slot]]
        if hop > 0:
            self.ring(name, way, hop - 1).wait_recv()
            terms.append(self.arrived[name].at[way, hop - 1])
        self.add(terms, self.blocks[name].at[slot])
        self.ring(name, way, hop).start()

    def finish(self, name, out):
        self.load(name, self.long_way[name], 0).wait()
        self.pair(name, self.long_way[name], 0).wait_recv()
        terms = [self.blocks[name].at[0], self.twins[name].at[0]]
        for way in range(2):
            last = self.hops(name, way) - 1
            self.ring(name, way, last).wait_recv()
            terms.append(self.arrived[name].at[way, last])
        self.add(terms, out)

    def drain(self, name):
        for way, distance in self.slots(name):
            self.pair(name, way, distance).wait_send()
        for way in range(2):
            for hop in range(self.hops(name, way)):
                self.ring(name, way, hop).wait_send()


SCATTER_NAMES = ("down", "in", "crossD", "crossE", "out", "qkv", "gains")


def reduce_kernel(wide, *refs):
    count = len(SCATTER_NAMES)
    grads = dict(zip(SCATTER_NAMES, refs[:count]))
    outs = dict(zip(("down", "in", "cross", "out", "qkv", "gains"), refs[count : 2 * count - 1]))
    refs = refs[2 * count - 1 :]
    blocks, twins, arrived = (dict(zip(SCATTER_NAMES, refs[n * count : (n + 1) * count])) for n in range(3))
    passed_out, passed_in = refs[3 * count : 3 * count + 2]
    sems = refs[3 * count + 2 :]
    rows = {n: grads[n].shape[0] // wide for n in SCATTER_NAMES}
    at = Place(wide)
    entry_barrier((at.ahead, at.behind, at.twin, at.across))
    passed = remote(passed_out, passed_in, sems[5], sems[6], at.across)

    def run(names, results):
        scatter = Scatter(at, SCATTER_NAMES, grads, rows, LONG_WAY, blocks, twins, arrived, sems[:5])
        for name in names:
            scatter.start(name)
        for hop in range(at.chips // 2):
            for name in names:
                for way in range(2):
                    scatter.step(name, way, hop)
        for name in names:
            scatter.finish(name, results[name])
            if name == "crossE":
                passed.start()
        for name in names:
            scatter.drain(name)

    @pl.when(at.section == 0)
    def _():
        run(("down", "in", "out", "qkv", "gains"), outs)
        passed.wait_recv()
        outs["cross"][...] = passed_in[...]

    @pl.when(at.section == 1)
    def _():
        run(("crossE", "down", "in", "crossD", "out", "qkv", "gains"), {**outs, "crossD": outs["cross"], "crossE": passed_out})
        passed.wait_send()


def scatter_scratch(shapes, dtypes, chips):
    return (
        [pltpu.VMEM((chips + 1,) + s, d) for s, d in zip(shapes, dtypes)]
        + [pltpu.VMEM((chips + 1,) + s, d) for s, d in zip(shapes, dtypes)]
        + [pltpu.VMEM((2, chips // 2) + s, d) for s, d in zip(shapes, dtypes)]
    )


def scatter_sems(count, chips):
    return [
        pltpu.SemaphoreType.DMA((count, chips + 1)),
        pltpu.SemaphoreType.DMA((count, chips + 1)),
        pltpu.SemaphoreType.DMA((count, chips + 1)),
        pltpu.SemaphoreType.DMA((count, 2, chips // 2)),
        pltpu.SemaphoreType.DMA((count, 2, chips // 2)),
        pltpu.SemaphoreType.DMA,
        pltpu.SemaphoreType.DMA,
    ]


def reduce_grads(wide, grads):
    chips = wide // 2
    shapes = [(grads[n].shape[0] // wide, grads[n].shape[1]) for n in SCATTER_NAMES]
    dtypes = [grads[n].dtype for n in SCATTER_NAMES]
    of = dict(zip(SCATTER_NAMES, shapes))
    outs = [of["down"], of["in"], of["crossD"], of["out"], of["qkv"], of["gains"]]
    return pl.pallas_call(
        partial(reduce_kernel, wide),
        out_shape=[jax.ShapeDtypeStruct(s, F32) for s in outs],
        in_specs=[ANY] * len(shapes),
        out_specs=[VMEM] * len(outs),
        scratch_shapes=scatter_scratch(shapes, dtypes, chips)
        + [pltpu.VMEM(of["crossE"], F32), pltpu.VMEM(of["crossE"], F32)]
        + scatter_sems(len(shapes), chips),
        name="reduce_grads",
        compiler_params=pltpu.CompilerParams(collective_id=1, has_side_effects=True, vmem_limit_bytes=VMEM_LIMIT),
    )(*(grads[n] for n in SCATTER_NAMES))


def dot(a, b, over_a=1, over_b=0):
    return lax.dot_general(a, b, (((over_a,), (over_b,)), ((), ())), preferred_element_type=F32)


def span(start, size):
    return pl.ds(pl.multiple_of(start, size), size)


def each(total, tile, work):
    @pl.loop(0, total // tile)
    def _(n):
        work(span(n * tile, tile))


ROWS = 64


def norm_into(h_ref, gain, out_ref):
    def work(at):
        h = h_ref[at].astype(F32)
        inv_root = lax.rsqrt(jnp.mean(h * h, axis=-1, keepdims=True) + EPS)
        out_ref[at] = (h * inv_root * gain).astype(out_ref.dtype)

    each(h_ref.shape[0], ROWS, work)


def norm_back(dn_ref, h_ref, gain, gain_sum, row, finish):
    gain_sum[row] = jnp.zeros(gain_sum.shape[1:], F32)

    def work(at):
        h, dn = h_ref[at].astype(F32), dn_ref[at].astype(F32)
        inv_root = lax.rsqrt(jnp.mean(h * h, axis=-1, keepdims=True) + EPS)
        scaled = h * inv_root
        product = dn * scaled
        gain_sum[row] += jnp.sum(product.reshape(-1, 8, product.shape[1]), axis=0)
        inner = dn * gain
        finish(at, inv_root * (inner - scaled * jnp.mean(product * gain, axis=-1, keepdims=True)))

    each(h_ref.shape[0], ROWS, work)


def pair_columns(ref, rows, start, two):
    return ref[rows, span(start + two * 2 * HEAD_DIM, 2 * HEAD_DIM)]


def side_masks():
    lane = lax.broadcasted_iota(jnp.int32, (1, 2 * HEAD_DIM), 1)
    first = lane < HEAD_DIM
    return first, (first.astype(F32).astype(BF16), (1 - first.astype(F32)).astype(BF16))


def masked_scores(q, k, seq, length):
    scores = dot(q, k, 1, 1) * HEAD_DIM ** (-0.5)
    if length is not None:
        query = lax.broadcasted_iota(jnp.int32, (seq, seq), 0)
        key = lax.broadcasted_iota(jnp.int32, (seq, seq), 1)
        scores = jnp.where((key <= query) & (key < length), scores, NEG)
    return scores


def softmax(scores):
    expo = jnp.exp(scores - jnp.max(scores, axis=-1, keepdims=True))
    return expo * (1.0 / jnp.sum(expo, axis=-1, keepdims=True))


def attend(q_ref, q_at, k_ref, k_at, v_ref, v_at, out_ref, seq, lengths, probs_ref=None):
    pairs = q_ref.shape[0] // seq
    first, keeps = side_masks()

    @pl.loop(0, pairs * (HEADS // 2))
    def _(n):
        pair, two = n // (HEADS // 2), lax.rem(n, HEADS // 2)
        rows = span(pair * seq, seq)
        length = None if lengths is None else lengths[pair]
        q, k, v = (pair_columns(r, rows, a, two) for r, a in ((q_ref, q_at), (k_ref, k_at), (v_ref, v_at)))
        halves = []
        for side in range(2):
            probs = softmax(masked_scores(q * keeps[side], k, seq, length)).astype(BF16)
            if probs_ref is not None:
                probs_ref[2 * n + side] = probs
            halves.append(dot(probs, v))
        out_ref[rows, span(two * 2 * HEAD_DIM, 2 * HEAD_DIM)] = jnp.where(first, *halves).astype(BF16)


def attend_back(q_ref, q_at, k_ref, k_at, v_ref, v_at, do_ref, dq, dk, dv, seq, lengths, probs_ref=None):
    pairs = q_ref.shape[0] // seq
    first, keeps = side_masks()

    @pl.loop(0, pairs * (HEADS // 2))
    def _(n):
        pair, two = n // (HEADS // 2), lax.rem(n, HEADS // 2)
        rows = span(pair * seq, seq)
        length = None if lengths is None else lengths[pair]
        q, k, v = (pair_columns(r, rows, a, two) for r, a in ((q_ref, q_at), (k_ref, k_at), (v_ref, v_at)))
        d_out = pair_columns(do_ref, rows, 0, two)
        sides = []
        for side in range(2):
            if probs_ref is None:
                probs = softmax(masked_scores(q * keeps[side], k, seq, length))
                probs_low = probs.astype(BF16)
            else:
                probs_low = probs_ref[2 * n + side]
                probs = probs_low.astype(F32)
            d_probs = dot(d_out * keeps[side], v, 1, 1)
            centre = jnp.sum(probs * d_probs, axis=-1, keepdims=True)
            d_scores = (probs * (d_probs - centre)).astype(BF16)
            sides.append((dot(d_scores, k), dot(d_scores, q, 0, 0), dot(probs_low, d_out, 0, 0)))
        for (ref, start), both, factor in zip((dq, dk, dv), zip(*sides), (HEAD_DIM ** (-0.5), HEAD_DIM ** (-0.5), 1.0)):
            ref[rows, span(start + two * 2 * HEAD_DIM, 2 * HEAD_DIM)] = (jnp.where(first, *both) * factor).astype(BF16)


def gelu_parts(gate):
    root, cubic = 0.7978845608028654, 0.044715
    square = gate * gate
    bent = jnp.tanh(root * gate * (1.0 + cubic * square))
    half = 0.5 * (1.0 + bent)
    slope = half + 0.5 * gate * (1.0 - bent * bent) * root * (1.0 + 3.0 * cubic * square)
    return gate * half, slope


FF_TILE = 512


def mlp_forward(a_ref, w_in, w_down, into_ref, hidden_ref=None, slopes_ref=None):
    ff = w_in.shape[1] // 2

    @pl.loop(0, ff // FF_TILE)
    def _(n):
        gates, uppers = span(n * FF_TILE, FF_TILE), span(ff + n * FF_TILE, FF_TILE)
        gate, upper = dot(a_ref[...], w_in[:, gates]), dot(a_ref[...], w_in[:, uppers])
        active, slope = gelu_parts(gate)
        hidden = (active * upper).astype(BF16)
        if hidden_ref is not None:
            hidden_ref[:, gates] = hidden
            slopes_ref[:, gates] = (slope * upper).astype(BF16)
            slopes_ref[:, uppers] = active.astype(BF16)
        if w_down is not None:
            into_ref[...] += dot(hidden, w_down[gates, :])


def mlp_back(d_low, w_in, w_down, slopes_ref, dn_ref):
    ff = w_in.shape[1] // 2
    dn_ref[...] = jnp.zeros(dn_ref.shape, F32)

    @pl.loop(0, ff // FF_TILE)
    def _(n):
        gates, uppers = span(n * FF_TILE, FF_TILE), span(ff + n * FF_TILE, FF_TILE)
        d_hidden = dot(d_low[...], w_down[gates, :], 1, 1)
        d_gate = (d_hidden * slopes_ref[:, gates]).astype(BF16)
        d_upper = (d_hidden * slopes_ref[:, uppers]).astype(BF16)
        slopes_ref[:, gates], slopes_ref[:, uppers] = d_gate, d_upper
        dn_ref[...] += dot(d_gate, w_in[:, gates], 1, 1) + dot(d_upper, w_in[:, uppers], 1, 1)


def product_into(a_ref, w_ref, out_ref, tile, w_at=0, transposed=False):
    width = out_ref.shape[1]

    @pl.loop(0, width // tile)
    def _(n):
        if transposed:
            value = dot(a_ref[...], w_ref[span(w_at + n * tile, tile), :], 1, 1)
        else:
            value = dot(a_ref[...], w_ref[:, span(w_at + n * tile, tile)])
        out_ref[:, span(n * tile, tile)] = value.astype(out_ref.dtype)


def add_product(base_ref, a_ref, w, out_ref):
    out_ref[...] = base_ref[...].astype(F32) + dot(a_ref[...], w)


class Moves:
    def __init__(self, sems):
        self.sems, self.used = sems, 0

    def start(self, src, dst):
        copy = pltpu.make_async_copy(src, dst, self.sems.at[self.used])
        self.used += 1
        copy.start()
        return copy


def weight_grad(moves, a_ref, y_ref, grad_hbm, tile_rows, tile_columns, column_at=0):
    depth, width = a_ref.shape[1], y_ref.shape[1]

    def inner(stage):
        copies = []
        for i in range(depth // tile_rows):
            for j in range(width // tile_columns):
                n = len(copies)
                if n >= 2:
                    copies[n - 2].wait()
                rows, columns = pl.ds(i * tile_rows, tile_rows), pl.ds(j * tile_columns, tile_columns)
                stage[n % 2] = dot(a_ref[:, rows], y_ref[:, columns], 0, 0).astype(BF16)
                goal = grad_hbm.at[rows, pl.ds(column_at + j * tile_columns, tile_columns)]
                copies.append(moves.start(stage.at[n % 2], goal))
        for copy in copies[-2:]:
            copy.wait()

    pl.run_scoped(inner, pltpu.VMEM((2, tile_rows, tile_columns), BF16))


def forward_kernel(
    seq, lengths, x_in, gains_in, w_qkv_in, w_out_in, w_in_in, w_down_in,
    joined_out, attended_out, middle_out, final_out, memory_out, landed,
    w_qkv, w_out, w_in, w_down, x, gains, normed, joined, attended, middle, load_sem, send_sem, recv_sem,
):
    section, me = lax.axis_index("section"), lax.axis_index("dp")
    across = (1 - section, me)
    entry_barrier((across,))
    pairs = x.shape[0] // seq
    moves = Moves(load_sem)
    loads = [moves.start(a, b) for a, b in ((x_in, x), (gains_in, gains), (w_qkv_in, w_qkv), (w_out_in, w_out))]

    def to_dec(pair):
        rows = pl.ds(pair * seq, seq)
        return remote(memory_out.at[rows], landed.at[rows], send_sem.at[pair], recv_sem.at[pair], across)

    def attention(lengths):
        loads[0].wait()
        loads[1].wait()
        norm_into(x, gains[0:1], normed)
        loads[2].wait()
        product_into(normed, w_qkv, joined, 768)
        width = x.shape[1]
        attend(joined, 0, joined, width, joined, 2 * width, attended, seq, lengths)
        loads[3].wait()
        add_product(x, attended, w_out[...], middle)
        return [moves.start(a, b) for a, b in ((joined, joined_out), (attended, attended_out), (middle, middle_out))]

    @pl.when(section == 0)
    def _():
        later = [moves.start(a, b) for a, b in ((w_in_in, w_in), (w_down_in, w_down))]
        stores = attention(None)
        norm_into(middle, gains[1:2], normed)
        for copy in later + stores[2:]:
            copy.wait()
        mlp_forward(normed, w_in, w_down, middle)
        stores.append(moves.start(middle, final_out))
        norm_into(middle, gains[2:3], normed)
        store = moves.start(normed, memory_out)
        store.wait()
        for pair in range(pairs):
            to_dec(pair).start()
        for copy in stores[:2] + stores[3:]:
            copy.wait()
        for pair in range(pairs):
            to_dec(pair).wait_send()

    @pl.when(section == 1)
    def _():
        for copy in attention(lengths):
            copy.wait()
        for pair in range(pairs):
            to_dec(pair).wait_recv()


def forward(x, lengths, gains, w_qkv, w_out, w_in, w_down, seq):
    rows, width = x.shape
    vmem = pltpu.VMEM
    return pl.pallas_call(
        partial(forward_kernel, seq),
        out_shape=[
            jax.ShapeDtypeStruct((rows, w_qkv.shape[1]), BF16),
            jax.ShapeDtypeStruct((rows, width), BF16),
            jax.ShapeDtypeStruct((rows, width), F32),
            jax.ShapeDtypeStruct((rows, width), F32),
            jax.ShapeDtypeStruct((rows, width), BF16),
            jax.ShapeDtypeStruct((rows, width), BF16),
        ],
        in_specs=[SMEM] + [ANY] * 6,
        out_specs=[ANY] * 6,
        scratch_shapes=[vmem(w.shape, BF16) for w in (w_qkv, w_out, w_in, w_down)]
        + [
            vmem((rows, width), BF16),
            vmem(gains.shape, F32),
            vmem((rows, width), BF16),
            vmem((rows, w_qkv.shape[1]), BF16),
            vmem((rows, width), BF16),
            vmem((rows, width), F32),
            pltpu.SemaphoreType.DMA((16,)),
            pltpu.SemaphoreType.DMA((rows // seq,)),
            pltpu.SemaphoreType.DMA((rows // seq,)),
        ],
        name="forward",
        compiler_params=pltpu.CompilerParams(collective_id=2, has_side_effects=True, vmem_limit_bytes=VMEM_LIMIT),
    )(lengths, x, gains, w_qkv, w_out, w_in, w_down)


def backward_kernel(
    seq, lengths, factors, x_in, gains_in, cot_in, joined_in, attended_in, middle_in, final_in, memory_in, landed,
    w_qkv_in, w_out_in, w_enc_in, w_dec_in, w_in_in, w_down_in,
    block_out, input_out, gains_out, g_down, g_in, g_dec, g_enc, g_out, g_qkv, returned,
    gains, gain_sum, back, load_sem, send_sem, recv_sem,
):
    section, me = lax.axis_index("section"), lax.axis_index("dp")
    across = (1 - section, me)
    entry_barrier((across,))
    rows, width = x_in.shape
    pairs = rows // seq
    moves = Moves(load_sem)
    vmem = pltpu.VMEM
    wide = vmem((rows, width), F32)
    slim = vmem((rows, width), BF16)
    copy = moves.start(gains_in, gains)
    copy.wait()

    def to_enc(pair):
        at = pl.ds(pair * seq, seq)
        return remote(back.at[at], returned.at[at], send_sem.at[pair], recv_sem.at[pair], across)

    def self_back(lengths, d_middle, x, normed, d_low, w_qkv, w_out, joined, attended, d_attended, dn, row):
        each(rows, ROWS, lambda at: d_low.__setitem__(at, d_middle[at].astype(BF16)))
        weight_grad(moves, attended, d_low, g_out, 768, 768)
        product_into(d_low, w_out, d_attended, 768, transposed=True)
        attend_back(
            joined, 0, joined, width, joined, 2 * width, d_attended,
            (joined, 0), (joined, width), (joined, 2 * width), seq, lengths,
        )
        weight_grad(moves, normed, joined, g_qkv, 768, 768)
        product_into(joined, w_qkv, dn, 768, transposed=True)

        def finish(at, d_input):
            d_middle[at] = d_middle[at] + d_input

        norm_back(dn, x, gains[row : row + 1], gain_sum, row, finish)
        store = moves.start(d_middle, input_out)
        store.wait()

    def encoder(w_qkv, w_out, w_in, w_down, x, joined, attended, middle, final, normed, hidden, slopes, d_low, d_attended, dn, d_memory):
        loads = [
            moves.start(a, b)
            for a, b in (
                (middle_in, middle), (w_in_in, w_in), (final_in, final), (w_down_in, w_down), (x_in, x),
                (joined_in, joined), (attended_in, attended), (w_out_in, w_out), (w_qkv_in, w_qkv), (memory_in, block_out),
            )
        ]
        for load in loads:
            load.wait()
        norm_into(middle, gains[1:2], normed)
        mlp_forward(normed, w_in, None, None, hidden, slopes)
        for pair in range(pairs):
            to_enc(pair).wait_recv()
        load = moves.start(returned, d_memory)
        load.wait()

        def finish_final(at, d_input):
            final[at] = d_input
            d_low[at] = d_input.astype(BF16)

        norm_back(d_memory, final, gains[2:3], gain_sum, 2, finish_final)
        weight_grad(moves, hidden, d_low, g_down, 1024, 768)
        mlp_back(d_low, w_in, w_down, slopes, dn)
        weight_grad(moves, normed, slopes, g_in, 768, 1024)

        def finish_middle(at, d_input):
            final[at] = final[at] + d_input

        norm_back(dn, middle, gains[1:2], gain_sum, 1, finish_middle)
        norm_into(x, gains[0:1], normed)
        self_back(None, final, x, normed, d_low, w_qkv, w_out, joined, attended, d_attended, dn, 0)

    @pl.when(section == 0)
    def _():
        ff = w_down_in.shape[0]
        pl.run_scoped(
            encoder,
            vmem(w_qkv_in.shape, BF16), vmem(w_out_in.shape, BF16), vmem(w_in_in.shape, BF16), vmem(w_down_in.shape, BF16),
            slim, vmem((rows, 3 * width), BF16), slim, wide, wide, slim,
            vmem((rows, ff), BF16), vmem((rows, 2 * ff), BF16), slim, slim, wide, slim,
        )

    def middle_part(w_enc, w_dec, w_in, w_down, memory, cot, normed_a, queries, keyval, probs, crossed, after, normed_b, slopes, hidden, d_low, dn, d_low2, d_crossed, middle):
        loads = [
            moves.start(a, b)
            for a, b in (
                (middle_in, middle), (w_dec_in, w_dec), (landed, memory), (w_enc_in, w_enc),
                (w_in_in, w_in), (w_down_in, w_down), (cot_in, cot),
            )
        ]
        loads[0].wait()
        norm_into(middle, gains[1:2], normed_a)
        loads[1].wait()
        product_into(normed_a, w_dec, queries, 768)
        loads[2].wait()
        loads[3].wait()
        product_into(memory, w_enc, keyval, 768)
        attend(queries, 0, keyval, 0, keyval, width, crossed, seq, None, probs)
        add_product(middle, crossed, w_dec[:, width:], after)
        norm_into(after, gains[2:3], normed_b)
        for load in loads[4:]:
            load.wait()
        final = dn
        final[...] = after[...]
        mlp_forward(normed_b, w_in, w_down, final, hidden, slopes)

        @pl.loop(0, pairs * (seq // ROWS))
        def _(n):
            pair, group = n // (seq // ROWS), lax.rem(n, seq // ROWS)
            at = span(n * ROWS, ROWS)
            position = group * ROWS + lax.broadcasted_iota(jnp.int32, (ROWS, 1), 0)
            d_low2[at] = final[at].astype(BF16)
            d_final = jnp.where(position < lengths[pair], cot[at].astype(F32) * factors[pair], 0.0)
            dn[at] = d_final
            d_low[at] = d_final.astype(BF16)

        store = moves.start(d_low2, block_out)
        d_after = middle_grad = None
        return store

    def decoder_middle(w_enc, w_dec, w_in, w_down, memory, cot, normed_a, queries, keyval, probs, crossed, after, normed_b, slopes, hidden, d_low, dn, d_low2, d_crossed, middle, d_after):
        store = middle_part(w_enc, w_dec, w_in, w_down, memory, cot, normed_a, queries, keyval, probs, crossed, after, normed_b, slopes, hidden, d_low, dn, d_low2, d_crossed, middle)
        d_after[...] = dn[...]
        mlp_back(d_low, w_in, w_down, slopes, dn)
        store.wait()

        def finish_after(at, d_input):
            total = d_after[at] + d_input
            d_after[at] = total
            d_low2[at] = total.astype(BF16)

        norm_back(dn, after, gains[2:3], gain_sum, 2, finish_after)
        @pl.loop(0, 1)
        def _(n):
            d_crossed[...] = dot(d_low2[...], w_dec[:, width:], 1, 1).astype(BF16)

        d_queries, d_keyval = cot, keyval
        attend_back(
            queries, 0, keyval, 0, keyval, width, d_crossed, (d_queries, 0), (d_keyval, 0), (d_keyval, width), seq, None, probs
        )
        for pair in range(pairs):
            at = pl.ds(pair * seq, seq)
            back[at] = dot(d_keyval[at], w_enc[...], 1, 1).astype(BF16)
            to_enc(pair).start()
        @pl.loop(0, 1)
        def _(n):
            dn[...] = dot(d_queries[...], w_dec[:, :width], 1, 1)

        def finish_middle(at, d_input):
            d_after[at] = d_after[at] + d_input

        norm_back(dn, middle, gains[1:2], gain_sum, 1, finish_middle)
        weight_grad(moves, hidden, d_low, g_down, 1024, 768)
        weight_grad(moves, normed_b, slopes, g_in, 768, 1024)
        weight_grad(moves, normed_a, d_queries, g_dec, 768, 768)
        weight_grad(moves, crossed, d_low2, g_dec, 768, 768, column_at=width)
        weight_grad(moves, memory, d_keyval, g_enc, 768, 768)

    def decoder(d_after):
        ff = w_down_in.shape[0]
        pl.run_scoped(
            lambda *refs: decoder_middle(*refs, d_after),
            vmem(w_enc_in.shape, BF16), vmem(w_dec_in.shape, BF16), vmem(w_in_in.shape, BF16), vmem(w_down_in.shape, BF16),
            slim, slim, slim, slim, vmem((rows, 2 * width), BF16), vmem((pairs * HEADS, seq, seq), BF16), slim, wide, slim,
            vmem((rows, 2 * ff), BF16), vmem((rows, ff), BF16), slim, wide, slim, slim, wide,
        )

        def front(w_qkv, w_out, x, joined, attended, normed, d_low, d_attended, dn):
            loads = [
                moves.start(a, b)
                for a, b in ((x_in, x), (attended_in, attended), (w_out_in, w_out), (joined_in, joined), (w_qkv_in, w_qkv))
            ]
            for load in loads:
                load.wait()
            norm_into(x, gains[0:1], normed)
            self_back(lengths, d_after, x, normed, d_low, w_qkv, w_out, joined, attended, d_attended, dn, 0)

        pl.run_scoped(
            front,
            vmem(w_qkv_in.shape, BF16), vmem(w_out_in.shape, BF16),
            slim, vmem((rows, 3 * width), BF16), slim, slim, slim, slim, wide,
        )
        for pair in range(pairs):
            to_enc(pair).wait_send()

    @pl.when(section == 1)
    def _():
        pl.run_scoped(decoder, wide)

    for row in range(3):
        gains_out[row : row + 1] = jnp.sum(gain_sum[row], axis=0, keepdims=True)


def backward(seq, lengths, factors, x, gains, cot, saved, landed, weights):
    joined, attended, middle, final, memory = saved
    w_qkv, w_out, w_enc, w_dec, w_in, w_down = weights
    rows, width = x.shape
    args = (lengths, factors, x, gains, cot, joined, attended, middle, final, memory, landed, *weights)
    shaped = jax.ShapeDtypeStruct
    return pl.pallas_call(
        partial(backward_kernel, seq),
        out_shape=[shaped((rows, width), BF16), shaped((rows, width), F32), shaped(gains.shape, F32)]
        + [shaped(w.shape, BF16) for w in (w_down, w_in, w_dec, w_enc, w_out, w_qkv)]
        + [shaped((rows, width), BF16)],
        in_specs=[SMEM] * 2 + [ANY] * (len(args) - 2),
        out_specs=[ANY, ANY, VMEM] + [ANY] * 7,
        scratch_shapes=[
            pltpu.VMEM(gains.shape, F32),
            pltpu.VMEM((3, 8, width), F32),
            pltpu.VMEM((rows, width), BF16),
            pltpu.SemaphoreType.DMA((64,)),
            pltpu.SemaphoreType.DMA((rows // seq,)),
            pltpu.SemaphoreType.DMA((rows // seq,)),
        ],
        name="backward",
        compiler_params=pltpu.CompilerParams(collective_id=3, has_side_effects=True, vmem_limit_bytes=VMEM_LIMIT),
    )(*args)


def shifted(block, axis, distance):
    devices = range(lax.axis_size(axis))
    route = [(i - distance, i) for i in devices if i - distance in devices]
    return lax.ppermute(block, axis, route)


def plain_product(a, b):
    return jnp.dot(a, b, preferred_element_type=jnp.float32)


def plain_split_heads(v):
    return v.reshape(v.shape[0], HEADS, -1)


def plain_norm_forward(h, norm_gain):
    inv_root = lax.rsqrt(jnp.mean(h * h, axis=-1, keepdims=True) + EPS)
    return (h * inv_root * norm_gain.astype(jnp.float32), inv_root)


def plain_norm_back(d_normed, h, inv_root, norm_gain):
    scaled = h * inv_root
    d_gain = jnp.sum(d_normed * scaled, axis=0)
    inner = d_normed * norm_gain.astype(jnp.float32)
    d_input = inv_root * (inner - scaled * jnp.mean(inner * scaled, axis=-1, keepdims=True))
    return (d_input, d_gain)


def plain_score_block(q, k, key_mask):
    scores = jnp.einsum(
        "qhd,khd->hqk", plain_split_heads(q), plain_split_heads(k), preferred_element_type=jnp.float32
    ) * HEAD_DIM ** (-0.5)
    if key_mask is not None:
        scores = jnp.where(key_mask[None], scores, NEG)
    return scores


def plain_attend_forward(q, k, v, key_mask):
    scores = plain_score_block(q, k, key_mask)
    highest = jnp.max(scores, axis=-1, keepdims=True)
    expo = jnp.exp(scores - highest)
    total = jnp.sum(expo, axis=-1, keepdims=True)
    weights = (expo / total).astype(jnp.bfloat16)
    output = jnp.einsum("hqk,khd->qhd", weights, plain_split_heads(v), preferred_element_type=jnp.float32)
    return (output.reshape(q.shape[0], -1), highest + jnp.log(total))


def plain_attend_back(q, k, v, key_mask, log_total, d_out):
    scores = plain_score_block(q, k, key_mask)
    probs = jnp.exp(scores - log_total)
    heads_dout = plain_split_heads(d_out)
    d_value = jnp.einsum(
        "hqk,qhd->khd", probs.astype(jnp.bfloat16), heads_dout, preferred_element_type=jnp.float32
    )
    d_probs = jnp.einsum(
        "qhd,khd->hqk", heads_dout, plain_split_heads(v), preferred_element_type=jnp.float32
    )
    centre = jnp.sum(probs * d_probs, axis=-1, keepdims=True)
    d_scores = (probs * (d_probs - centre)).astype(jnp.bfloat16)
    d_query = jnp.einsum(
        "hqk,khd->qhd", d_scores, plain_split_heads(k), preferred_element_type=jnp.float32
    ) * HEAD_DIM ** (-0.5)
    d_key = jnp.einsum(
        "hqk,qhd->khd", d_scores, plain_split_heads(q), preferred_element_type=jnp.float32
    ) * HEAD_DIM ** (-0.5)
    rows_query = q.shape[0]
    rows_key = k.shape[0]
    return (
        d_query.reshape(rows_query, -1),
        d_key.reshape(rows_key, -1),
        d_value.reshape(rows_key, -1),
    )


def plain_attention_forward(h, norm_gain, w_qkv, w_out, key_mask):
    normed, inv_root = plain_norm_forward(h, norm_gain)
    normed_low = normed.astype(jnp.bfloat16)
    joined = plain_product(normed_low, w_qkv).astype(jnp.bfloat16)
    q, k, v = jnp.split(joined, 3, axis=1)
    output, log_total = plain_attend_forward(q, k, v, key_mask)
    output_low = output.astype(jnp.bfloat16)
    return (normed_low, inv_root, joined, output_low, log_total, plain_product(output_low, w_out))


def plain_attention_back(d_h, h, saved, norm_gain, w_qkv, w_out, key_mask):
    normed_low, inv_root, joined, output_low, log_total, unused = saved
    d_low = d_h.astype(jnp.bfloat16)
    d_wout = plain_product(output_low.T, d_low)
    d_output = plain_product(d_low, w_out.T).astype(jnp.bfloat16)
    q, k, v = jnp.split(joined, 3, axis=1)
    d_query, d_key, d_value = plain_attend_back(q, k, v, key_mask, log_total, d_output)
    d_joined = jnp.concatenate([d_query, d_key, d_value], axis=1).astype(jnp.bfloat16)
    d_wqkv = plain_product(normed_low.T, d_joined)
    d_normed = plain_product(d_joined, w_qkv.T)
    d_input, d_gain = plain_norm_back(d_normed, h, inv_root, norm_gain)
    return (d_input, d_gain, d_wqkv, d_wout)


def plain_mlp_forward(h, norm_gain, w_in, w_down):
    normed, inv_root = plain_norm_forward(h, norm_gain)
    normed_low = normed.astype(jnp.bfloat16)
    joined = plain_product(normed_low, w_in)
    gate, upper = jnp.split(joined, 2, axis=1)
    hidden_low = (jax.nn.gelu(gate, approximate=True) * upper).astype(jnp.bfloat16)
    return (normed_low, inv_root, joined, hidden_low, plain_product(hidden_low, w_down))


def plain_mlp_back(d_h, h, saved, norm_gain, w_in, w_down):
    normed_low, inv_root, joined, hidden_low, unused = saved
    d_low = d_h.astype(jnp.bfloat16)
    d_wdown = plain_product(hidden_low.T, d_low)
    d_hidden = plain_product(d_low, w_down.T)
    gate, upper = jnp.split(joined, 2, axis=1)
    active, active_back = jax.vjp(partial(jax.nn.gelu, approximate=True), gate)
    d_gate = active_back(d_hidden * upper)[0]
    d_upper = d_hidden * active
    d_joined = jnp.concatenate([d_gate, d_upper], axis=1).astype(jnp.bfloat16)
    d_win = plain_product(normed_low.T, d_joined)
    d_normed = plain_product(d_joined, w_in.T)
    d_input, d_gain = plain_norm_back(d_normed, h, inv_root, norm_gain)
    return (d_input, d_gain, d_win, d_wdown)


def encoder_forward(weights, source):
    gains, w_qkv, w_out, w_cross, w_in, w_down = weights
    inputs = source.astype(jnp.float32)
    attn_saved = plain_attention_forward(inputs, gains[0], w_qkv, w_out, None)
    middle = inputs + attn_saved[-1]
    mlp_saved = plain_mlp_forward(middle, gains[1], w_in, w_down)
    final = middle + mlp_saved[-1]
    normed, inv_root = plain_norm_forward(final, gains[2])
    memory = normed.astype(jnp.bfloat16)
    key_value = plain_product(memory, w_cross).astype(jnp.bfloat16)
    return (inputs, attn_saved, middle, mlp_saved, final, inv_root, memory, key_value)


def encoder_front(weights, source):
    saved = encoder_forward(weights, source)
    return (saved[7], saved[6])


def encoder_back_saved(weights, saved, d_keyvalue):
    gains, w_qkv, w_out, w_cross, w_in, w_down = weights
    inputs, attn_saved, middle, mlp_saved, final, inv_root, memory, key_value = saved
    d_wcross = plain_product(memory.T, d_keyvalue)
    d_memory = plain_product(d_keyvalue, w_cross.T)
    d_final, gain_last = plain_norm_back(d_memory, final, inv_root, gains[2])
    d_part, gain_mlp, d_win, d_wdown = plain_mlp_back(d_final, middle, mlp_saved, gains[1], w_in, w_down)
    d_middle = d_final + d_part
    d_first, gain_attn, d_wqkv, d_wout = plain_attention_back(
        d_middle, inputs, attn_saved, gains[0], w_qkv, w_out, None
    )
    grads = (jnp.stack([gain_attn, gain_mlp, gain_last]), d_wqkv, d_wout, d_wcross, d_win, d_wdown)
    return (d_middle + d_first, grads)


def encoder_back(weights, source, d_keyvalue):
    return encoder_back_saved(weights, encoder_forward(weights, source), d_keyvalue)


def decoder_pass(weights, source, key_value, weight_cot, length, factor):
    gains, w_qkv, w_out, w_cross, w_in, w_down = weights
    width = source.shape[1]
    inputs = source.astype(jnp.float32)
    position = jnp.arange(inputs.shape[0], dtype=jnp.int32)
    is_valid = position < length
    key_mask = (position[None, :] <= position[:, None]) & is_valid[None, :]
    attn_saved = plain_attention_forward(inputs, gains[0], w_qkv, w_out, key_mask)
    middle = inputs + attn_saved[-1]
    normed, inv_root = plain_norm_forward(middle, gains[1])
    normed_low = normed.astype(jnp.bfloat16)
    w_query = w_cross[:, :width]
    w_back = w_cross[:, width:]
    queries = plain_product(normed_low, w_query).astype(jnp.bfloat16)
    mem_keys = key_value[:, :width]
    mem_values = key_value[:, width:]
    cross_out, cross_total = plain_attend_forward(queries, mem_keys, mem_values, None)
    cross_low = cross_out.astype(jnp.bfloat16)
    after = middle + plain_product(cross_low, w_back)
    mlp_saved = plain_mlp_forward(after, gains[2], w_in, w_down)
    final = after + mlp_saved[-1]
    d_final = jnp.where(is_valid[:, None], weight_cot.astype(jnp.float32) * factor, 0.0)
    d_part, gain_mlp, d_win, d_wdown = plain_mlp_back(d_final, after, mlp_saved, gains[2], w_in, w_down)
    d_after = d_final + d_part
    d_low = d_after.astype(jnp.bfloat16)
    d_wback = plain_product(cross_low.T, d_low)
    d_cross = plain_product(d_low, w_back.T).astype(jnp.bfloat16)
    d_query, d_key, d_value = plain_attend_back(queries, mem_keys, mem_values, None, cross_total, d_cross)
    d_query_low = d_query.astype(jnp.bfloat16)
    d_wquery = plain_product(normed_low.T, d_query_low)
    d_normed = plain_product(d_query_low, w_query.T)
    d_norm_in, gain_cross = plain_norm_back(d_normed, middle, inv_root, gains[1])
    d_middle = d_after + d_norm_in
    d_keyvalue = jnp.concatenate([d_key, d_value], axis=1).astype(jnp.bfloat16)
    d_first, gain_attn, d_wqkv, d_wout = plain_attention_back(
        d_middle, inputs, attn_saved, gains[0], w_qkv, w_out, key_mask
    )
    grads = (
        jnp.stack([gain_attn, gain_cross, gain_mlp]),
        d_wqkv,
        d_wout,
        jnp.concatenate([d_wquery, d_wback], axis=1),
        d_win,
        d_wdown,
    )
    return (final.astype(jnp.bfloat16), d_middle + d_first, d_keyvalue, grads)


def on_section(flag, work, operands):

    def run_work(values):
        return work(*values)

    def skip_work(values):
        return jax.tree.map(jnp.zeros_like, work(*values))

    return lax.cond(flag, run_work, skip_work, operands)


def plain_body(
    block_in,
    cotangent,
    lengths,
    sources,
    loss_weight,
    gains,
    qkv_weight,
    out_weight,
    cross_weight,
    in_weight,
    down_weight,
):
    is_encoder = lax.axis_index("section") == 0
    is_decoder = jnp.logical_not(is_encoder)
    wide = lax.axis_size("dp")
    gathered = (
        lax.all_gather(gains, "dp", axis=2, tiled=True),
        lax.all_gather(qkv_weight, "dp", axis=1, tiled=True),
        lax.all_gather(out_weight, "dp", axis=1, tiled=True),
        lax.all_gather(cross_weight, "dp", axis=1, tiled=True),
        lax.all_gather(in_weight, "dp", axis=1, tiled=True),
        lax.all_gather(down_weight, "dp", axis=1, tiled=True),
    )
    weights = tuple((w[0] for w in gathered))
    onehot = (sources[:, None] == jnp.arange(3, dtype=jnp.int32)[None, :]).astype(jnp.float32)
    counts = lax.psum(jnp.sum(onehot * lengths[:, None].astype(jnp.float32), axis=0), "dp")
    own_count = jnp.sum(onehot * counts[None, :], axis=1)
    own_weight = jnp.sum(onehot * loss_weight[None, :].astype(jnp.float32), axis=1)
    scale = own_weight * (lengths.shape[0] * wide * block_in.shape[2] / 3.0) / own_count

    def step(carry, item):
        source, weight_cot, length, factor = item
        key_value, memory = on_section(is_encoder, encoder_front, (weights, source))
        received = shifted(key_value, "section", 1)
        decoded, table_grad, d_keyvalue, dec_grads = on_section(
            is_decoder, decoder_pass, (weights, source, received, weight_cot, length, factor)
        )
        returned = shifted(d_keyvalue, "section", -1)
        plot_grad, enc_grads = on_section(is_encoder, encoder_back, (weights, source, returned))
        grads = tuple((a + b for a, b in zip(dec_grads, enc_grads)))
        carry = tuple((a + b for a, b in zip(carry, grads)))
        return (carry, (memory + decoded, plot_grad + table_grad))

    start = tuple((jnp.zeros(w.shape, jnp.float32) for w in weights))
    carry, (outputs, input_grads) = lax.scan(step, start, (block_in[0], cotangent, lengths, scale))
    gain_total, qkv_total, out_total, cross_sum, in_total, down_total = carry
    reduced = (
        lax.psum_scatter(gain_total[None], "dp", scatter_dimension=2, tiled=True),
        lax.psum_scatter(qkv_total[None], "dp", scatter_dimension=1, tiled=True),
        lax.psum_scatter(out_total[None], "dp", scatter_dimension=1, tiled=True),
        lax.psum_scatter(cross_sum[None], "dp", scatter_dimension=1, tiled=True),
        lax.psum_scatter(in_total[None], "dp", scatter_dimension=1, tiled=True),
        lax.psum_scatter(down_total[None], "dp", scatter_dimension=1, tiled=True),
    )
    return (
        outputs[None],
        input_grads[None],
        reduced[0],
        reduced[1],
        reduced[2],
        reduced[3],
        reduced[4],
        reduced[5],
    )


def pad_block(block, rows, columns):
    return jnp.pad(block, ((0, rows - block.shape[0]), (0, columns - block.shape[1])))


def tiled_body(
    block_in, cotangent, lengths, sources, loss_weight, gains, qkv_weight, out_weight, cross_weight, in_weight, down_weight
):
    wide = lax.axis_size("dp")
    pairs, seq, width = block_in.shape[1:]
    own = gains.shape[2]
    onehot = (sources[:, None] == jnp.arange(3, dtype=jnp.int32)[None, :]).astype(jnp.float32)
    counted = jnp.sum(onehot * lengths[:, None].astype(jnp.float32), axis=0, keepdims=True)
    gains_wide, counts_wide, w_qkv, w_out, w_enc, w_dec, w_in, w_down = gather_weights(
        wide,
        pad_block(gains[0], 16, 128),
        pad_block(counted, 8, 128),
        qkv_weight[0],
        out_weight[0],
        cross_weight[0],
        in_weight[0],
        down_weight[0],
    )
    counts = jnp.sum(counts_wide.reshape(wide, 8, 128)[:, 0, :3], axis=0)
    gains_full = gains_wide.reshape(wide, 16, 128)[:, :8, :own].transpose(1, 0, 2).reshape(8, width).astype(jnp.float32)
    own_count = jnp.sum(onehot * counts[None, :], axis=1)
    own_weight = jnp.sum(onehot * loss_weight[None, :].astype(jnp.float32), axis=1)
    scale = own_weight * (pairs * wide * seq / 3.0) / own_count

    x = block_in.reshape(pairs * seq, width)
    *saved, landed = forward(x, lengths, gains_full, w_qkv, w_out, w_in, w_down, seq)
    block_out, input_grad, gains_part, g_down, g_in, g_dec, g_enc, g_out, g_qkv, _ = backward(
        seq, lengths, scale, x, gains_full, cotangent.reshape(pairs * seq, width), saved, landed,
        (w_qkv, w_out, w_enc, w_dec, w_in, w_down),
    )
    g_gains = gains_part.reshape(8, wide, own).transpose(1, 0, 2)
    g_gains = jnp.pad(g_gains, ((0, 0), (0, 0), (0, 128 - own))).reshape(wide * 8, 128)
    down, inner, cross, out, qkv, gains_sum = reduce_grads(
        wide,
        {"down": g_down, "in": g_in, "crossD": g_dec, "crossE": g_enc, "out": g_out, "qkv": g_qkv, "gains": g_gains},
    )
    return (
        block_out.reshape(block_in.shape),
        input_grad.reshape(block_in.shape),
        gains_sum[None, :3, :own],
        qkv[None],
        out[None],
        cross[None],
        inner[None],
        down[None],
    )


def solution(mesh):
    in_specs = (
        P("section", "dp", None, None),
        P("dp", None, None),
        P("dp"),
        P("dp"),
        P(),
        P("section", None, "dp"),
        P("section", "dp", None),
        P("section", "dp", None),
        P("section", "dp", None),
        P("section", "dp", None),
        P("section", "dp", None),
    )
    out_specs = (
        P("section", "dp", None, None),
        P("section", "dp", None, None),
        P("section", None, "dp"),
        P("section", "dp", None),
        P("section", "dp", None),
        P("section", "dp", None),
        P("section", "dp", None),
        P("section", "dp", None),
    )

    def body(*args):
        shards = args[6:]
        tiled = args[5].shape[2] <= 128 and all(w.shape[1] % 16 == 0 for w in shards)
        return (tiled_body if tiled else plain_body)(*args)

    return jax.shard_map(body, mesh=mesh, in_specs=in_specs, out_specs=out_specs, check_vma=False)
```

```python
from functools import partial

import jax
import jax.numpy as jnp
from jax import lax
from jax.experimental import pallas as pl
from jax.experimental.pallas import tpu as pltpu
from jax.sharding import PartitionSpec as P

HEADS = 12
HEAD_DIM = 64


EPS = 1e-06
NEG = -1000000000.0


MESH = pl.DeviceIdType.MESH
VMEM_LIMIT = 62 * 2**20
F32, BF16 = jnp.float32, jnp.bfloat16
ANY = pl.BlockSpec(memory_space=pl.ANY)
SMEM = pl.BlockSpec(memory_space=pltpu.SMEM)
VMEM = pl.BlockSpec(memory_space=pltpu.VMEM)


def ring_position(chip, chips):
    return jnp.where(chip % 2 == 0, chip // 2, chips - 1 - chip // 2)


def ring_chip(position, chips):
    position = lax.rem(position + 2 * chips, chips)
    return jnp.where(position < chips // 2, 2 * position, 2 * (chips - 1 - position) + 1)


def ring_hops(long_way, chips):
    long, short = chips // 2, chips - 1 - chips // 2
    return (long, short) if long_way == 0 else (short, long)


def slot_of(long_way, way, distance, chips):
    return distance if distance == 0 or way == long_way else chips // 2 + distance


def entry_barrier(partners):
    barrier = pltpu.get_barrier_semaphore()
    for partner in partners:
        pl.semaphore_signal(barrier, inc=1, device_id=partner, device_id_type=MESH)
    pl.semaphore_wait(barrier, len(partners))


def remote(src, dst, send_sem, recv_sem, target):
    return pltpu.make_async_remote_copy(
        src_ref=src,
        dst_ref=dst,
        send_sem=send_sem,
        recv_sem=recv_sem,
        device_id=target,
        device_id_type=MESH,
    )


class Place:
    def __init__(self, wide):
        self.chips = wide // 2
        self.section, self.me = lax.axis_index("section"), lax.axis_index("dp")
        self.chip, self.core = self.me // 2, lax.rem(self.me, 2)
        self.spot = ring_position(self.chip, self.chips)
        self.ahead = (self.section, 2 * ring_chip(self.spot + 1, self.chips) + self.core)
        self.behind = (self.section, 2 * ring_chip(self.spot - 1, self.chips) + self.core)
        self.twin = (self.section, 2 * self.chip + 1 - self.core)
        self.across = (1 - self.section, self.me)

    def next_of(self, way):
        return self.ahead if way == 0 else self.behind

    def chip_at(self, way, distance):
        return ring_chip(self.spot + distance if way == 0 else self.spot - distance, self.chips)


def block_rows(ref, rows, chip, core):
    return ref.at[pl.ds(pl.multiple_of((2 * chip + core) * rows, rows), rows)]


class Gather:
    def __init__(self, place, names, shards, fulls, rows, long_way, sems):
        self.place, self.names = place, names
        self.shards, self.fulls, self.rows, self.long_way = shards, fulls, rows, long_way
        self.own_sem, self.ring_send, self.ring_recv, self.twin_send, self.twin_recv = sems

    def hops(self, name, way):
        return ring_hops(self.long_way[name], self.place.chips)[way]

    def pieces(self, name, way, hop):
        at = self.place
        origin = at.chip_at(way, -hop)
        target = block_rows(self.fulls[name], self.rows[name], origin, at.core)
        own = self.shards.get(name)
        return (own if hop == 0 and own is not None else target), target

    def ring(self, name, way, hop):
        source, target = self.pieces(name, way, hop)
        i = self.names.index(name)
        return remote(
            source, target, self.ring_send.at[i, way, hop], self.ring_recv.at[i, way, hop], self.place.next_of(way)
        )

    def pair(self, name, way, hop):
        source, target = self.pieces(name, way, hop)
        i, slot = self.names.index(name), slot_of(self.long_way[name], way, hop, self.place.chips)
        return remote(source, target, self.twin_send.at[i, slot], self.twin_recv.at[i, slot], self.place.twin)

    def own(self, name):
        source, target = self.pieces(name, 0, 0)
        return pltpu.make_async_copy(source, target, self.own_sem.at[self.names.index(name)])

    def start(self, name):
        for way in range(2):
            self.ring(name, way, 0).start()
        self.pair(name, 0, 0).start()
        if name in self.shards:
            self.own(name).start()

    def step(self, name, hop):
        for way in range(2):
            hops = self.hops(name, way)
            if hop < hops:
                self.ring(name, way, hop).wait_recv()
                if hop + 1 < hops:
                    self.ring(name, way, hop + 1).start()
                self.pair(name, way, hop + 1).start()

    def complete(self, name):
        if name in self.shards:
            self.own(name).wait()
        self.pair(name, 0, 0).wait_recv()
        for way in range(2):
            for hop in range(self.hops(name, way)):
                self.pair(name, way, hop + 1).wait_recv()

    def drain(self, names):
        for name in names:
            self.pair(name, 0, 0).wait_send()
            for way in range(2):
                for hop in range(self.hops(name, way)):
                    self.pair(name, way, hop + 1).wait_send()
                    self.ring(name, way, hop).wait_send()


LONG_WAY = {"small": 0, "qkv": 0, "out": 1, "crossE": 0, "crossD": 1, "in": 1, "down": 0, "gains": 0}


class Scatter:
    def __init__(self, place, names, grads, rows, long_way, blocks, twins, arrived, sems):
        self.place, self.names, self.grads, self.rows, self.long_way = place, names, grads, rows, long_way
        self.blocks, self.twins, self.arrived = blocks, twins, arrived
        self.load_sem, self.twin_send, self.twin_recv, self.ring_send, self.ring_recv = sems

    def hops(self, name, way):
        return ring_hops(self.long_way[name], self.place.chips)[way]

    def landing(self, name, way, hop):
        return self.arrived[name].at[hop if way == self.long_way[name] else self.place.chips // 2 + hop]

    def pair(self, name, way, distance):
        at, i = self.place, self.names.index(name)
        slot = slot_of(self.long_way[name], way, distance, at.chips)
        source = block_rows(self.grads[name], self.rows[name], at.chip_at(way, distance), 1 - at.core)
        return remote(source, self.twins[name].at[slot], self.twin_send.at[i, slot], self.twin_recv.at[i, slot], at.twin)

    def load(self, name, way, distance):
        at, i = self.place, self.names.index(name)
        slot = slot_of(self.long_way[name], way, distance, at.chips)
        source = block_rows(self.grads[name], self.rows[name], at.chip_at(way, distance), at.core)
        return pltpu.make_async_copy(source, self.blocks[name].at[slot], self.load_sem.at[i, slot])

    def ring(self, name, way, hop):
        at, i = self.place, self.names.index(name)
        slot = slot_of(self.long_way[name], way, self.hops(name, way) - hop, at.chips)
        return remote(
            self.blocks[name].at[slot],
            self.landing(name, way, hop),
            self.ring_send.at[i, way, hop],
            self.ring_recv.at[i, way, hop],
            at.next_of(way),
        )

    def slots(self, name):
        found = []
        for hop in range(self.place.chips // 2 + 1):
            for way in range(2):
                distance = self.hops(name, way) - hop
                if distance > 0 or (distance == 0 and way == self.long_way[name]):
                    found.append((way, distance))
        return found

    def start(self, name):
        for way, distance in self.slots(name):
            self.pair(name, way, distance).start()
            self.load(name, way, distance).start()

    def add(self, terms, out):
        group = 16 if out.shape[0] % 16 == 0 else out.shape[0]

        @pl.loop(0, out.shape[0] // group)
        def _(n):
            rows = pl.ds(pl.multiple_of(n * group, group), group)
            total = terms[0][rows].astype(F32)
            for term in terms[1:]:
                total += term[rows].astype(F32)
            out[rows] = total.astype(out.dtype)

    def step(self, name, way, hop):
        distance = self.hops(name, way) - hop
        if distance <= 0:
            return
        slot = slot_of(self.long_way[name], way, distance, self.place.chips)
        self.load(name, way, distance).wait()
        self.pair(name, way, distance).wait_recv()
        terms = [self.blocks[name].at[slot], self.twins[name].at[slot]]
        if hop > 0:
            self.ring(name, way, hop - 1).wait_recv()
            terms.append(self.landing(name, way, hop - 1))
        self.add(terms, self.blocks[name].at[slot])
        self.ring(name, way, hop).start()

    def finish(self, name, out):
        self.load(name, self.long_way[name], 0).wait()
        self.pair(name, self.long_way[name], 0).wait_recv()
        terms = [self.blocks[name].at[0], self.twins[name].at[0]]
        for way in range(2):
            last = self.hops(name, way) - 1
            self.ring(name, way, last).wait_recv()
            terms.append(self.landing(name, way, last))
        self.add(terms, out)

    def drain(self, name):
        for way, distance in self.slots(name):
            self.pair(name, way, distance).wait_send()
        for way in range(2):
            for hop in range(self.hops(name, way)):
                self.ring(name, way, hop).wait_send()


def dot(a, b, over_a=1, over_b=0):
    return lax.dot_general(a, b, (((over_a,), (over_b,)), ((), ())), preferred_element_type=F32)


def span(start, size):
    return pl.ds(pl.multiple_of(start, size), size)


def each(total, tile, work):
    @pl.loop(0, total // tile)
    def _(n):
        work(span(n * tile, tile))


ROWS = 64


def norm_into(h_ref, gain, out_ref):
    def work(at):
        h = h_ref[at].astype(F32)
        inv_root = lax.rsqrt(jnp.mean(h * h, axis=-1, keepdims=True) + EPS)
        out_ref[at] = (h * inv_root * gain).astype(out_ref.dtype)

    each(h_ref.shape[0], ROWS, work)


def norm_back(dn_ref, h_ref, gain, gain_sum, row, finish):
    gain_sum[row] = jnp.zeros(gain_sum.shape[1:], F32)

    def work(at):
        h, dn = h_ref[at].astype(F32), dn_ref[at].astype(F32)
        inv_root = lax.rsqrt(jnp.mean(h * h, axis=-1, keepdims=True) + EPS)
        scaled = h * inv_root
        product = dn * scaled
        gain_sum[row] += jnp.sum(product.reshape(-1, 8, product.shape[1]), axis=0)
        inner = dn * gain
        finish(at, inv_root * (inner - scaled * jnp.mean(product * gain, axis=-1, keepdims=True)))

    each(h_ref.shape[0], ROWS, work)


def pair_columns(ref, rows, start, two):
    return ref[rows, span(start + two * 2 * HEAD_DIM, 2 * HEAD_DIM)]


def side_masks():
    lane = lax.broadcasted_iota(jnp.int32, (1, 2 * HEAD_DIM), 1)
    first = lane < HEAD_DIM
    return first, (first.astype(F32).astype(BF16), (1 - first.astype(F32)).astype(BF16))


def expo_columns(q, k, seq, length):
    scores = dot(k, q, 1, 1) * HEAD_DIM ** (-0.5)
    if length is not None:
        key = lax.broadcasted_iota(jnp.int32, (seq, seq), 0)
        query = lax.broadcasted_iota(jnp.int32, (seq, seq), 1)
        scores = jnp.where((key <= query) & (key < length), scores, NEG)
    expo = jnp.exp(scores - jnp.max(scores, axis=0, keepdims=True))
    return expo, jnp.sum(expo, axis=0, keepdims=True)


def attend(q_ref, q_at, k_ref, k_at, v_ref, v_at, out_ref, seq, lengths):
    pairs = q_ref.shape[0] // seq
    first, keeps = side_masks()
    each_time = HEADS // 2

    @pl.loop(0, pairs * (HEADS // 2) // each_time)
    def _(m):
        work = []
        for g in range(each_time):
            n = m * each_time + g
            pair, two = n // (HEADS // 2), lax.rem(n, HEADS // 2)
            rows = span(pair * seq, seq)
            length = None if lengths is None else lengths[pair]
            q, k, v = (pair_columns(r, rows, a, two) for r, a in ((q_ref, q_at), (k_ref, k_at), (v_ref, v_at)))
            for side in range(2):
                work.append((rows, two, length, q, k, v, side))
        expos = [expo_columns(q * keeps[side], k, seq, length) for rows, two, length, q, k, v, side in work]
        outs = [dot((e * (1.0 / t)).astype(BF16), w[5], 0, 0) for (e, t), w in zip(expos, work)]
        for g in range(each_time):
            rows, two = work[2 * g][:2]
            value = jnp.where(first, outs[2 * g], outs[2 * g + 1])
            out_ref[rows, span(two * 2 * HEAD_DIM, 2 * HEAD_DIM)] = value.astype(BF16)


def attend_back(q_ref, q_at, k_ref, k_at, v_ref, v_at, do_ref, dq, dk, dv, seq, lengths):
    pairs = q_ref.shape[0] // seq
    first, keeps = side_masks()
    root = HEAD_DIM ** (-0.5)
    each_time = HEADS // 4

    @pl.loop(0, pairs * (HEADS // 2) // each_time)
    def _(m):
        work = []
        for g in range(each_time):
            n = m * each_time + g
            pair, two = n // (HEADS // 2), lax.rem(n, HEADS // 2)
            rows = span(pair * seq, seq)
            length = None if lengths is None else lengths[pair]
            q, k, v = (pair_columns(r, rows, a, two) for r, a in ((q_ref, q_at), (k_ref, k_at), (v_ref, v_at)))
            d_out = pair_columns(do_ref, rows, 0, two)
            for side in range(2):
                work.append((rows, two, length, q, k, v, d_out, side))
        expos = [expo_columns(q * keeps[side], k, seq, length) for rows, two, length, q, k, v, d_out, side in work]
        d_probs = [dot(v, d_out * keeps[side], 1, 1) for rows, two, length, q, k, v, d_out, side in work]
        probs = [e * (1.0 / t) for e, t in expos]
        d_scores = [(p * (d - jnp.sum(p * d, axis=0, keepdims=True))).astype(BF16) for p, d in zip(probs, d_probs)]
        dvs = [dot(p.astype(BF16), w[6]) for p, w in zip(probs, work)]
        dqs = [dot(d, w[4], 0, 0) for d, w in zip(d_scores, work)]
        dks = [dot(d, w[3]) for d, w in zip(d_scores, work)]
        for g in range(each_time):
            rows, two = work[2 * g][:2]
            for (ref, start), both, factor in ((dq, dqs, root), (dk, dks, root), (dv, dvs, 1.0)):
                value = jnp.where(first, both[2 * g], both[2 * g + 1]) * factor
                ref[rows, span(start + two * 2 * HEAD_DIM, 2 * HEAD_DIM)] = value.astype(BF16)


def gelu_parts(gate):
    root, cubic = 0.7978845608028654, 0.044715
    square = gate * gate
    bent = jnp.tanh(root * gate * (1.0 + cubic * square))
    half = 0.5 * (1.0 + bent)
    slope = half + 0.5 * gate * (1.0 - bent * bent) * root * (1.0 + 3.0 * cubic * square)
    return gate * half, slope


FF_TILE = 512


def mlp_forward(a_ref, w_in, w_down, into_ref, hidden_ref=None, slopes_ref=None):
    ff = w_in.shape[1] // 2

    @pl.loop(0, ff // FF_TILE)
    def _(n):
        gates, uppers = span(n * FF_TILE, FF_TILE), span(ff + n * FF_TILE, FF_TILE)
        gate, upper = dot(a_ref[...], w_in[:, gates]), dot(a_ref[...], w_in[:, uppers])
        active, slope = gelu_parts(gate)
        hidden = (active * upper).astype(BF16)
        if hidden_ref is not None:
            hidden_ref[:, gates] = hidden
            slopes_ref[:, gates] = (slope * upper).astype(BF16)
            slopes_ref[:, uppers] = active.astype(BF16)
        if w_down is not None:
            into_ref[...] += dot(hidden, w_down[gates, :])


def mlp_back(d_low, w_in, w_down, slopes_ref, dn_ref):
    ff = w_in.shape[1] // 2
    dn_ref[...] = jnp.zeros(dn_ref.shape, F32)

    @pl.loop(0, ff // FF_TILE)
    def _(n):
        gates, uppers = span(n * FF_TILE, FF_TILE), span(ff + n * FF_TILE, FF_TILE)
        d_hidden = dot(d_low[...], w_down[gates, :], 1, 1)
        d_gate = (d_hidden * slopes_ref[:, gates]).astype(BF16)
        d_upper = (d_hidden * slopes_ref[:, uppers]).astype(BF16)
        slopes_ref[:, gates], slopes_ref[:, uppers] = d_gate, d_upper
        dn_ref[...] += dot(d_gate, w_in[:, gates], 1, 1) + dot(d_upper, w_in[:, uppers], 1, 1)


def product_into(a_ref, w_ref, out_ref, tile, w_at=0, transposed=False):
    width = out_ref.shape[1]

    @pl.loop(0, width // tile)
    def _(n):
        if transposed:
            value = dot(a_ref[...], w_ref[span(w_at + n * tile, tile), :], 1, 1)
        else:
            value = dot(a_ref[...], w_ref[:, span(w_at + n * tile, tile)])
        out_ref[:, span(n * tile, tile)] = value.astype(out_ref.dtype)


def add_product(base_ref, a_ref, w, out_ref):
    out_ref[...] = base_ref[...].astype(F32) + dot(a_ref[...], w)


class Moves:
    def __init__(self, sems):
        self.sems, self.used = sems, 0

    def start(self, src, dst):
        copy = pltpu.make_async_copy(src, dst, self.sems.at[self.used])
        self.used += 1
        copy.start()
        return copy


def weight_grad(moves, a_ref, y_ref, grad_hbm, tile_rows, tile_columns, column_at=0):
    depth, width = a_ref.shape[1], y_ref.shape[1]

    def inner(stage):
        copies = []
        for i in range(depth // tile_rows):
            for j in range(width // tile_columns):
                n = len(copies)
                if n >= 2:
                    copies[n - 2].wait()
                rows, columns = pl.ds(i * tile_rows, tile_rows), pl.ds(j * tile_columns, tile_columns)
                stage[n % 2] = dot(a_ref[:, rows], y_ref[:, columns], 0, 0).astype(BF16)
                goal = grad_hbm.at[rows, pl.ds(column_at + j * tile_columns, tile_columns)]
                copies.append(moves.start(stage.at[n % 2], goal))
        for copy in copies[-2:]:
            copy.wait()

    pl.run_scoped(inner, pltpu.VMEM((2, tile_rows, tile_columns), BF16))


GATHER_NAMES = ("small", "qkv", "out", "crossE", "crossD", "in", "down")
BLOCK = (8, 128)


def spread_gains(small, own, width):
    lane = lax.broadcasted_iota(jnp.int32, BLOCK, 1)
    total = jnp.zeros((BLOCK[0], width), F32)
    for n in range(width // own):
        part = jnp.where(lane < own, small[n * BLOCK[0] : (n + 1) * BLOCK[0], :], 0.0)
        wide = jnp.concatenate([part, jnp.zeros((BLOCK[0], width - BLOCK[1]), F32)], axis=1)
        total += wide if n == 0 else pltpu.roll(wide, n * own, 1)
    return total


def gather_blocks(gains_grad, own, out_ref):
    width = gains_grad.shape[1]
    lane = lax.broadcasted_iota(jnp.int32, BLOCK, 1)
    for n in range(width // own):
        turned = gains_grad if n == 0 else pltpu.roll(gains_grad, width - n * own, 1)
        out_ref[n * BLOCK[0] : (n + 1) * BLOCK[0], :] = jnp.where(lane < own, turned[:, : BLOCK[1]], 0.0)


def forward_kernel(
    wide, seq, lengths, sources, loss_weight, gains_in, x_in, qkv_in, out_in, cross_in, in_in, down_in,
    small_out, qkv_full, out_full, enc_full, dec_full, in_full, down_full,
    joined_out, attended_out, middle_out, final_out, memory_out, landed, gains, factors,
    small_own, small, w_qkv, w_out, w_in, w_down, x, normed, joined, attended, middle,
    load_sem, send_sem, recv_sem, *gather_sems,
):
    at = Place(wide)
    pairs, width = x.shape[0] // seq, x.shape[1]
    own = gains_in.shape[1]
    lane = lax.broadcasted_iota(jnp.int32, (1, BLOCK[1]), 1)
    counted = jnp.zeros((1, BLOCK[1]), F32)
    for pair in range(pairs):
        counted += jnp.where(lane == sources[pair], lengths[pair].astype(F32), 0.0)
    small_own[...] = jnp.zeros(BLOCK, F32)
    small_own[0:3, 0:own] = gains_in[...].astype(F32)
    small_own[3:4, :] = counted
    entry_barrier((at.ahead, at.behind, at.twin, at.across))
    fulls = dict(zip(GATHER_NAMES, (small_out, qkv_full, out_full, enc_full, dec_full, in_full, down_full)))
    rows = {n: f.shape[0] // wide for n, f in fulls.items()}
    passed = remote(
        cross_in,
        block_rows(enc_full, rows["crossE"], at.chip, at.core),
        send_sem.at[pairs],
        recv_sem.at[pairs],
        at.across,
    )
    moves = Moves(load_sem)

    def to_dec(pair):
        rows = pl.ds(pair * seq, seq)
        return remote(memory_out.at[rows], landed.at[rows], send_sem.at[pair], recv_sem.at[pair], at.across)

    def run(names, shards, lengths, later):
        load_x = moves.start(x_in, x)
        gather = Gather(at, GATHER_NAMES, shards, fulls, rows, LONG_WAY, gather_sems)
        for name in names:
            if name == "crossE":
                passed.wait_recv()
            gather.start(name)
        for hop in range(at.chips // 2 - 1):
            for name in names:
                gather.step(name, hop)

        def arrive(*some):
            for name in some:
                gather.step(name, at.chips // 2 - 1)

        def load(name, into):
            gather.complete(name)
            return moves.start(fulls[name], into)

        arrive("small", "qkv")
        load("small", small).wait()
        gains[...] = spread_gains(small, own, width)
        totals = jnp.zeros((1, BLOCK[1]), F32)
        for n in range(wide):
            totals += small[n * BLOCK[0] + 3 : n * BLOCK[0] + 4, :]
        factors[...] = jnp.zeros(factors.shape, F32)
        for pair in range(pairs):
            source = sources[pair]
            weight = jnp.where(source == 0, loss_weight[0], jnp.where(source == 1, loss_weight[1], loss_weight[2]))
            count = jnp.sum(jnp.where(lane == source, totals, 0.0), axis=1, keepdims=True)
            factor = jnp.full((1, 1), weight.astype(F32) * (pairs * wide * seq / 3.0), F32) / count
            factors[pair : pair + 1, :] = jnp.broadcast_to(factor, (1, BLOCK[1]))
        load_x.wait()
        norm_into(x, gains[0:1], normed)
        load_qkv = load("qkv", w_qkv)
        arrive("out")
        load_qkv.wait()
        product_into(normed, w_qkv, joined, width)
        arrive(*(n for n in names if n not in ("small", "qkv", "out")))
        attend(joined, 0, joined, width, joined, 2 * width, attended, seq, lengths)
        load("out", w_out).wait()
        add_product(x, attended, w_out[...], middle)
        stores = [moves.start(a, b) for a, b in ((joined, joined_out), (attended, attended_out), (middle, middle_out))]
        later(gather, load, stores)
        gather.drain(names)

    @pl.when(at.section == 0)
    def _():
        passed.start()

        def later(gather, load, stores):
            norm_into(middle, gains[1:2], normed)
            loads = [load("in", w_in), load("down", w_down)]
            for copy in loads + stores[2:]:
                copy.wait()
            mlp_forward(normed, w_in, w_down, middle)
            stores.append(moves.start(middle, final_out))
            norm_into(middle, gains[2:3], normed)
            moves.start(normed, memory_out).wait()
            for pair in range(pairs):
                to_dec(pair).start()
            for copy in stores[:2] + stores[3:]:
                copy.wait()
            for pair in range(pairs):
                to_dec(pair).wait_send()

        run(
            ("small", "qkv", "out", "in", "down"),
            {"small": small_own, "qkv": qkv_in, "out": out_in, "in": in_in, "down": down_in},
            None,
            later,
        )
        passed.wait_send()

    @pl.when(at.section == 1)
    def _():
        def later(gather, load, stores):
            for name in ("crossD", "crossE", "in", "down"):
                gather.complete(name)
            for copy in stores:
                copy.wait()
            for pair in range(pairs):
                to_dec(pair).wait_recv()

        run(
            ("small", "qkv", "out", "crossD", "crossE", "in", "down"),
            {"small": small_own, "qkv": qkv_in, "out": out_in, "crossD": cross_in, "in": in_in, "down": down_in},
            lengths,
            later,
        )


def forward(wide, seq, lengths, sources, loss_weight, gains, x, w_qkv, w_out, w_cross, w_in, w_down):
    (rows, width), chips, count = x.shape, wide // 2, len(GATHER_NAMES)
    vmem, shaped, dma = pltpu.VMEM, jax.ShapeDtypeStruct, pltpu.SemaphoreType.DMA
    fulls = [(wide * w.shape[0], w.shape[1]) for w in (w_qkv, w_out, w_cross, w_cross, w_in, w_down)]
    return pl.pallas_call(
        partial(forward_kernel, wide, seq),
        out_shape=[shaped((wide * BLOCK[0], BLOCK[1]), F32)]
        + [shaped(f, BF16) for f in fulls]
        + [
            shaped((rows, w_qkv.shape[1]), BF16),
            shaped((rows, width), BF16),
            shaped((rows, width), F32),
            shaped((rows, width), F32),
            shaped((rows, width), BF16),
            shaped((rows, width), BF16),
            shaped((BLOCK[0], width), F32),
            shaped(BLOCK, F32),
        ],
        in_specs=[SMEM] * 3 + [VMEM] + [ANY] * 6,
        out_specs=[ANY] * 13 + [VMEM] * 2,
        scratch_shapes=[vmem(BLOCK, F32), vmem((wide * BLOCK[0], BLOCK[1]), F32)]
        + [vmem(fulls[n], BF16) for n in (0, 1, 4, 5)]
        + [
            vmem((rows, width), BF16),
            vmem((rows, width), BF16),
            vmem((rows, w_qkv.shape[1]), BF16),
            vmem((rows, width), BF16),
            vmem((rows, width), F32),
            dma((32,)),
            dma((rows // seq + 1,)),
            dma((rows // seq + 1,)),
            dma((count,)),
            dma((count, 2, chips // 2)),
            dma((count, 2, chips // 2)),
            dma((count, chips)),
            dma((count, chips)),
        ],
        name="gather_and_forward",
        compiler_params=pltpu.CompilerParams(collective_id=0, has_side_effects=True, vmem_limit_bytes=VMEM_LIMIT),
    )(lengths, sources, loss_weight, gains, x, w_qkv, w_out, w_cross, w_in, w_down)


SCATTER_NAMES = ("down", "in", "crossD", "crossE", "out", "qkv", "gains")


def backward_kernel(
    wide, seq, own, lengths, factors, x_in, gains_in, cot_in, joined_in, attended_in, middle_in, final_in, memory_in, landed,
    w_qkv_in, w_out_in, w_enc_in, w_dec_in, w_in_in, w_down_in,
    block_out, input_out, returned, g_down, g_in, g_dec, g_enc, g_out, g_qkv,
    down_sum, in_sum, cross_sum, out_sum, qkv_sum, gains_sum,
    gains, gain_sum, back, g_gains, passed_out, passed_in, down_blocks, *refs,
):
    count = len(SCATTER_NAMES)
    twins, arrived = dict(zip(SCATTER_NAMES, refs[:count])), dict(zip(SCATTER_NAMES, refs[count : 2 * count]))
    load_sem, send_sem, recv_sem, *scatter_sems = refs[2 * count :]
    at = Place(wide)
    rows, width = x_in.shape
    pairs, ff = rows // seq, w_down_in.shape[0]
    moves = Moves(load_sem)
    vmem = pltpu.VMEM
    broad, slim = vmem((rows, width), F32), vmem((rows, width), BF16)
    grads = dict(zip(SCATTER_NAMES, (g_down, g_in, g_dec, g_enc, g_out, g_qkv, g_gains)))
    share = {n: g.shape[0] // wide for n, g in grads.items()}
    blocks = {"down": down_blocks}
    scatter = Scatter(at, SCATTER_NAMES, grads, share, LONG_WAY, blocks, twins, arrived, scatter_sems)
    sums = {"down": down_sum, "in": in_sum, "out": out_sum, "qkv": qkv_sum, "gains": gains_sum}
    sums.update(crossD=cross_sum, crossE=passed_out)
    moves.start(gains_in, gains).wait()
    entry_barrier((at.ahead, at.behind, at.twin, at.across))
    passed = remote(passed_out, passed_in, send_sem.at[pairs], recv_sem.at[pairs], at.across)
    done = {}

    def blocks_of(name):
        return vmem((at.chips, share[name], grads[name].shape[1]), grads[name].dtype)

    def hop(*names):
        for name in names:
            for way in range(2):
                scatter.step(name, way, done.get(name, 0))
            done[name] = done.get(name, 0) + 1

    def ready(name):
        scatter.start(name)
        hop(name)

    def rest(names):
        for step in range(at.chips // 2 + 1):
            for name in names:
                if done[name] == step < at.chips // 2:
                    hop(name)
                elif done[name] == step:
                    scatter.finish(name, sums[name])
                    done[name] += 1
                    if name == "crossE":
                        passed.start()
        for name in names:
            scatter.drain(name)

    def to_enc(pair):
        part = pl.ds(pair * seq, seq)
        return remote(back.at[part], returned.at[part], send_sem.at[pair], recv_sem.at[pair], at.across)

    def self_back(lengths, d_middle, x, normed, d_low, w_qkv, w_out, joined, attended, d_attended, dn, first, second):
        norm_into(x, gains[0:1], normed)
        each(rows, ROWS, lambda part: d_low.__setitem__(part, d_middle[part].astype(BF16)))
        weight_grad(moves, attended, d_low, g_out, width, width)
        ready("out")
        product_into(d_low, w_out, d_attended, width, transposed=True)
        hop(*first)
        attend_back(
            joined, 0, joined, width, joined, 2 * width, d_attended,
            (joined, 0), (joined, width), (joined, 2 * width), seq, lengths,
        )
        hop(*second)
        weight_grad(moves, normed, joined, g_qkv, width, width)
        ready("qkv")
        product_into(joined, w_qkv, dn, width, transposed=True)

        def finish(part, d_input):
            d_middle[part] = d_middle[part] + d_input

        norm_back(dn, x, gains[0:1], gain_sum, 0, finish)
        store = moves.start(d_middle, input_out)
        lines = [jnp.sum(gain_sum[row], axis=0, keepdims=True) for row in range(3)]
        gather_blocks(jnp.concatenate(lines + [jnp.zeros((BLOCK[0] - 3, width), F32)], axis=0), own, g_gains)
        ready("gains")
        return store

    def encoder(
        w_qkv, w_out, w_in, w_down, x, joined, attended, middle, final, normed, hidden, slopes, d_low, d_attended, dn, d_memory,
        in_blocks, out_blocks, qkv_blocks, gains_blocks,
    ):
        blocks.update({"in": in_blocks, "out": out_blocks, "qkv": qkv_blocks, "gains": gains_blocks})
        loads = [
            moves.start(a, b)
            for a, b in (
                (middle_in, middle), (w_in_in, w_in), (final_in, final), (w_down_in, w_down), (x_in, x),
                (joined_in, joined), (attended_in, attended), (w_out_in, w_out), (w_qkv_in, w_qkv), (memory_in, block_out),
            )
        ]
        for load in loads:
            load.wait()
        norm_into(middle, gains[1:2], normed)
        mlp_forward(normed, w_in, None, None, hidden, slopes)
        for pair in range(pairs):
            to_enc(pair).wait_recv()
        moves.start(returned, d_memory).wait()

        def finish_final(part, d_input):
            final[part] = d_input
            d_low[part] = d_input.astype(BF16)

        norm_back(d_memory, final, gains[2:3], gain_sum, 2, finish_final)
        weight_grad(moves, hidden, d_low, g_down, ff // 4, width)
        ready("down")
        mlp_back(d_low, w_in, w_down, slopes, dn)
        hop("down")
        weight_grad(moves, normed, slopes, g_in, width, ff // 4)
        ready("in")
        hop("down")

        def finish_middle(part, d_input):
            final[part] = final[part] + d_input

        norm_back(dn, middle, gains[1:2], gain_sum, 1, finish_middle)
        store = self_back(
            None, final, x, normed, d_low, w_qkv, w_out, joined, attended, d_attended, dn, ("in",), ("down",)
        )
        rest(("down", "in", "out", "qkv", "gains"))
        store.wait()

    @pl.when(at.section == 0)
    def _():
        done.clear()
        pl.run_scoped(
            encoder,
            vmem(w_qkv_in.shape, BF16), vmem(w_out_in.shape, BF16), vmem(w_in_in.shape, BF16), vmem(w_down_in.shape, BF16),
            slim, vmem((rows, 3 * width), BF16), slim, broad, broad, slim,
            vmem((rows, ff), BF16), vmem((rows, 2 * ff), BF16), slim, slim, broad, slim,
            *(blocks_of(n) for n in ("in", "out", "qkv", "gains")),
        )
        passed.wait_recv()
        cross_sum[...] = passed_in[...]

    def decoder(
        memory, cot, normed_a, queries, keyval, crossed, after, normed_b, slopes, hidden, d_low, dn, d_low2, d_crossed,
        middle, d_after,
    ):
        d_queries, d_keyval = cot, keyval

        def to_memory(w_enc, w_dec, w_in, w_down):
            loads = [
                moves.start(a, b)
                for a, b in (
                    (middle_in, middle), (w_dec_in, w_dec), (landed, memory), (w_enc_in, w_enc),
                    (w_in_in, w_in), (w_down_in, w_down), (cot_in, cot),
                )
            ]
            loads[0].wait()
            norm_into(middle, gains[1:2], normed_a)
            loads[1].wait()
            product_into(normed_a, w_dec, queries, width)
            loads[2].wait()
            loads[3].wait()
            product_into(memory, w_enc, keyval, width)
            attend(queries, 0, keyval, 0, keyval, width, crossed, seq, None)
            add_product(middle, crossed, w_dec[:, width:], after)
            norm_into(after, gains[2:3], normed_b)
            for load in loads[4:]:
                load.wait()
            dn[...] = after[...]
            mlp_forward(normed_b, w_in, w_down, dn, hidden, slopes)

            for pair in range(pairs):

                @pl.loop(0, seq // ROWS)
                def _(n):
                    part = span(pair * seq + n * ROWS, ROWS)
                    position = n * ROWS + lax.broadcasted_iota(jnp.int32, (ROWS, 1), 0)
                    d_low2[part] = dn[part].astype(BF16)
                    factor = factors[pair : pair + 1, 0:1]
                    d_final = jnp.where(position < lengths[pair], cot[part].astype(F32) * factor, 0.0)
                    d_after[part] = d_final
                    d_low[part] = d_final.astype(BF16)

            store = moves.start(d_low2, block_out)
            weight_grad(moves, hidden, d_low, g_down, ff // 4, width)
            ready("down")
            mlp_back(d_low, w_in, w_down, slopes, dn)
            hop("down")
            store.wait()

            def finish_after(part, d_input):
                total = d_after[part] + d_input
                d_after[part] = total
                d_low2[part] = total.astype(BF16)

            norm_back(dn, after, gains[2:3], gain_sum, 2, finish_after)
            d_crossed[...] = dot(d_low2[...], w_dec[:, width:], 1, 1).astype(BF16)
            attend_back(
                queries, 0, keyval, 0, keyval, width, d_crossed, (d_queries, 0), (d_keyval, 0), (d_keyval, width), seq, None
            )
            for pair in range(pairs):
                part = pl.ds(pair * seq, seq)
                back[part] = dot(d_keyval[part], w_enc[...], 1, 1).astype(BF16)
                to_enc(pair).start()
            dn[...] = dot(d_queries[...], w_dec[:, :width], 1, 1)

        pl.run_scoped(
            to_memory,
            vmem(w_enc_in.shape, BF16), vmem(w_dec_in.shape, BF16), vmem(w_in_in.shape, BF16), vmem(w_down_in.shape, BF16),
        )

        def to_input(w_qkv, w_out, in_blocks, dec_blocks, enc_blocks, out_blocks, qkv_blocks, gains_blocks):
            blocks.update({"in": in_blocks, "crossD": dec_blocks, "crossE": enc_blocks})
            blocks.update({"out": out_blocks, "qkv": qkv_blocks, "gains": gains_blocks})
            loads = [moves.start(w_out_in, w_out), moves.start(w_qkv_in, w_qkv)]
            weight_grad(moves, normed_b, slopes, g_in, width, ff // 4)
            ready("in")
            joined = slopes.at[:, pl.ds(0, 3 * width)]
            loads.append(moves.start(joined_in, joined))
            weight_grad(moves, memory, d_keyval, g_enc, width, width)
            ready("crossE")
            loads.append(moves.start(x_in, memory))
            weight_grad(moves, crossed, d_low2, g_dec, width, width, column_at=width)
            loads.append(moves.start(attended_in, crossed))
            weight_grad(moves, normed_a, d_queries, g_dec, width, width)
            ready("crossD")

            def finish_middle(part, d_input):
                d_after[part] = d_after[part] + d_input

            norm_back(dn, middle, gains[1:2], gain_sum, 1, finish_middle)
            for load in loads:
                load.wait()
            store = self_back(
                lengths, d_after, memory, normed_a, d_low, w_qkv, w_out, joined, crossed, d_crossed, dn, ("down",), ("in",)
            )
            rest(("crossE", "down", "in", "crossD", "out", "qkv", "gains"))
            store.wait()

        pl.run_scoped(
            to_input,
            vmem(w_qkv_in.shape, BF16), vmem(w_out_in.shape, BF16),
            *(blocks_of(n) for n in ("in", "crossD", "crossE", "out", "qkv", "gains")),
        )
        for pair in range(pairs):
            to_enc(pair).wait_send()
        passed.wait_send()

    @pl.when(at.section == 1)
    def _():
        done.clear()
        pl.run_scoped(
            decoder,
            slim, slim, slim, slim, vmem((rows, 2 * width), BF16), slim, broad, slim,
            vmem((rows, 2 * ff), BF16), vmem((rows, ff), BF16), slim, broad, slim, slim, broad, broad,
        )


def backward(wide, seq, own, lengths, factors, x, gains, cot, saved, weights):
    w_qkv, w_out, w_enc, w_dec, w_in, w_down = weights
    rows, width = x.shape
    chips, count, pairs = wide // 2, len(SCATTER_NAMES), rows // seq
    args = (lengths, factors, x, gains, cot, *saved, *weights)
    vmem, shaped, dma = pltpu.VMEM, jax.ShapeDtypeStruct, pltpu.SemaphoreType.DMA
    shares = [(w.shape[0] // wide, w.shape[1]) for w in (w_down, w_in, w_dec, w_enc, w_out, w_qkv)] + [BLOCK]
    types = [BF16] * (count - 1) + [F32]
    return pl.pallas_call(
        partial(backward_kernel, wide, seq, own),
        out_shape=[shaped((rows, width), BF16), shaped((rows, width), F32), shaped((rows, width), BF16)]
        + [shaped(w.shape, BF16) for w in (w_down, w_in, w_dec, w_enc, w_out, w_qkv)]
        + [shaped(shares[n], F32) for n in (0, 1, 2, 4, 5, 6)],
        in_specs=[SMEM, VMEM] + [ANY] * (len(args) - 2),
        out_specs=[ANY] * 9 + [VMEM] * 6,
        scratch_shapes=[
            vmem(gains.shape, F32),
            vmem((3, 8, width), F32),
            vmem((rows, width), BF16),
            vmem((wide * BLOCK[0], BLOCK[1]), F32),
            vmem(shares[3], F32),
            vmem(shares[3], F32),
            vmem((chips,) + shares[0], BF16),
        ]
        + [vmem((chips,) + s, t) for s, t in zip(shares, types)]
        + [vmem((chips - 1,) + s, t) for s, t in zip(shares, types)]
        + [
            dma((96,)),
            dma((pairs + 1,)),
            dma((pairs + 1,)),
            dma((count, chips)),
            dma((count, chips)),
            dma((count, chips)),
            dma((count, 2, chips // 2)),
            dma((count, 2, chips // 2)),
        ],
        name="backward_and_reduce",
        compiler_params=pltpu.CompilerParams(collective_id=1, has_side_effects=True, vmem_limit_bytes=VMEM_LIMIT),
    )(*args)


def shifted(block, axis, distance):
    devices = range(lax.axis_size(axis))
    route = [(i - distance, i) for i in devices if i - distance in devices]
    return lax.ppermute(block, axis, route)


def plain_product(a, b):
    return jnp.dot(a, b, preferred_element_type=jnp.float32)


def plain_split_heads(v):
    return v.reshape(v.shape[0], HEADS, -1)


def plain_norm_forward(h, norm_gain):
    inv_root = lax.rsqrt(jnp.mean(h * h, axis=-1, keepdims=True) + EPS)
    return (h * inv_root * norm_gain.astype(jnp.float32), inv_root)


def plain_norm_back(d_normed, h, inv_root, norm_gain):
    scaled = h * inv_root
    d_gain = jnp.sum(d_normed * scaled, axis=0)
    inner = d_normed * norm_gain.astype(jnp.float32)
    d_input = inv_root * (inner - scaled * jnp.mean(inner * scaled, axis=-1, keepdims=True))
    return (d_input, d_gain)


def plain_score_block(q, k, key_mask):
    scores = jnp.einsum(
        "qhd,khd->hqk", plain_split_heads(q), plain_split_heads(k), preferred_element_type=jnp.float32
    ) * HEAD_DIM ** (-0.5)
    if key_mask is not None:
        scores = jnp.where(key_mask[None], scores, NEG)
    return scores


def plain_attend_forward(q, k, v, key_mask):
    scores = plain_score_block(q, k, key_mask)
    highest = jnp.max(scores, axis=-1, keepdims=True)
    expo = jnp.exp(scores - highest)
    total = jnp.sum(expo, axis=-1, keepdims=True)
    weights = (expo / total).astype(jnp.bfloat16)
    output = jnp.einsum("hqk,khd->qhd", weights, plain_split_heads(v), preferred_element_type=jnp.float32)
    return (output.reshape(q.shape[0], -1), highest + jnp.log(total))


def plain_attend_back(q, k, v, key_mask, log_total, d_out):
    scores = plain_score_block(q, k, key_mask)
    probs = jnp.exp(scores - log_total)
    heads_dout = plain_split_heads(d_out)
    d_value = jnp.einsum(
        "hqk,qhd->khd", probs.astype(jnp.bfloat16), heads_dout, preferred_element_type=jnp.float32
    )
    d_probs = jnp.einsum(
        "qhd,khd->hqk", heads_dout, plain_split_heads(v), preferred_element_type=jnp.float32
    )
    centre = jnp.sum(probs * d_probs, axis=-1, keepdims=True)
    d_scores = (probs * (d_probs - centre)).astype(jnp.bfloat16)
    d_query = jnp.einsum(
        "hqk,khd->qhd", d_scores, plain_split_heads(k), preferred_element_type=jnp.float32
    ) * HEAD_DIM ** (-0.5)
    d_key = jnp.einsum(
        "hqk,qhd->khd", d_scores, plain_split_heads(q), preferred_element_type=jnp.float32
    ) * HEAD_DIM ** (-0.5)
    rows_query = q.shape[0]
    rows_key = k.shape[0]
    return (
        d_query.reshape(rows_query, -1),
        d_key.reshape(rows_key, -1),
        d_value.reshape(rows_key, -1),
    )


def plain_attention_forward(h, norm_gain, w_qkv, w_out, key_mask):
    normed, inv_root = plain_norm_forward(h, norm_gain)
    normed_low = normed.astype(jnp.bfloat16)
    joined = plain_product(normed_low, w_qkv).astype(jnp.bfloat16)
    q, k, v = jnp.split(joined, 3, axis=1)
    output, log_total = plain_attend_forward(q, k, v, key_mask)
    output_low = output.astype(jnp.bfloat16)
    return (normed_low, inv_root, joined, output_low, log_total, plain_product(output_low, w_out))


def plain_attention_back(d_h, h, saved, norm_gain, w_qkv, w_out, key_mask):
    normed_low, inv_root, joined, output_low, log_total, unused = saved
    d_low = d_h.astype(jnp.bfloat16)
    d_wout = plain_product(output_low.T, d_low)
    d_output = plain_product(d_low, w_out.T).astype(jnp.bfloat16)
    q, k, v = jnp.split(joined, 3, axis=1)
    d_query, d_key, d_value = plain_attend_back(q, k, v, key_mask, log_total, d_output)
    d_joined = jnp.concatenate([d_query, d_key, d_value], axis=1).astype(jnp.bfloat16)
    d_wqkv = plain_product(normed_low.T, d_joined)
    d_normed = plain_product(d_joined, w_qkv.T)
    d_input, d_gain = plain_norm_back(d_normed, h, inv_root, norm_gain)
    return (d_input, d_gain, d_wqkv, d_wout)


def plain_mlp_forward(h, norm_gain, w_in, w_down):
    normed, inv_root = plain_norm_forward(h, norm_gain)
    normed_low = normed.astype(jnp.bfloat16)
    joined = plain_product(normed_low, w_in)
    gate, upper = jnp.split(joined, 2, axis=1)
    hidden_low = (jax.nn.gelu(gate, approximate=True) * upper).astype(jnp.bfloat16)
    return (normed_low, inv_root, joined, hidden_low, plain_product(hidden_low, w_down))


def plain_mlp_back(d_h, h, saved, norm_gain, w_in, w_down):
    normed_low, inv_root, joined, hidden_low, unused = saved
    d_low = d_h.astype(jnp.bfloat16)
    d_wdown = plain_product(hidden_low.T, d_low)
    d_hidden = plain_product(d_low, w_down.T)
    gate, upper = jnp.split(joined, 2, axis=1)
    active, active_back = jax.vjp(partial(jax.nn.gelu, approximate=True), gate)
    d_gate = active_back(d_hidden * upper)[0]
    d_upper = d_hidden * active
    d_joined = jnp.concatenate([d_gate, d_upper], axis=1).astype(jnp.bfloat16)
    d_win = plain_product(normed_low.T, d_joined)
    d_normed = plain_product(d_joined, w_in.T)
    d_input, d_gain = plain_norm_back(d_normed, h, inv_root, norm_gain)
    return (d_input, d_gain, d_win, d_wdown)


def encoder_forward(weights, source):
    gains, w_qkv, w_out, w_cross, w_in, w_down = weights
    inputs = source.astype(jnp.float32)
    attn_saved = plain_attention_forward(inputs, gains[0], w_qkv, w_out, None)
    middle = inputs + attn_saved[-1]
    mlp_saved = plain_mlp_forward(middle, gains[1], w_in, w_down)
    final = middle + mlp_saved[-1]
    normed, inv_root = plain_norm_forward(final, gains[2])
    memory = normed.astype(jnp.bfloat16)
    key_value = plain_product(memory, w_cross).astype(jnp.bfloat16)
    return (inputs, attn_saved, middle, mlp_saved, final, inv_root, memory, key_value)


def encoder_front(weights, source):
    saved = encoder_forward(weights, source)
    return (saved[7], saved[6])


def encoder_back_saved(weights, saved, d_keyvalue):
    gains, w_qkv, w_out, w_cross, w_in, w_down = weights
    inputs, attn_saved, middle, mlp_saved, final, inv_root, memory, key_value = saved
    d_wcross = plain_product(memory.T, d_keyvalue)
    d_memory = plain_product(d_keyvalue, w_cross.T)
    d_final, gain_last = plain_norm_back(d_memory, final, inv_root, gains[2])
    d_part, gain_mlp, d_win, d_wdown = plain_mlp_back(d_final, middle, mlp_saved, gains[1], w_in, w_down)
    d_middle = d_final + d_part
    d_first, gain_attn, d_wqkv, d_wout = plain_attention_back(
        d_middle, inputs, attn_saved, gains[0], w_qkv, w_out, None
    )
    grads = (jnp.stack([gain_attn, gain_mlp, gain_last]), d_wqkv, d_wout, d_wcross, d_win, d_wdown)
    return (d_middle + d_first, grads)


def encoder_back(weights, source, d_keyvalue):
    return encoder_back_saved(weights, encoder_forward(weights, source), d_keyvalue)


def decoder_pass(weights, source, key_value, weight_cot, length, factor):
    gains, w_qkv, w_out, w_cross, w_in, w_down = weights
    width = source.shape[1]
    inputs = source.astype(jnp.float32)
    position = jnp.arange(inputs.shape[0], dtype=jnp.int32)
    is_valid = position < length
    key_mask = (position[None, :] <= position[:, None]) & is_valid[None, :]
    attn_saved = plain_attention_forward(inputs, gains[0], w_qkv, w_out, key_mask)
    middle = inputs + attn_saved[-1]
    normed, inv_root = plain_norm_forward(middle, gains[1])
    normed_low = normed.astype(jnp.bfloat16)
    w_query = w_cross[:, :width]
    w_back = w_cross[:, width:]
    queries = plain_product(normed_low, w_query).astype(jnp.bfloat16)
    mem_keys = key_value[:, :width]
    mem_values = key_value[:, width:]
    cross_out, cross_total = plain_attend_forward(queries, mem_keys, mem_values, None)
    cross_low = cross_out.astype(jnp.bfloat16)
    after = middle + plain_product(cross_low, w_back)
    mlp_saved = plain_mlp_forward(after, gains[2], w_in, w_down)
    final = after + mlp_saved[-1]
    d_final = jnp.where(is_valid[:, None], weight_cot.astype(jnp.float32) * factor, 0.0)
    d_part, gain_mlp, d_win, d_wdown = plain_mlp_back(d_final, after, mlp_saved, gains[2], w_in, w_down)
    d_after = d_final + d_part
    d_low = d_after.astype(jnp.bfloat16)
    d_wback = plain_product(cross_low.T, d_low)
    d_cross = plain_product(d_low, w_back.T).astype(jnp.bfloat16)
    d_query, d_key, d_value = plain_attend_back(queries, mem_keys, mem_values, None, cross_total, d_cross)
    d_query_low = d_query.astype(jnp.bfloat16)
    d_wquery = plain_product(normed_low.T, d_query_low)
    d_normed = plain_product(d_query_low, w_query.T)
    d_norm_in, gain_cross = plain_norm_back(d_normed, middle, inv_root, gains[1])
    d_middle = d_after + d_norm_in
    d_keyvalue = jnp.concatenate([d_key, d_value], axis=1).astype(jnp.bfloat16)
    d_first, gain_attn, d_wqkv, d_wout = plain_attention_back(
        d_middle, inputs, attn_saved, gains[0], w_qkv, w_out, key_mask
    )
    grads = (
        jnp.stack([gain_attn, gain_cross, gain_mlp]),
        d_wqkv,
        d_wout,
        jnp.concatenate([d_wquery, d_wback], axis=1),
        d_win,
        d_wdown,
    )
    return (final.astype(jnp.bfloat16), d_middle + d_first, d_keyvalue, grads)


def on_section(flag, work, operands):

    def run_work(values):
        return work(*values)

    def skip_work(values):
        return jax.tree.map(jnp.zeros_like, work(*values))

    return lax.cond(flag, run_work, skip_work, operands)


def plain_body(
    block_in,
    cotangent,
    lengths,
    sources,
    loss_weight,
    gains,
    qkv_weight,
    out_weight,
    cross_weight,
    in_weight,
    down_weight,
):
    is_encoder = lax.axis_index("section") == 0
    is_decoder = jnp.logical_not(is_encoder)
    wide = lax.axis_size("dp")
    gathered = (
        lax.all_gather(gains, "dp", axis=2, tiled=True),
        lax.all_gather(qkv_weight, "dp", axis=1, tiled=True),
        lax.all_gather(out_weight, "dp", axis=1, tiled=True),
        lax.all_gather(cross_weight, "dp", axis=1, tiled=True),
        lax.all_gather(in_weight, "dp", axis=1, tiled=True),
        lax.all_gather(down_weight, "dp", axis=1, tiled=True),
    )
    weights = tuple((w[0] for w in gathered))
    onehot = (sources[:, None] == jnp.arange(3, dtype=jnp.int32)[None, :]).astype(jnp.float32)
    counts = lax.psum(jnp.sum(onehot * lengths[:, None].astype(jnp.float32), axis=0), "dp")
    own_count = jnp.sum(onehot * counts[None, :], axis=1)
    own_weight = jnp.sum(onehot * loss_weight[None, :].astype(jnp.float32), axis=1)
    scale = own_weight * (lengths.shape[0] * wide * block_in.shape[2] / 3.0) / own_count

    def step(carry, item):
        source, weight_cot, length, factor = item
        key_value, memory = on_section(is_encoder, encoder_front, (weights, source))
        received = shifted(key_value, "section", 1)
        decoded, table_grad, d_keyvalue, dec_grads = on_section(
            is_decoder, decoder_pass, (weights, source, received, weight_cot, length, factor)
        )
        returned = shifted(d_keyvalue, "section", -1)
        plot_grad, enc_grads = on_section(is_encoder, encoder_back, (weights, source, returned))
        grads = tuple((a + b for a, b in zip(dec_grads, enc_grads)))
        carry = tuple((a + b for a, b in zip(carry, grads)))
        return (carry, (memory + decoded, plot_grad + table_grad))

    start = tuple((jnp.zeros(w.shape, jnp.float32) for w in weights))
    carry, (outputs, input_grads) = lax.scan(step, start, (block_in[0], cotangent, lengths, scale))
    gain_total, qkv_total, out_total, cross_sum, in_total, down_total = carry
    reduced = (
        lax.psum_scatter(gain_total[None], "dp", scatter_dimension=2, tiled=True),
        lax.psum_scatter(qkv_total[None], "dp", scatter_dimension=1, tiled=True),
        lax.psum_scatter(out_total[None], "dp", scatter_dimension=1, tiled=True),
        lax.psum_scatter(cross_sum[None], "dp", scatter_dimension=1, tiled=True),
        lax.psum_scatter(in_total[None], "dp", scatter_dimension=1, tiled=True),
        lax.psum_scatter(down_total[None], "dp", scatter_dimension=1, tiled=True),
    )
    return (
        outputs[None],
        input_grads[None],
        reduced[0],
        reduced[1],
        reduced[2],
        reduced[3],
        reduced[4],
        reduced[5],
    )


def tiled_body(
    block_in, cotangent, lengths, sources, loss_weight, gains, qkv_weight, out_weight, cross_weight, in_weight, down_weight
):
    wide = lax.axis_size("dp")
    pairs, seq, width = block_in.shape[1:]
    own = gains.shape[2]
    x = block_in.reshape(pairs * seq, width)
    (
        _, w_qkv, w_out, w_enc, w_dec, w_in, w_down, *saved, gains_full, factors
    ) = forward(
        wide, seq, lengths, sources, loss_weight, gains[0], x,
        qkv_weight[0], out_weight[0], cross_weight[0], in_weight[0], down_weight[0],
    )
    block_out, input_grad, *_, down, inner, cross, out, qkv, gains_sum = backward(
        wide, seq, own, lengths, factors, x, gains_full, cotangent.reshape(pairs * seq, width), saved,
        (w_qkv, w_out, w_enc, w_dec, w_in, w_down),
    )
    return (
        block_out.reshape(block_in.shape),
        input_grad.reshape(block_in.shape),
        gains_sum[None, :3, :own],
        qkv[None],
        out[None],
        cross[None],
        inner[None],
        down[None],
    )


def solution(mesh):
    in_specs = (
        P("section", "dp", None, None),
        P("dp", None, None),
        P("dp"),
        P("dp"),
        P(),
        P("section", None, "dp"),
        P("section", "dp", None),
        P("section", "dp", None),
        P("section", "dp", None),
        P("section", "dp", None),
        P("section", "dp", None),
    )
    out_specs = (
        P("section", "dp", None, None),
        P("section", "dp", None, None),
        P("section", None, "dp"),
        P("section", "dp", None),
        P("section", "dp", None),
        P("section", "dp", None),
        P("section", "dp", None),
        P("section", "dp", None),
    )

    def body(*args):
        shards = args[6:]
        tiled = args[5].shape[2] <= 128 and all(w.shape[1] % 16 == 0 for w in shards)
        return (tiled_body if tiled else plain_body)(*args)

    return jax.shard_map(body, mesh=mesh, in_specs=in_specs, out_specs=out_specs, check_vma=False)
```

```python
from functools import partial

import jax
import jax.numpy as jnp
from jax import lax
from jax.experimental import pallas as pl
from jax.experimental.pallas import tpu as pltpu
from jax.sharding import PartitionSpec as P

HEADS = 12
HEAD_DIM = 64


EPS = 1e-06
NEG = -1000000000.0


MESH = pl.DeviceIdType.MESH
VMEM_LIMIT = 62 * 2**20
F32, BF16 = jnp.float32, jnp.bfloat16
ANY = pl.BlockSpec(memory_space=pl.ANY)
SMEM = pl.BlockSpec(memory_space=pltpu.SMEM)
VMEM = pl.BlockSpec(memory_space=pltpu.VMEM)


def ring_position(chip, chips):
    return jnp.where(chip % 2 == 0, chip // 2, chips - 1 - chip // 2)


def ring_chip(position, chips):
    position = lax.rem(position + 2 * chips, chips)
    return jnp.where(position < chips // 2, 2 * position, 2 * (chips - 1 - position) + 1)


def ring_hops(long_way, chips):
    long, short = chips // 2, chips - 1 - chips // 2
    return (long, short) if long_way == 0 else (short, long)


def slot_of(long_way, way, distance, chips):
    return distance if distance == 0 or way == long_way else chips // 2 + distance


def entry_barrier(partners):
    barrier = pltpu.get_barrier_semaphore()
    for partner in partners:
        pl.semaphore_signal(barrier, inc=1, device_id=partner, device_id_type=MESH)
    pl.semaphore_wait(barrier, len(partners))


def remote(src, dst, send_sem, recv_sem, target):
    return pltpu.make_async_remote_copy(
        src_ref=src,
        dst_ref=dst,
        send_sem=send_sem,
        recv_sem=recv_sem,
        device_id=target,
        device_id_type=MESH,
    )


class Place:
    def __init__(self, wide):
        self.chips = wide // 2
        self.section, self.me = lax.axis_index("section"), lax.axis_index("dp")
        self.chip, self.core = self.me // 2, lax.rem(self.me, 2)
        self.spot = ring_position(self.chip, self.chips)
        self.ahead = (self.section, 2 * ring_chip(self.spot + 1, self.chips) + self.core)
        self.behind = (self.section, 2 * ring_chip(self.spot - 1, self.chips) + self.core)
        self.twin = (self.section, 2 * self.chip + 1 - self.core)
        self.across = (1 - self.section, self.me)

    def next_of(self, way):
        return self.ahead if way == 0 else self.behind

    def chip_at(self, way, distance):
        return ring_chip(self.spot + distance if way == 0 else self.spot - distance, self.chips)


def block_rows(ref, rows, chip, core):
    return ref.at[pl.ds(pl.multiple_of((2 * chip + core) * rows, rows), rows)]


class Gather:
    def __init__(self, place, names, shards, fulls, rows, long_way, sems):
        self.place, self.names = place, names
        self.shards, self.fulls, self.rows, self.long_way = shards, fulls, rows, long_way
        self.own_sem, self.ring_send, self.ring_recv, self.twin_send, self.twin_recv = sems

    def hops(self, name, way):
        return ring_hops(self.long_way[name], self.place.chips)[way]

    def pieces(self, name, way, hop):
        at = self.place
        origin = at.chip_at(way, -hop)
        target = block_rows(self.fulls[name], self.rows[name], origin, at.core)
        own = self.shards.get(name)
        return (own if hop == 0 and own is not None else target), target

    def ring(self, name, way, hop):
        source, target = self.pieces(name, way, hop)
        i = self.names.index(name)
        return remote(
            source, target, self.ring_send.at[i, way, hop], self.ring_recv.at[i, way, hop], self.place.next_of(way)
        )

    def pair(self, name, way, hop):
        source, target = self.pieces(name, way, hop)
        i, slot = self.names.index(name), slot_of(self.long_way[name], way, hop, self.place.chips)
        return remote(source, target, self.twin_send.at[i, slot], self.twin_recv.at[i, slot], self.place.twin)

    def own(self, name):
        source, target = self.pieces(name, 0, 0)
        return pltpu.make_async_copy(source, target, self.own_sem.at[self.names.index(name)])

    def start(self, name):
        for way in range(2):
            self.ring(name, way, 0).start()
        self.pair(name, 0, 0).start()
        if name in self.shards:
            self.own(name).start()

    def step(self, name, hop):
        for way in range(2):
            hops = self.hops(name, way)
            if hop < hops:
                self.ring(name, way, hop).wait_recv()
                if hop + 1 < hops:
                    self.ring(name, way, hop + 1).start()
                self.pair(name, way, hop + 1).start()

    def complete(self, name):
        if name in self.shards:
            self.own(name).wait()
        self.pair(name, 0, 0).wait_recv()
        for way in range(2):
            for hop in range(self.hops(name, way)):
                self.pair(name, way, hop + 1).wait_recv()

    def drain(self, names):
        for name in names:
            self.pair(name, 0, 0).wait_send()
            for way in range(2):
                for hop in range(self.hops(name, way)):
                    self.pair(name, way, hop + 1).wait_send()
                    self.ring(name, way, hop).wait_send()


LONG_WAY = {"small": 0, "qkv": 0, "out": 1, "crossE": 0, "crossD": 1, "in": 1, "down": 0, "gains": 0}


class Scatter:
    def __init__(self, place, names, grads, rows, long_way, twins, arrived, sems):
        self.place, self.names, self.grads, self.rows, self.long_way = place, names, grads, rows, long_way
        self.twins, self.arrived = twins, arrived
        self.twin_send, self.twin_recv, self.ring_send, self.ring_recv = sems

    def hops(self, name, way):
        return ring_hops(self.long_way[name], self.place.chips)[way]

    def landing(self, name, way, hop):
        return self.arrived[name].at[hop if way == self.long_way[name] else self.place.chips // 2 + hop]

    def block(self, name, way, distance, core):
        return block_rows(self.grads[name], self.rows[name], self.place.chip_at(way, distance), core)

    def pair(self, name, way, distance):
        at, i = self.place, self.names.index(name)
        slot = slot_of(self.long_way[name], way, distance, at.chips)
        source = self.block(name, way, distance, 1 - at.core)
        return remote(source, self.twins[name].at[slot], self.twin_send.at[i, slot], self.twin_recv.at[i, slot], at.twin)

    def ring(self, name, way, hop):
        at, i = self.place, self.names.index(name)
        return remote(
            self.block(name, way, self.hops(name, way) - hop, at.core),
            self.landing(name, way, hop),
            self.ring_send.at[i, way, hop],
            self.ring_recv.at[i, way, hop],
            at.next_of(way),
        )

    def slots(self, name):
        found = []
        for hop in range(self.place.chips // 2 + 1):
            for way in range(2):
                distance = self.hops(name, way) - hop
                if distance > 0 or (distance == 0 and way == self.long_way[name]):
                    found.append((way, distance))
        return found

    def start(self, name):
        for way, distance in self.slots(name):
            self.pair(name, way, distance).start()

    def add(self, name, way, distance, terms, out=None):
        at, rows, grad = self.place, self.rows[name], self.grads[name]
        group = rows if rows * grad.shape[1] <= 48 * 1536 else (16 if rows % 64 else 64)
        first = (2 * at.chip_at(way, distance) + at.core) * rows
        slot = slot_of(self.long_way[name], way, distance, at.chips)

        @pl.loop(0, rows // group)
        def _(n):
            part = span(n * group, group)
            own = pl.ds(pl.multiple_of(first + n * group, group), group)
            total = grad[own].astype(F32) + self.twins[name][slot, part].astype(F32)
            for term in terms:
                total += term[part].astype(F32)
            if out is None:
                grad[own] = total.astype(grad.dtype)
            else:
                out[part] = total

    def step(self, name, way, hop):
        distance = self.hops(name, way) - hop
        if distance <= 0:
            return
        self.pair(name, way, distance).wait_recv()
        terms = []
        if hop > 0:
            self.ring(name, way, hop - 1).wait_recv()
            terms.append(self.landing(name, way, hop - 1))
        self.add(name, way, distance, terms)
        self.ring(name, way, hop).start()

    def finish(self, name, out):
        self.pair(name, self.long_way[name], 0).wait_recv()
        terms = []
        for way in range(2):
            last = self.hops(name, way) - 1
            self.ring(name, way, last).wait_recv()
            terms.append(self.landing(name, way, last))
        self.add(name, self.long_way[name], 0, terms, out)

    def drain(self, name):
        for way, distance in self.slots(name):
            self.pair(name, way, distance).wait_send()
        for way in range(2):
            for hop in range(self.hops(name, way)):
                self.ring(name, way, hop).wait_send()


def dot(a, b, over_a=1, over_b=0):
    return lax.dot_general(a, b, (((over_a,), (over_b,)), ((), ())), preferred_element_type=F32)


def span(start, size):
    return pl.ds(pl.multiple_of(start, size), size)


def each(total, tile, work):
    @pl.loop(0, total // tile)
    def _(n):
        work(span(n * tile, tile))


ROWS = 64


def norm_into(h_ref, gain, out_ref):
    def work(at):
        h = h_ref[at].astype(F32)
        inv_root = lax.rsqrt(jnp.mean(h * h, axis=-1, keepdims=True) + EPS)
        out_ref[at] = (h * inv_root * gain).astype(out_ref.dtype)

    each(h_ref.shape[0], ROWS, work)


def norm_back(dn_ref, h_ref, gain, gain_sum, row, finish, start=0, size=None):
    if start == 0:
        gain_sum[row] = jnp.zeros(gain_sum.shape[1:], F32)

    def work(part):
        at = span(start + part.start, ROWS)
        h, dn = h_ref[at].astype(F32), dn_ref[at].astype(F32)
        inv_root = lax.rsqrt(jnp.mean(h * h, axis=-1, keepdims=True) + EPS)
        scaled = h * inv_root
        product = dn * scaled
        gain_sum[row] += jnp.sum(product.reshape(-1, 8, product.shape[1]), axis=0)
        inner = dn * gain
        finish(at, inv_root * (inner - scaled * jnp.mean(product * gain, axis=-1, keepdims=True)))

    each(size or h_ref.shape[0], ROWS, work)


def pair_columns(ref, rows, start, two):
    return ref[rows, span(start + two * 2 * HEAD_DIM, 2 * HEAD_DIM)]


def side_masks():
    lane = lax.broadcasted_iota(jnp.int32, (1, 2 * HEAD_DIM), 1)
    first = lane < HEAD_DIM
    return first, (first.astype(F32).astype(BF16), (1 - first.astype(F32)).astype(BF16))


def expo_columns(q, k, seq, length):
    scores = dot(k, q, 1, 1) * HEAD_DIM ** (-0.5)
    if length is not None:
        key = lax.broadcasted_iota(jnp.int32, (seq, seq), 0)
        query = lax.broadcasted_iota(jnp.int32, (seq, seq), 1)
        scores = jnp.where((key <= query) & (key < length), scores, NEG)
    expo = jnp.exp(scores - jnp.max(scores, axis=0, keepdims=True))
    return expo, jnp.sum(expo, axis=0, keepdims=True)


def attend(q_ref, q_at, k_ref, k_at, v_ref, v_at, out_ref, seq, lengths, chosen=None):
    start, stop = chosen or (0, q_ref.shape[0] // seq)
    first, keeps = side_masks()
    each_time = HEADS // 2

    @pl.loop(start * (HEADS // 2) // each_time, stop * (HEADS // 2) // each_time)
    def _(m):
        work = []
        for g in range(each_time):
            n = m * each_time + g
            pair, two = n // (HEADS // 2), lax.rem(n, HEADS // 2)
            rows = span(pair * seq, seq)
            length = None if lengths is None else lengths[pair]
            q, k, v = (pair_columns(r, rows, a, two) for r, a in ((q_ref, q_at), (k_ref, k_at), (v_ref, v_at)))
            for side in range(2):
                work.append((rows, two, length, q, k, v, side))
        expos = [expo_columns(q * keeps[side], k, seq, length) for rows, two, length, q, k, v, side in work]
        outs = [dot((e * (1.0 / t)).astype(BF16), w[5], 0, 0) for (e, t), w in zip(expos, work)]
        for g in range(each_time):
            rows, two = work[2 * g][:2]
            value = jnp.where(first, outs[2 * g], outs[2 * g + 1])
            out_ref[rows, span(two * 2 * HEAD_DIM, 2 * HEAD_DIM)] = value.astype(BF16)


def attend_back(q_ref, q_at, k_ref, k_at, v_ref, v_at, do_ref, dq, dk, dv, seq, lengths, chosen=None):
    start, stop = chosen or (0, q_ref.shape[0] // seq)
    first, keeps = side_masks()
    root = HEAD_DIM ** (-0.5)
    each_time = HEADS // 4

    @pl.loop(start * (HEADS // 2) // each_time, stop * (HEADS // 2) // each_time)
    def _(m):
        work = []
        for g in range(each_time):
            n = m * each_time + g
            pair, two = n // (HEADS // 2), lax.rem(n, HEADS // 2)
            rows = span(pair * seq, seq)
            length = None if lengths is None else lengths[pair]
            q, k, v = (pair_columns(r, rows, a, two) for r, a in ((q_ref, q_at), (k_ref, k_at), (v_ref, v_at)))
            d_out = pair_columns(do_ref, rows, 0, two)
            for side in range(2):
                work.append((rows, two, length, q, k, v, d_out, side))
        expos = [expo_columns(q * keeps[side], k, seq, length) for rows, two, length, q, k, v, d_out, side in work]
        d_probs = [dot(v, d_out * keeps[side], 1, 1) for rows, two, length, q, k, v, d_out, side in work]
        probs = [e * (1.0 / t) for e, t in expos]
        d_scores = [(p * (d - jnp.sum(p * d, axis=0, keepdims=True))).astype(BF16) for p, d in zip(probs, d_probs)]
        dvs = [dot(p.astype(BF16), w[6]) for p, w in zip(probs, work)]
        dqs = [dot(d, w[4], 0, 0) for d, w in zip(d_scores, work)]
        dks = [dot(d, w[3]) for d, w in zip(d_scores, work)]
        for g in range(each_time):
            rows, two = work[2 * g][:2]
            for (ref, start), both, factor in ((dq, dqs, root), (dk, dks, root), (dv, dvs, 1.0)):
                value = jnp.where(first, both[2 * g], both[2 * g + 1]) * factor
                ref[rows, span(start + two * 2 * HEAD_DIM, 2 * HEAD_DIM)] = value.astype(BF16)


def gelu_parts(gate):
    root, cubic = 0.7978845608028654, 0.044715
    square = gate * gate
    bent = jnp.tanh(root * gate * (1.0 + cubic * square))
    half = 0.5 * (1.0 + bent)
    slope = half + 0.5 * gate * (1.0 - bent * bent) * root * (1.0 + 3.0 * cubic * square)
    return gate * half, slope


FF_TILE = 512


def mlp_forward(a_ref, w_in, w_down, into_ref, hidden_ref=None, slopes_ref=None):
    ff = w_in.shape[1] // 2

    @pl.loop(0, ff // FF_TILE)
    def _(n):
        gates, uppers = span(n * FF_TILE, FF_TILE), span(ff + n * FF_TILE, FF_TILE)
        gate, upper = dot(a_ref[...], w_in[:, gates]), dot(a_ref[...], w_in[:, uppers])
        active, slope = gelu_parts(gate)
        hidden = (active * upper).astype(BF16)
        if hidden_ref is not None:
            hidden_ref[:, gates] = hidden
            slopes_ref[:, gates] = (slope * upper).astype(BF16)
            slopes_ref[:, uppers] = active.astype(BF16)
        if w_down is not None:
            into_ref[...] += dot(hidden, w_down[gates, :])


def mlp_back(d_low, w_in, w_down, slopes_ref, dn_ref, half):
    ff = w_in.shape[1] // 2
    if half == 0:
        dn_ref[...] = jnp.zeros(dn_ref.shape, F32)

    @pl.loop(half * ff // FF_TILE // 2, (half + 1) * ff // FF_TILE // 2)
    def _(n):
        gates, uppers = span(n * FF_TILE, FF_TILE), span(ff + n * FF_TILE, FF_TILE)
        d_hidden = dot(d_low[...], w_down[gates, :], 1, 1)
        d_gate = (d_hidden * slopes_ref[:, gates]).astype(BF16)
        d_upper = (d_hidden * slopes_ref[:, uppers]).astype(BF16)
        slopes_ref[:, gates], slopes_ref[:, uppers] = d_gate, d_upper
        dn_ref[...] += dot(d_gate, w_in[:, gates], 1, 1) + dot(d_upper, w_in[:, uppers], 1, 1)


def product_into(a_ref, w_ref, out_ref, tile, w_at=0, transposed=False):
    width = out_ref.shape[1]

    @pl.loop(0, width // tile)
    def _(n):
        if transposed:
            value = dot(a_ref[...], w_ref[span(w_at + n * tile, tile), :], 1, 1)
        else:
            value = dot(a_ref[...], w_ref[:, span(w_at + n * tile, tile)])
        out_ref[:, span(n * tile, tile)] = value.astype(out_ref.dtype)


def add_product(base_ref, a_ref, w, out_ref):
    out_ref[...] = base_ref[...].astype(F32) + dot(a_ref[...], w)


class Moves:
    def __init__(self, sems):
        self.sems, self.used = sems, 0

    def start(self, src, dst):
        copy = pltpu.make_async_copy(src, dst, self.sems.at[self.used])
        self.used += 1
        copy.start()
        return copy


def weight_grad(a_ref, y_ref, grad, tile_rows, tile_columns, column_at=0):
    depth, width = a_ref.shape[1], y_ref.shape[1]
    for i in range(depth // tile_rows):
        for j in range(width // tile_columns):
            rows, columns = pl.ds(i * tile_rows, tile_rows), pl.ds(j * tile_columns, tile_columns)
            value = dot(a_ref[:, rows], y_ref[:, columns], 0, 0).astype(BF16)
            grad[rows, pl.ds(column_at + j * tile_columns, tile_columns)] = value


GATHER_NAMES = ("small", "qkv", "out", "crossE", "crossD", "in", "down")
SCATTER_NAMES = ("down", "in", "crossD", "crossE", "out", "qkv", "gains")
BLOCK = (8, 128)


def spread_gains(small, own, width):
    lane = lax.broadcasted_iota(jnp.int32, BLOCK, 1)
    total = jnp.zeros((BLOCK[0], width), F32)
    for n in range(width // own):
        part = jnp.where(lane < own, small[n * BLOCK[0] : (n + 1) * BLOCK[0], :], 0.0)
        wide = jnp.concatenate([part, jnp.zeros((BLOCK[0], width - BLOCK[1]), F32)], axis=1)
        total += wide if n == 0 else pltpu.roll(wide, n * own, 1)
    return total


def gather_blocks(gains_grad, own, out_ref):
    width = gains_grad.shape[1]
    lane = lax.broadcasted_iota(jnp.int32, BLOCK, 1)
    for n in range(width // own):
        turned = gains_grad if n == 0 else pltpu.roll(gains_grad, width - n * own, 1)
        out_ref[n * BLOCK[0] : (n + 1) * BLOCK[0], :] = jnp.where(lane < own, turned[:, : BLOCK[1]], 0.0)


def step_kernel(
    wide, seq, lengths, sources, loss_weight, gains_in, x_in, cot_in, qkv_in, out_in, cross_in, in_in, down_in,
    small_full, qkv_full, out_full, enc_full, dec_full, in_full, down_full,
    joined_kept, attended_kept, middle_kept, final_kept,
    block_out, input_out, down_sum, in_sum, cross_sum, out_sum, qkv_sum, gains_sum,
    small_own, gains, factors, gain_sum, landing, back, passed_out, passed_in, g_gains, g_down, *refs,
):
    count = len(SCATTER_NAMES)
    twins, arrived = dict(zip(SCATTER_NAMES, refs[:count])), dict(zip(SCATTER_NAMES, refs[count : 2 * count]))
    load_sem, send_sem, recv_sem = refs[2 * count : 2 * count + 3]
    gather_sems, scatter_sems = refs[2 * count + 3 : 2 * count + 8], refs[2 * count + 8 :]
    at = Place(wide)
    rows, width = x_in.shape
    pairs, own = rows // seq, gains_in.shape[1]
    vmem = pltpu.VMEM
    broad, slim = vmem((rows, width), F32), vmem((rows, width), BF16)
    lane = lax.broadcasted_iota(jnp.int32, (1, BLOCK[1]), 1)
    counted = jnp.zeros((1, BLOCK[1]), F32)
    for pair in range(pairs):
        counted += jnp.where(lane == sources[pair], lengths[pair].astype(F32), 0.0)
    small_own[...] = jnp.zeros(BLOCK, F32)
    small_own[0:3, 0:own] = gains_in[...].astype(F32)
    small_own[3:4, :] = counted
    entry_barrier((at.ahead, at.behind, at.twin, at.across))

    fulls = dict(zip(GATHER_NAMES, (small_full, qkv_full, out_full, enc_full, dec_full, in_full, down_full)))
    full_rows = {n: f.shape[0] // wide for n, f in fulls.items()}
    w_qkv_shape, w_out_shape, w_cross_shape = qkv_full.shape, out_full.shape, dec_full.shape
    w_in_shape, w_down_shape = in_full.shape, down_full.shape
    ff = w_down_shape[0]
    shapes = dict(zip(SCATTER_NAMES, (w_down_shape, w_in_shape, w_cross_shape, w_cross_shape, w_out_shape, w_qkv_shape)))
    shapes["gains"] = g_gains.shape
    share = {n: s[0] // wide for n, s in shapes.items()}
    grads = {"down": g_down, "gains": g_gains}
    scatter = Scatter(at, SCATTER_NAMES, grads, share, LONG_WAY, twins, arrived, scatter_sems)
    sums = {"down": down_sum, "in": in_sum, "out": out_sum, "qkv": qkv_sum, "gains": gains_sum}
    sums.update(crossD=cross_sum, crossE=passed_out)
    passed_weight = remote(
        cross_in, block_rows(enc_full, full_rows["crossE"], at.chip, at.core), send_sem.at[0], recv_sem.at[0], at.across
    )
    passed_sum = remote(passed_out, passed_in, send_sem.at[1], recv_sem.at[1], at.across)

    def grad_space(*names):
        return [vmem(shapes[n], BF16) for n in names]

    def to_dec(pair):
        part = pl.ds(pair * seq, seq)
        return remote(back.at[part], landing.at[part], send_sem.at[2 + pair], recv_sem.at[2 + pair], at.across)

    def to_enc(pair):
        part, i = pl.ds(pair * seq, seq), 2 + pairs + pair
        return remote(back.at[part], landing.at[part], send_sem.at[i], recv_sem.at[i], at.across)

    class Hops:
        def __init__(self):
            self.done = {}

        def hop(self, *names):
            for name in names:
                for way in range(2):
                    scatter.step(name, way, self.done.get(name, 0))
                self.done[name] = self.done.get(name, 0) + 1

        def ready(self, name):
            scatter.start(name)
            self.hop(name)

        def rest(self, names):
            for step in range(at.chips // 2 + 1):
                for name in names:
                    if self.done[name] == step < at.chips // 2:
                        self.hop(name)
                    elif self.done[name] == step:
                        scatter.finish(name, sums[name])
                        self.done[name] += 1
                        if name == "crossE":
                            passed_sum.start()

    def first_part(moves, gather, names, lengths, x, small, w_qkv, w_out, normed, joined, attended, middle, between):
        load_x = moves.start(x_in, x)
        for name in names:
            if name == "crossE":
                passed_weight.wait_recv()
            gather.start(name)
        for hop in range(at.chips // 2 - 1):
            for name in names:
                gather.step(name, hop)

        def load(name, into):
            gather.complete(name)
            return moves.start(fulls[name], into)

        gather.step("small", at.chips // 2 - 1)
        load("small", small).wait()
        gains[...] = spread_gains(small, own, width)
        totals = jnp.zeros((1, BLOCK[1]), F32)
        for n in range(wide):
            totals += small[n * BLOCK[0] + 3 : n * BLOCK[0] + 4, :]
        factors[...] = jnp.zeros(factors.shape, F32)
        for pair in range(pairs):
            source = sources[pair]
            weight = jnp.where(source == 0, loss_weight[0], jnp.where(source == 1, loss_weight[1], loss_weight[2]))
            total = jnp.sum(jnp.where(lane == source, totals, 0.0), axis=1, keepdims=True)
            factor = jnp.full((1, 1), weight.astype(F32) * (pairs * wide * seq / 3.0), F32) / total
            factors[pair : pair + 1, :] = jnp.broadcast_to(factor, (1, BLOCK[1]))
        load_x.wait()
        norm_into(x, gains[0:1], normed)
        gather.step("qkv", at.chips // 2 - 1)
        gather.step("out", at.chips // 2 - 1)
        load_qkv = load("qkv", w_qkv)
        load_out = load("out", w_out)
        load_qkv.wait()
        product_into(normed, w_qkv, joined, width)
        for name in names[3:]:
            gather.step(name, at.chips // 2 - 1)
        for pair in range(pairs):
            attend(joined, 0, joined, width, joined, 2 * width, attended, seq, lengths, (pair, pair + 1))
            if pair == 0:
                between()
        load_out.wait()
        add_product(x, attended, w_out[...], middle)
        return [moves.start(a, b) for a, b in ((middle, middle_kept), (joined, joined_kept), (attended, attended_kept))]

    def self_back(hops, lengths, d_middle, x, normed, d_low, w_qkv, w_out, joined, attended, d_attended, dn, loads, first, second, third):
        each(rows, ROWS, lambda part: d_low.__setitem__(part, d_middle[part].astype(BF16)))
        weight_grad(attended, d_low, grads["out"], width, width)
        hops.ready("out")
        product_into(d_low, w_out, d_attended, width, transposed=True)
        hops.hop(*first)
        for load in loads:
            load.wait()
        for pair in range(pairs):
            attend_back(
                joined, 0, joined, width, joined, 2 * width, d_attended,
                (joined, 0), (joined, width), (joined, 2 * width), seq, lengths, (pair, pair + 1),
            )
            hops.hop(*(second, third)[min(pair, 1)])
        norm_into(x, gains[0:1], normed)
        weight_grad(normed, joined, grads["qkv"], width, width)
        hops.ready("qkv")
        product_into(joined, w_qkv, dn, width, transposed=True)

        def finish(part, d_input):
            d_middle[part] = d_middle[part] + d_input

        norm_back(dn, x, gains[0:1], gain_sum, 0, finish)

    def gains_ready(hops):
        lines = [jnp.sum(gain_sum[row], axis=0, keepdims=True) for row in range(3)]
        gather_blocks(jnp.concatenate(lines + [jnp.zeros((BLOCK[0] - 3, width), F32)], axis=0), own, g_gains)
        hops.ready("gains")

    @pl.when(at.section == 0)
    def _():
        moves, hops = Moves(load_sem), Hops()
        passed_weight.start()
        names = ("small", "qkv", "out", "in", "down")
        shards = dict(zip(names, (small_own, qkv_in, out_in, in_in, down_in)))
        gather = Gather(at, GATHER_NAMES, shards, fulls, full_rows, LONG_WAY, gather_sems)

        def ahead(x, small, w_qkv, w_out, normed, joined, attended, middle, w_in, w_down):
            loads = []

            def between():
                for name, into in (("in", w_in), ("down", w_down)):
                    gather.complete(name)
                    loads.append(moves.start(fulls[name], into))

            stores = first_part(
                moves, gather, names, None, x, small, w_qkv, w_out, normed, joined, attended, middle, between
            )
            norm_into(middle, gains[1:2], normed)
            for copy in loads + stores[:1]:
                copy.wait()
            mlp_forward(normed, w_in, w_down, middle)
            stores.append(moves.start(middle, final_kept))
            for pair in range(pairs):
                part = pl.ds(pair * seq, seq)
                norm_into(middle.at[part], gains[2:3], back.at[part])
                to_dec(pair).start()
            stores.append(moves.start(back, block_out))
            for copy in stores[1:]:
                copy.wait()

        pl.run_scoped(
            ahead,
            slim, vmem(small_full.shape, F32), vmem(w_qkv_shape, BF16), vmem(w_out_shape, BF16),
            slim, vmem((rows, 3 * width), BF16), slim, broad, vmem(w_in_shape, BF16), vmem(w_down_shape, BF16),
        )

        def backward(final, normed, w_out, attended, g_in, g_out, g_qkv):
            grads.update({"in": g_in, "out": g_out, "qkv": g_qkv})
            early = [moves.start(a, b) for a, b in ((out_full, w_out), (attended_kept, attended))]

            def feed(w_in, w_down, middle, hidden, slopes, d_low, dn):
                loads = [
                    moves.start(a, b)
                    for a, b in ((middle_kept, middle), (in_full, w_in), (final_kept, final), (down_full, w_down))
                ]
                for load in loads:
                    load.wait()
                norm_into(middle, gains[1:2], normed)
                mlp_forward(normed, w_in, None, None, hidden, slopes)

                def finish_final(part, d_input):
                    final[part] = d_input
                    d_low[part] = d_input.astype(BF16)

                for pair in range(pairs):
                    to_enc(pair).wait_recv()
                    norm_back(landing, final, gains[2:3], gain_sum, 2, finish_final, pair * seq, seq)
                weight_grad(hidden, d_low, g_down, ff // 4, width)
                hops.ready("down")
                for half in range(2):
                    mlp_back(d_low, w_in, w_down, slopes, dn, half)
                    hops.hop("down")
                weight_grad(normed, slopes, g_in, width, ff // 4)
                hops.ready("in")
                hops.hop("down")

                def finish_middle(part, d_input):
                    final[part] = final[part] + d_input

                norm_back(dn, middle, gains[1:2], gain_sum, 1, finish_middle)

            pl.run_scoped(
                feed,
                vmem(w_in_shape, BF16), vmem(w_down_shape, BF16), broad, vmem((rows, ff), BF16), vmem((rows, 2 * ff), BF16),
                slim, broad,
            )

            def attention(w_qkv, x, joined, d_low, d_attended, dn):
                loads = [moves.start(a, b) for a, b in ((joined_kept, joined), (x_in, x), (qkv_full, w_qkv))]
                for load in early:
                    load.wait()
                self_back(
                    hops, None, final, x, normed, d_low, w_qkv, w_out, joined, attended, d_attended, dn, loads, ("in",), ("out",), ("in",)
                )
                store = moves.start(final, input_out)
                gains_ready(hops)
                hops.rest(("down", "in", "out", "qkv", "gains"))
                store.wait()

            pl.run_scoped(
                attention,
                vmem(w_qkv_shape, BF16), slim, vmem((rows, 3 * width), BF16), slim, slim, broad,
            )
            for name in ("down", "in", "out", "qkv", "gains"):
                scatter.drain(name)

        pl.run_scoped(backward, broad, slim, vmem(w_out_shape, BF16), slim, *grad_space("in", "out", "qkv"))
        gather.drain(names)
        passed_weight.wait_send()
        for pair in range(pairs):
            to_dec(pair).wait_send()
        passed_sum.wait_recv()
        cross_sum[...] = passed_in[...]

    @pl.when(at.section == 1)
    def _():
        moves, hops = Moves(load_sem), Hops()
        names = ("small", "qkv", "out", "crossD", "crossE", "in", "down")
        shards = {"small": small_own, "qkv": qkv_in, "out": out_in, "crossD": cross_in, "in": in_in, "down": down_in}
        gather = Gather(at, GATHER_NAMES, shards, fulls, full_rows, LONG_WAY, gather_sems)

        def ahead(x, small, w_qkv, w_out, normed, joined, attended, middle):
            stores = first_part(
                moves, gather, names, lengths, x, small, w_qkv, w_out, normed, joined, attended, middle, lambda: None
            )
            for store in stores:
                store.wait()

        pl.run_scoped(
            ahead,
            slim, vmem(small_full.shape, F32), vmem(w_qkv_shape, BF16), vmem(w_out_shape, BF16),
            slim, vmem((rows, 3 * width), BF16), slim, broad,
        )

        def rest(cot, normed_a, keyval, crossed, normed_b, slopes, d_low2, d_after):
            d_queries, d_keyval, memory = cot, keyval, landing

            def to_memory(w_enc, w_dec, w_in, w_down, queries, after, hidden, d_low, dn, d_crossed, middle):
                load_middle = moves.start(middle_kept, middle)
                load_cot = moves.start(cot_in, cot)
                loads = []
                for name, into in (("crossD", w_dec), ("crossE", w_enc)):
                    gather.complete(name)
                    loads.append(moves.start(fulls[name], into))
                load_middle.wait()
                norm_into(middle, gains[1:2], normed_a)
                loads[0].wait()
                product_into(normed_a, w_dec, queries, width)
                loads[1].wait()
                for pair in range(pairs):
                    part = pl.ds(pair * seq, seq)
                    to_dec(pair).wait_recv()
                    product_into(memory.at[part], w_enc, keyval.at[part], width)
                    attend(queries, 0, keyval, 0, keyval, width, crossed, seq, None, (pair, pair + 1))
                    if pair == 0:
                        for name, into in (("in", w_in), ("down", w_down)):
                            gather.complete(name)
                            loads.append(moves.start(fulls[name], into))
                add_product(middle, crossed, w_dec[:, width:], after)
                norm_into(after, gains[2:3], normed_b)
                for load in loads[2:] + [load_cot]:
                    load.wait()
                dn[...] = after[...]
                mlp_forward(normed_b, w_in, w_down, dn, hidden, slopes)

                for pair in range(pairs):

                    @pl.loop(0, seq // ROWS)
                    def _(n):
                        part = span(pair * seq + n * ROWS, ROWS)
                        position = n * ROWS + lax.broadcasted_iota(jnp.int32, (ROWS, 1), 0)
                        d_low2[part] = dn[part].astype(BF16)
                        factor = factors[pair : pair + 1, 0:1]
                        d_final = jnp.where(position < lengths[pair], cot[part].astype(F32) * factor, 0.0)
                        d_after[part] = d_final
                        d_low[part] = d_final.astype(BF16)

                store = moves.start(d_low2, block_out)
                weight_grad(hidden, d_low, g_down, ff // 4, width)
                hops.ready("down")
                for half in range(2):
                    mlp_back(d_low, w_in, w_down, slopes, dn, half)
                hops.hop("down")
                store.wait()

                def finish_after(part, d_input):
                    total = d_after[part] + d_input
                    d_after[part] = total
                    d_low2[part] = total.astype(BF16)

                norm_back(dn, after, gains[2:3], gain_sum, 2, finish_after)
                d_crossed[...] = dot(d_low2[...], w_dec[:, width:], 1, 1).astype(BF16)
                for pair in range(pairs):
                    part = pl.ds(pair * seq, seq)
                    attend_back(
                        queries, 0, keyval, 0, keyval, width, d_crossed,
                        (d_queries, 0), (d_keyval, 0), (d_keyval, width), seq, None, (pair, pair + 1),
                    )
                    back[part] = dot(d_keyval[part], w_enc[...], 1, 1).astype(BF16)
                    to_enc(pair).start()
                hops.hop("down")
                dn[...] = dot(d_queries[...], w_dec[:, :width], 1, 1)

                def finish_middle(part, d_input):
                    d_after[part] = d_after[part] + d_input

                norm_back(dn, middle, gains[1:2], gain_sum, 1, finish_middle)

            pl.run_scoped(
                to_memory,
                vmem(w_cross_shape, BF16), vmem(w_cross_shape, BF16), vmem(w_in_shape, BF16), vmem(w_down_shape, BF16),
                slim, broad, vmem((rows, ff), BF16), slim, broad, slim, broad,
            )

            def to_input(w_qkv, w_out, d_low, d_attended, dn, g_in, g_dec, g_enc, g_out, g_qkv):
                grads.update({"in": g_in, "crossD": g_dec, "crossE": g_enc, "out": g_out, "qkv": g_qkv})
                load_out = moves.start(out_full, w_out)
                loads = [moves.start(qkv_full, w_qkv)]
                weight_grad(normed_b, slopes, g_in, width, ff // 4)
                hops.ready("in")
                joined = slopes.at[:, pl.ds(0, 3 * width)]
                loads.append(moves.start(joined_kept, joined))
                weight_grad(memory, d_keyval, g_enc, width, width)
                hops.ready("crossE")
                loads.append(moves.start(x_in, memory))
                weight_grad(crossed, d_low2, g_dec, width, width, column_at=width)
                load_attended = moves.start(attended_kept, crossed)
                weight_grad(normed_a, d_queries, g_dec, width, width)
                hops.ready("crossD")
                load_out.wait()
                load_attended.wait()
                self_back(
                    hops, lengths, d_after, memory, normed_a, d_low, w_qkv, w_out, joined, crossed, d_attended, dn, loads,
                    ("down",), ("in",), ("crossE",),
                )
                store = moves.start(d_after, input_out)
                gains_ready(hops)
                hops.rest(("crossE", "down", "in", "crossD", "out", "qkv", "gains"))
                store.wait()
                for name in SCATTER_NAMES:
                    scatter.drain(name)

            pl.run_scoped(
                to_input,
                vmem(w_qkv_shape, BF16), vmem(w_out_shape, BF16), slim, slim, broad,
                *grad_space("in", "crossD", "crossE", "out", "qkv"),
            )

        pl.run_scoped(
            rest,
            slim, slim, vmem((rows, 2 * width), BF16), slim, slim, vmem((rows, 2 * ff), BF16), slim, broad,
        )
        gather.drain(names)
        for pair in range(pairs):
            to_enc(pair).wait_send()
        passed_sum.wait_send()


def run_step(wide, seq, lengths, sources, loss_weight, gains, x, cot, w_qkv, w_out, w_cross, w_in, w_down):
    (rows, width), chips, pairs = x.shape, wide // 2, x.shape[0] // seq
    vmem, shaped, dma = pltpu.VMEM, jax.ShapeDtypeStruct, pltpu.SemaphoreType.DMA
    fulls = [(wide * w.shape[0], w.shape[1]) for w in (w_qkv, w_out, w_cross, w_cross, w_in, w_down)]
    shares = [w.shape for w in (w_down, w_in, w_cross, w_cross, w_out, w_qkv)] + [BLOCK]
    types = [BF16] * 6 + [F32]
    gathered, scattered = len(GATHER_NAMES), len(SCATTER_NAMES)
    return pl.pallas_call(
        partial(step_kernel, wide, seq),
        out_shape=[shaped((wide * BLOCK[0], BLOCK[1]), F32)]
        + [shaped(f, BF16) for f in fulls]
        + [shaped((rows, 3 * width), BF16), shaped((rows, width), BF16)]
        + [shaped((rows, width), F32)] * 2
        + [shaped((rows, width), BF16), shaped((rows, width), F32)]
        + [shaped(shares[n], F32) for n in (0, 1, 2, 4, 5, 6)],
        in_specs=[SMEM] * 3 + [VMEM] + [ANY] * 7,
        out_specs=[ANY] * 13 + [VMEM] * 6,
        scratch_shapes=[
            vmem(BLOCK, F32),
            vmem((BLOCK[0], width), F32),
            vmem(BLOCK, F32),
            vmem((3, 8, width), F32),
            vmem((rows, width), BF16),
            vmem((rows, width), BF16),
            vmem(w_cross.shape, F32),
            vmem(w_cross.shape, F32),
            vmem((wide * BLOCK[0], BLOCK[1]), F32),
            vmem(fulls[5], BF16),
        ]
        + [vmem((chips,) + s, t) for s, t in zip(shares, types)]
        + [vmem((chips - 1,) + s, t) for s, t in zip(shares, types)]
        + [dma((64,)), dma((2 + 2 * pairs,)), dma((2 + 2 * pairs,))]
        + [dma((gathered,)), dma((gathered, 2, chips // 2)), dma((gathered, 2, chips // 2))]
        + [dma((gathered, chips)), dma((gathered, chips)), dma((scattered, chips)), dma((scattered, chips))]
        + [dma((scattered, 2, chips // 2)), dma((scattered, 2, chips // 2))],
        name="encoder_and_decoder",
        compiler_params=pltpu.CompilerParams(collective_id=0, has_side_effects=True, vmem_limit_bytes=VMEM_LIMIT),
    )(lengths, sources, loss_weight, gains, x, cot, w_qkv, w_out, w_cross, w_in, w_down)


def copy_kernel(count, *refs):
    blocks, gains, stored, gains_out = refs[:count], refs[count], refs[count + 1 : 2 * count + 1], refs[2 * count + 1]
    held, sems = refs[2 * count + 2 : -1], refs[-1]
    loads = [pltpu.make_async_copy(blocks[n], held[n], sems.at[n]) for n in range(count)]
    stores = [pltpu.make_async_copy(held[n], stored[n], sems.at[count + n]) for n in range(count)]
    for load in loads:
        load.start()
    gains_out[...] = gains[0 : gains_out.shape[0], 0 : gains_out.shape[1]]
    for load, store in zip(loads, stores):
        load.wait()
        store.start()
    for store in stores:
        store.wait()


def copied(arrays, gains, gains_shape):
    count = len(arrays)
    return pl.pallas_call(
        partial(copy_kernel, count),
        out_shape=[jax.ShapeDtypeStruct(a.shape, a.dtype) for a in arrays] + [jax.ShapeDtypeStruct(gains_shape, F32)],
        in_specs=[ANY] * count + [VMEM],
        out_specs=[ANY] * count + [VMEM],
        scratch_shapes=[pltpu.VMEM(a.shape, a.dtype) for a in arrays] + [pltpu.SemaphoreType.DMA((2 * count,))],
        name="outputs",
    )(*arrays, gains)


def shifted(block, axis, distance):
    devices = range(lax.axis_size(axis))
    route = [(i - distance, i) for i in devices if i - distance in devices]
    return lax.ppermute(block, axis, route)


def plain_product(a, b):
    return jnp.dot(a, b, preferred_element_type=jnp.float32)


def plain_split_heads(v):
    return v.reshape(v.shape[0], HEADS, -1)


def plain_norm_forward(h, norm_gain):
    inv_root = lax.rsqrt(jnp.mean(h * h, axis=-1, keepdims=True) + EPS)
    return (h * inv_root * norm_gain.astype(jnp.float32), inv_root)


def plain_norm_back(d_normed, h, inv_root, norm_gain):
    scaled = h * inv_root
    d_gain = jnp.sum(d_normed * scaled, axis=0)
    inner = d_normed * norm_gain.astype(jnp.float32)
    d_input = inv_root * (inner - scaled * jnp.mean(inner * scaled, axis=-1, keepdims=True))
    return (d_input, d_gain)


def plain_score_block(q, k, key_mask):
    scores = jnp.einsum(
        "qhd,khd->hqk", plain_split_heads(q), plain_split_heads(k), preferred_element_type=jnp.float32
    ) * HEAD_DIM ** (-0.5)
    if key_mask is not None:
        scores = jnp.where(key_mask[None], scores, NEG)
    return scores


def plain_attend_forward(q, k, v, key_mask):
    scores = plain_score_block(q, k, key_mask)
    highest = jnp.max(scores, axis=-1, keepdims=True)
    expo = jnp.exp(scores - highest)
    total = jnp.sum(expo, axis=-1, keepdims=True)
    weights = (expo / total).astype(jnp.bfloat16)
    output = jnp.einsum("hqk,khd->qhd", weights, plain_split_heads(v), preferred_element_type=jnp.float32)
    return (output.reshape(q.shape[0], -1), highest + jnp.log(total))


def plain_attend_back(q, k, v, key_mask, log_total, d_out):
    scores = plain_score_block(q, k, key_mask)
    probs = jnp.exp(scores - log_total)
    heads_dout = plain_split_heads(d_out)
    d_value = jnp.einsum(
        "hqk,qhd->khd", probs.astype(jnp.bfloat16), heads_dout, preferred_element_type=jnp.float32
    )
    d_probs = jnp.einsum(
        "qhd,khd->hqk", heads_dout, plain_split_heads(v), preferred_element_type=jnp.float32
    )
    centre = jnp.sum(probs * d_probs, axis=-1, keepdims=True)
    d_scores = (probs * (d_probs - centre)).astype(jnp.bfloat16)
    d_query = jnp.einsum(
        "hqk,khd->qhd", d_scores, plain_split_heads(k), preferred_element_type=jnp.float32
    ) * HEAD_DIM ** (-0.5)
    d_key = jnp.einsum(
        "hqk,qhd->khd", d_scores, plain_split_heads(q), preferred_element_type=jnp.float32
    ) * HEAD_DIM ** (-0.5)
    rows_query = q.shape[0]
    rows_key = k.shape[0]
    return (
        d_query.reshape(rows_query, -1),
        d_key.reshape(rows_key, -1),
        d_value.reshape(rows_key, -1),
    )


def plain_attention_forward(h, norm_gain, w_qkv, w_out, key_mask):
    normed, inv_root = plain_norm_forward(h, norm_gain)
    normed_low = normed.astype(jnp.bfloat16)
    joined = plain_product(normed_low, w_qkv).astype(jnp.bfloat16)
    q, k, v = jnp.split(joined, 3, axis=1)
    output, log_total = plain_attend_forward(q, k, v, key_mask)
    output_low = output.astype(jnp.bfloat16)
    return (normed_low, inv_root, joined, output_low, log_total, plain_product(output_low, w_out))


def plain_attention_back(d_h, h, saved, norm_gain, w_qkv, w_out, key_mask):
    normed_low, inv_root, joined, output_low, log_total, unused = saved
    d_low = d_h.astype(jnp.bfloat16)
    d_wout = plain_product(output_low.T, d_low)
    d_output = plain_product(d_low, w_out.T).astype(jnp.bfloat16)
    q, k, v = jnp.split(joined, 3, axis=1)
    d_query, d_key, d_value = plain_attend_back(q, k, v, key_mask, log_total, d_output)
    d_joined = jnp.concatenate([d_query, d_key, d_value], axis=1).astype(jnp.bfloat16)
    d_wqkv = plain_product(normed_low.T, d_joined)
    d_normed = plain_product(d_joined, w_qkv.T)
    d_input, d_gain = plain_norm_back(d_normed, h, inv_root, norm_gain)
    return (d_input, d_gain, d_wqkv, d_wout)


def plain_mlp_forward(h, norm_gain, w_in, w_down):
    normed, inv_root = plain_norm_forward(h, norm_gain)
    normed_low = normed.astype(jnp.bfloat16)
    joined = plain_product(normed_low, w_in)
    gate, upper = jnp.split(joined, 2, axis=1)
    hidden_low = (jax.nn.gelu(gate, approximate=True) * upper).astype(jnp.bfloat16)
    return (normed_low, inv_root, joined, hidden_low, plain_product(hidden_low, w_down))


def plain_mlp_back(d_h, h, saved, norm_gain, w_in, w_down):
    normed_low, inv_root, joined, hidden_low, unused = saved
    d_low = d_h.astype(jnp.bfloat16)
    d_wdown = plain_product(hidden_low.T, d_low)
    d_hidden = plain_product(d_low, w_down.T)
    gate, upper = jnp.split(joined, 2, axis=1)
    active, active_back = jax.vjp(partial(jax.nn.gelu, approximate=True), gate)
    d_gate = active_back(d_hidden * upper)[0]
    d_upper = d_hidden * active
    d_joined = jnp.concatenate([d_gate, d_upper], axis=1).astype(jnp.bfloat16)
    d_win = plain_product(normed_low.T, d_joined)
    d_normed = plain_product(d_joined, w_in.T)
    d_input, d_gain = plain_norm_back(d_normed, h, inv_root, norm_gain)
    return (d_input, d_gain, d_win, d_wdown)


def encoder_forward(weights, source):
    gains, w_qkv, w_out, w_cross, w_in, w_down = weights
    inputs = source.astype(jnp.float32)
    attn_saved = plain_attention_forward(inputs, gains[0], w_qkv, w_out, None)
    middle = inputs + attn_saved[-1]
    mlp_saved = plain_mlp_forward(middle, gains[1], w_in, w_down)
    final = middle + mlp_saved[-1]
    normed, inv_root = plain_norm_forward(final, gains[2])
    memory = normed.astype(jnp.bfloat16)
    key_value = plain_product(memory, w_cross).astype(jnp.bfloat16)
    return (inputs, attn_saved, middle, mlp_saved, final, inv_root, memory, key_value)


def encoder_front(weights, source):
    saved = encoder_forward(weights, source)
    return (saved[7], saved[6])


def encoder_back_saved(weights, saved, d_keyvalue):
    gains, w_qkv, w_out, w_cross, w_in, w_down = weights
    inputs, attn_saved, middle, mlp_saved, final, inv_root, memory, key_value = saved
    d_wcross = plain_product(memory.T, d_keyvalue)
    d_memory = plain_product(d_keyvalue, w_cross.T)
    d_final, gain_last = plain_norm_back(d_memory, final, inv_root, gains[2])
    d_part, gain_mlp, d_win, d_wdown = plain_mlp_back(d_final, middle, mlp_saved, gains[1], w_in, w_down)
    d_middle = d_final + d_part
    d_first, gain_attn, d_wqkv, d_wout = plain_attention_back(
        d_middle, inputs, attn_saved, gains[0], w_qkv, w_out, None
    )
    grads = (jnp.stack([gain_attn, gain_mlp, gain_last]), d_wqkv, d_wout, d_wcross, d_win, d_wdown)
    return (d_middle + d_first, grads)


def encoder_back(weights, source, d_keyvalue):
    return encoder_back_saved(weights, encoder_forward(weights, source), d_keyvalue)


def decoder_pass(weights, source, key_value, weight_cot, length, factor):
    gains, w_qkv, w_out, w_cross, w_in, w_down = weights
    width = source.shape[1]
    inputs = source.astype(jnp.float32)
    position = jnp.arange(inputs.shape[0], dtype=jnp.int32)
    is_valid = position < length
    key_mask = (position[None, :] <= position[:, None]) & is_valid[None, :]
    attn_saved = plain_attention_forward(inputs, gains[0], w_qkv, w_out, key_mask)
    middle = inputs + attn_saved[-1]
    normed, inv_root = plain_norm_forward(middle, gains[1])
    normed_low = normed.astype(jnp.bfloat16)
    w_query = w_cross[:, :width]
    w_back = w_cross[:, width:]
    queries = plain_product(normed_low, w_query).astype(jnp.bfloat16)
    mem_keys = key_value[:, :width]
    mem_values = key_value[:, width:]
    cross_out, cross_total = plain_attend_forward(queries, mem_keys, mem_values, None)
    cross_low = cross_out.astype(jnp.bfloat16)
    after = middle + plain_product(cross_low, w_back)
    mlp_saved = plain_mlp_forward(after, gains[2], w_in, w_down)
    final = after + mlp_saved[-1]
    d_final = jnp.where(is_valid[:, None], weight_cot.astype(jnp.float32) * factor, 0.0)
    d_part, gain_mlp, d_win, d_wdown = plain_mlp_back(d_final, after, mlp_saved, gains[2], w_in, w_down)
    d_after = d_final + d_part
    d_low = d_after.astype(jnp.bfloat16)
    d_wback = plain_product(cross_low.T, d_low)
    d_cross = plain_product(d_low, w_back.T).astype(jnp.bfloat16)
    d_query, d_key, d_value = plain_attend_back(queries, mem_keys, mem_values, None, cross_total, d_cross)
    d_query_low = d_query.astype(jnp.bfloat16)
    d_wquery = plain_product(normed_low.T, d_query_low)
    d_normed = plain_product(d_query_low, w_query.T)
    d_norm_in, gain_cross = plain_norm_back(d_normed, middle, inv_root, gains[1])
    d_middle = d_after + d_norm_in
    d_keyvalue = jnp.concatenate([d_key, d_value], axis=1).astype(jnp.bfloat16)
    d_first, gain_attn, d_wqkv, d_wout = plain_attention_back(
        d_middle, inputs, attn_saved, gains[0], w_qkv, w_out, key_mask
    )
    grads = (
        jnp.stack([gain_attn, gain_cross, gain_mlp]),
        d_wqkv,
        d_wout,
        jnp.concatenate([d_wquery, d_wback], axis=1),
        d_win,
        d_wdown,
    )
    return (final.astype(jnp.bfloat16), d_middle + d_first, d_keyvalue, grads)


def on_section(flag, work, operands):

    def run_work(values):
        return work(*values)

    def skip_work(values):
        return jax.tree.map(jnp.zeros_like, work(*values))

    return lax.cond(flag, run_work, skip_work, operands)


def plain_body(
    block_in,
    cotangent,
    lengths,
    sources,
    loss_weight,
    gains,
    qkv_weight,
    out_weight,
    cross_weight,
    in_weight,
    down_weight,
):
    is_encoder = lax.axis_index("section") == 0
    is_decoder = jnp.logical_not(is_encoder)
    wide = lax.axis_size("dp")
    gathered = (
        lax.all_gather(gains, "dp", axis=2, tiled=True),
        lax.all_gather(qkv_weight, "dp", axis=1, tiled=True),
        lax.all_gather(out_weight, "dp", axis=1, tiled=True),
        lax.all_gather(cross_weight, "dp", axis=1, tiled=True),
        lax.all_gather(in_weight, "dp", axis=1, tiled=True),
        lax.all_gather(down_weight, "dp", axis=1, tiled=True),
    )
    weights = tuple((w[0] for w in gathered))
    onehot = (sources[:, None] == jnp.arange(3, dtype=jnp.int32)[None, :]).astype(jnp.float32)
    counts = lax.psum(jnp.sum(onehot * lengths[:, None].astype(jnp.float32), axis=0), "dp")
    own_count = jnp.sum(onehot * counts[None, :], axis=1)
    own_weight = jnp.sum(onehot * loss_weight[None, :].astype(jnp.float32), axis=1)
    scale = own_weight * (lengths.shape[0] * wide * block_in.shape[2] / 3.0) / own_count

    def step(carry, item):
        source, weight_cot, length, factor = item
        key_value, memory = on_section(is_encoder, encoder_front, (weights, source))
        received = shifted(key_value, "section", 1)
        decoded, table_grad, d_keyvalue, dec_grads = on_section(
            is_decoder, decoder_pass, (weights, source, received, weight_cot, length, factor)
        )
        returned = shifted(d_keyvalue, "section", -1)
        plot_grad, enc_grads = on_section(is_encoder, encoder_back, (weights, source, returned))
        grads = tuple((a + b for a, b in zip(dec_grads, enc_grads)))
        carry = tuple((a + b for a, b in zip(carry, grads)))
        return (carry, (memory + decoded, plot_grad + table_grad))

    start = tuple((jnp.zeros(w.shape, jnp.float32) for w in weights))
    carry, (outputs, input_grads) = lax.scan(step, start, (block_in[0], cotangent, lengths, scale))
    gain_total, qkv_total, out_total, cross_sum, in_total, down_total = carry
    reduced = (
        lax.psum_scatter(gain_total[None], "dp", scatter_dimension=2, tiled=True),
        lax.psum_scatter(qkv_total[None], "dp", scatter_dimension=1, tiled=True),
        lax.psum_scatter(out_total[None], "dp", scatter_dimension=1, tiled=True),
        lax.psum_scatter(cross_sum[None], "dp", scatter_dimension=1, tiled=True),
        lax.psum_scatter(in_total[None], "dp", scatter_dimension=1, tiled=True),
        lax.psum_scatter(down_total[None], "dp", scatter_dimension=1, tiled=True),
    )
    return (
        outputs[None],
        input_grads[None],
        reduced[0],
        reduced[1],
        reduced[2],
        reduced[3],
        reduced[4],
        reduced[5],
    )


def tiled_body(
    block_in, cotangent, lengths, sources, loss_weight, gains, qkv_weight, out_weight, cross_weight, in_weight, down_weight
):
    wide = lax.axis_size("dp")
    pairs, seq, width = block_in.shape[1:]
    x, cot = block_in.reshape(pairs * seq, width), cotangent.reshape(pairs * seq, width)
    results = run_step(
        wide, seq, lengths, sources, loss_weight, gains[0], x, cot,
        qkv_weight[0], out_weight[0], cross_weight[0], in_weight[0], down_weight[0],
    )
    block_out, input_grad, down, inner, cross, out, qkv, gains_sum = copied(results[-8:-1], results[-1], gains.shape[1:])
    return (
        block_out.reshape(block_in.shape),
        input_grad.reshape(block_in.shape),
        gains_sum[None],
        qkv[None],
        out[None],
        cross[None],
        inner[None],
        down[None],
    )


def solution(mesh):
    in_specs = (
        P("section", "dp", None, None),
        P("dp", None, None),
        P("dp"),
        P("dp"),
        P(),
        P("section", None, "dp"),
        P("section", "dp", None),
        P("section", "dp", None),
        P("section", "dp", None),
        P("section", "dp", None),
        P("section", "dp", None),
    )
    out_specs = (
        P("section", "dp", None, None),
        P("section", "dp", None, None),
        P("section", None, "dp"),
        P("section", "dp", None),
        P("section", "dp", None),
        P("section", "dp", None),
        P("section", "dp", None),
        P("section", "dp", None),
    )

    def body(*args):
        shards = args[6:]
        tiled = args[5].shape[2] <= 128 and all(w.shape[1] % 16 == 0 for w in shards)
        return (tiled_body if tiled else plain_body)(*args)

    return jax.shard_map(body, mesh=mesh, in_specs=in_specs, out_specs=out_specs, check_vma=False)
```

```python
from functools import partial

import jax
import jax.numpy as jnp
from jax import lax
from jax.experimental import pallas as pl
from jax.experimental.pallas import tpu as pltpu
from jax.sharding import PartitionSpec as P

HEADS = 12
HEAD_DIM = 64


EPS = 1e-06
NEG = -1000000000.0


MESH = pl.DeviceIdType.MESH
VMEM_LIMIT = 62 * 2**20
F32, BF16 = jnp.float32, jnp.bfloat16
ANY = pl.BlockSpec(memory_space=pl.ANY)
SMEM = pl.BlockSpec(memory_space=pltpu.SMEM)
VMEM = pl.BlockSpec(memory_space=pltpu.VMEM)


def ring_position(chip, chips):
    return jnp.where(chip % 2 == 0, chip // 2, chips - 1 - chip // 2)


def ring_chip(position, chips):
    position = lax.rem(position + 2 * chips, chips)
    return jnp.where(position < chips // 2, 2 * position, 2 * (chips - 1 - position) + 1)


def ring_hops(long_way, chips):
    long, short = chips // 2, chips - 1 - chips // 2
    return (long, short) if long_way == 0 else (short, long)


def slot_of(long_way, way, distance, chips):
    return distance if distance == 0 or way == long_way else chips // 2 + distance


def entry_barrier(partners):
    barrier = pltpu.get_barrier_semaphore()
    for partner in partners:
        pl.semaphore_signal(barrier, inc=1, device_id=partner, device_id_type=MESH)
    pl.semaphore_wait(barrier, len(partners))


def remote(src, dst, send_sem, recv_sem, target):
    return pltpu.make_async_remote_copy(
        src_ref=src,
        dst_ref=dst,
        send_sem=send_sem,
        recv_sem=recv_sem,
        device_id=target,
        device_id_type=MESH,
    )


class Place:
    def __init__(self, wide):
        self.chips = wide // 2
        self.section, self.me = lax.axis_index("section"), lax.axis_index("dp")
        self.chip, self.core = self.me // 2, lax.rem(self.me, 2)
        self.spot = ring_position(self.chip, self.chips)
        self.ahead = (self.section, 2 * ring_chip(self.spot + 1, self.chips) + self.core)
        self.behind = (self.section, 2 * ring_chip(self.spot - 1, self.chips) + self.core)
        self.twin = (self.section, 2 * self.chip + 1 - self.core)
        self.across = (1 - self.section, self.me)

    def next_of(self, way):
        return self.ahead if way == 0 else self.behind

    def chip_at(self, way, distance):
        return ring_chip(self.spot + distance if way == 0 else self.spot - distance, self.chips)


def block_rows(ref, rows, chip, core):
    return ref.at[pl.ds(pl.multiple_of((2 * chip + core) * rows, rows), rows)]


class Gather:
    def __init__(self, place, names, shards, fulls, rows, long_way, sems):
        self.place, self.names = place, names
        self.shards, self.fulls, self.rows, self.long_way = shards, fulls, rows, long_way
        self.own_sem, self.ring_send, self.ring_recv, self.twin_send, self.twin_recv = sems

    def hops(self, name, way):
        return ring_hops(self.long_way[name], self.place.chips)[way]

    def pieces(self, name, way, hop):
        at = self.place
        origin = at.chip_at(way, -hop)
        target = block_rows(self.fulls[name], self.rows[name], origin, at.core)
        own = self.shards.get(name)
        return (own if hop == 0 and own is not None else target), target

    def ring(self, name, way, hop):
        source, target = self.pieces(name, way, hop)
        i = self.names.index(name)
        return remote(
            source, target, self.ring_send.at[i, way, hop], self.ring_recv.at[i, way, hop], self.place.next_of(way)
        )

    def pair(self, name, way, hop):
        source, target = self.pieces(name, way, hop)
        i, slot = self.names.index(name), slot_of(self.long_way[name], way, hop, self.place.chips)
        return remote(source, target, self.twin_send.at[i, slot], self.twin_recv.at[i, slot], self.place.twin)

    def own(self, name):
        source, target = self.pieces(name, 0, 0)
        return pltpu.make_async_copy(source, target, self.own_sem.at[self.names.index(name)])

    def start(self, name):
        for way in range(2):
            self.ring(name, way, 0).start()
        self.pair(name, 0, 0).start()
        if name in self.shards:
            self.own(name).start()

    def step(self, name, hop):
        for way in range(2):
            hops = self.hops(name, way)
            if hop < hops:
                self.ring(name, way, hop).wait_recv()
                if hop + 1 < hops:
                    self.ring(name, way, hop + 1).start()
                self.pair(name, way, hop + 1).start()

    def complete(self, name):
        if name in self.shards:
            self.own(name).wait()
        self.pair(name, 0, 0).wait_recv()
        for way in range(2):
            for hop in range(self.hops(name, way)):
                self.pair(name, way, hop + 1).wait_recv()

    def drain(self, names):
        for name in names:
            self.pair(name, 0, 0).wait_send()
            for way in range(2):
                for hop in range(self.hops(name, way)):
                    self.pair(name, way, hop + 1).wait_send()
                    self.ring(name, way, hop).wait_send()


LONG_WAY = {"small": 0, "qkv": 0, "out": 1, "crossE": 0, "crossD": 1, "in": 1, "down": 0, "gains": 0}


class Scatter:
    def __init__(self, place, names, grads, rows, long_way, twins, arrived, sems):
        self.place, self.names, self.grads, self.rows, self.long_way = place, names, grads, rows, long_way
        self.twins, self.arrived = twins, arrived
        self.twin_send, self.twin_recv, self.ring_send, self.ring_recv = sems

    def hops(self, name, way):
        return ring_hops(self.long_way[name], self.place.chips)[way]

    def landing(self, name, way, hop):
        return self.arrived[name].at[hop if way == self.long_way[name] else self.place.chips // 2 + hop]

    def block(self, name, way, distance, core):
        return block_rows(self.grads[name], self.rows[name], self.place.chip_at(way, distance), core)

    def pair(self, name, way, distance):
        at, i = self.place, self.names.index(name)
        slot = slot_of(self.long_way[name], way, distance, at.chips)
        source = self.block(name, way, distance, 1 - at.core)
        return remote(source, self.twins[name].at[slot], self.twin_send.at[i, slot], self.twin_recv.at[i, slot], at.twin)

    def ring(self, name, way, hop):
        at, i = self.place, self.names.index(name)
        return remote(
            self.block(name, way, self.hops(name, way) - hop, at.core),
            self.landing(name, way, hop),
            self.ring_send.at[i, way, hop],
            self.ring_recv.at[i, way, hop],
            at.next_of(way),
        )

    def slots(self, name):
        found = []
        for hop in range(self.place.chips // 2 + 1):
            for way in range(2):
                distance = self.hops(name, way) - hop
                if distance > 0 or (distance == 0 and way == self.long_way[name]):
                    found.append((way, distance))
        return found

    def start(self, name):
        for way, distance in self.slots(name):
            self.pair(name, way, distance).start()

    def add(self, name, way, distance, terms, out=None):
        at, rows, grad = self.place, self.rows[name], self.grads[name]
        group = 16 if rows % 16 == 0 else rows
        tile = next(t for t in (1024, 768, 128) if grad.shape[1] % t == 0)
        first = (2 * at.chip_at(way, distance) + at.core) * rows
        slot = slot_of(self.long_way[name], way, distance, at.chips)

        @pl.loop(0, rows // group)
        def _(n):
            part = span(n * group, group)
            own = pl.ds(pl.multiple_of(first + n * group, group), group)

            @pl.loop(0, grad.shape[1] // tile)
            def _(m):
                columns = span(m * tile, tile)
                total = grad[own, columns].astype(F32) + self.twins[name][slot, part, columns].astype(F32)
                for term in terms:
                    total += term[part, columns].astype(F32)
                if out is None:
                    grad[own, columns] = total.astype(grad.dtype)
                else:
                    out[part, columns] = total

    def step(self, name, way, hop):
        distance = self.hops(name, way) - hop
        if distance <= 0:
            return
        self.pair(name, way, distance).wait_recv()
        terms = []
        if hop > 0:
            self.ring(name, way, hop - 1).wait_recv()
            terms.append(self.landing(name, way, hop - 1))
        self.add(name, way, distance, terms)
        self.ring(name, way, hop).start()

    def finish(self, name, out):
        self.pair(name, self.long_way[name], 0).wait_recv()
        terms = []
        for way in range(2):
            last = self.hops(name, way) - 1
            self.ring(name, way, last).wait_recv()
            terms.append(self.landing(name, way, last))
        self.add(name, self.long_way[name], 0, terms, out)

    def drain(self, name):
        for way, distance in self.slots(name):
            self.pair(name, way, distance).wait_send()
        for way in range(2):
            for hop in range(self.hops(name, way)):
                self.ring(name, way, hop).wait_send()


def dot(a, b, over_a=1, over_b=0):
    return lax.dot_general(a, b, (((over_a,), (over_b,)), ((), ())), preferred_element_type=F32)


def span(start, size):
    return pl.ds(start, size) if isinstance(start, int) else pl.ds(pl.multiple_of(start, size), size)


def each(total, tile, work):
    @pl.loop(0, total // tile)
    def _(n):
        work(span(n * tile, tile))


ROWS = 64


def norm_into(h_ref, gain, out_ref):
    def work(at):
        h = h_ref[at].astype(F32)
        inv_root = lax.rsqrt(jnp.mean(h * h, axis=-1, keepdims=True) + EPS)
        out_ref[at] = (h * inv_root * gain).astype(out_ref.dtype)

    each(h_ref.shape[0], ROWS, work)


def norm_back(dn_ref, h_ref, gain, gain_sum, row, finish, start=0, size=None):
    if start == 0:
        gain_sum[row] = jnp.zeros(gain_sum.shape[1:], F32)

    def work(part):
        at = span(start + part.start, ROWS)
        h, dn = h_ref[at].astype(F32), dn_ref[at].astype(F32)
        inv_root = lax.rsqrt(jnp.mean(h * h, axis=-1, keepdims=True) + EPS)
        scaled = h * inv_root
        product = dn * scaled
        gain_sum[row] += jnp.sum(product.reshape(-1, 8, product.shape[1]), axis=0)
        inner = dn * gain
        finish(at, inv_root * (inner - scaled * jnp.mean(product * gain, axis=-1, keepdims=True)))

    each(size or h_ref.shape[0], ROWS, work)


def pair_columns(ref, rows, start, two):
    return ref[rows, span(start + two * 2 * HEAD_DIM, 2 * HEAD_DIM)]


def side_masks():
    lane = lax.broadcasted_iota(jnp.int32, (1, 2 * HEAD_DIM), 1)
    first = lane < HEAD_DIM
    return first, (first.astype(F32).astype(BF16), (1 - first.astype(F32)).astype(BF16))


def expo_columns(q, k, seq, length):
    scores = dot(k, q, 1, 1) * HEAD_DIM ** (-0.5)
    if length is not None:
        key = lax.broadcasted_iota(jnp.int32, (seq, seq), 0)
        query = lax.broadcasted_iota(jnp.int32, (seq, seq), 1)
        scores = jnp.where((key <= query) & (key < length), scores, NEG)
    expo = jnp.exp(scores - jnp.max(scores, axis=0, keepdims=True))
    return expo, jnp.sum(expo, axis=0, keepdims=True)


def attend(q_ref, q_at, k_ref, k_at, v_ref, v_at, out_ref, seq, lengths, chosen=None):
    start, stop = chosen or (0, q_ref.shape[0] // seq)
    first, keeps = side_masks()
    each_time = HEADS // 4

    @pl.loop(start * (HEADS // 2 // each_time), stop * (HEADS // 2 // each_time))
    def _(m):
        work = []
        for g in range(each_time):
            n = m * each_time + g
            pair, two = n // (HEADS // 2), lax.rem(n, HEADS // 2)
            rows = span(pair * seq, seq)
            length = None if lengths is None else lengths[pair]
            q, k, v = (pair_columns(r, rows, a, two) for r, a in ((q_ref, q_at), (k_ref, k_at), (v_ref, v_at)))
            for side in range(2):
                work.append((rows, two, length, q, k, v, side))
        expos = [expo_columns(q * keeps[side], k, seq, length) for rows, two, length, q, k, v, side in work]
        outs = [dot((e * (1.0 / t)).astype(BF16), w[5], 0, 0) for (e, t), w in zip(expos, work)]
        for g in range(each_time):
            rows, two = work[2 * g][:2]
            value = jnp.where(first, outs[2 * g], outs[2 * g + 1])
            out_ref[rows, span(two * 2 * HEAD_DIM, 2 * HEAD_DIM)] = value.astype(BF16)


def attend_back(q_ref, q_at, k_ref, k_at, v_ref, v_at, do_ref, dq, dk, dv, seq, lengths, chosen=None):
    start, stop = chosen or (0, q_ref.shape[0] // seq)
    first, keeps = side_masks()
    root = HEAD_DIM ** (-0.5)
    each_time = HEADS // 6

    @pl.loop(start * (HEADS // 2 // each_time), stop * (HEADS // 2 // each_time))
    def _(m):
        work = []
        for g in range(each_time):
            n = m * each_time + g
            pair, two = n // (HEADS // 2), lax.rem(n, HEADS // 2)
            rows = span(pair * seq, seq)
            length = None if lengths is None else lengths[pair]
            q, k, v = (pair_columns(r, rows, a, two) for r, a in ((q_ref, q_at), (k_ref, k_at), (v_ref, v_at)))
            d_out = pair_columns(do_ref, rows, 0, two)
            for side in range(2):
                work.append((rows, two, length, q, k, v, d_out, side))
        expos = [expo_columns(q * keeps[side], k, seq, length) for rows, two, length, q, k, v, d_out, side in work]
        d_probs = [dot(v, d_out * keeps[side], 1, 1) for rows, two, length, q, k, v, d_out, side in work]
        probs = [e * (1.0 / t) for e, t in expos]
        d_scores = [(p * (d - jnp.sum(p * d, axis=0, keepdims=True))).astype(BF16) for p, d in zip(probs, d_probs)]
        dvs = [dot(p.astype(BF16), w[6]) for p, w in zip(probs, work)]
        dqs = [dot(d, w[4], 0, 0) for d, w in zip(d_scores, work)]
        dks = [dot(d, w[3]) for d, w in zip(d_scores, work)]
        for g in range(each_time):
            rows, two = work[2 * g][:2]
            for (ref, start), both, factor in ((dq, dqs, root), (dk, dks, root), (dv, dvs, 1.0)):
                value = jnp.where(first, both[2 * g], both[2 * g + 1]) * factor
                ref[rows, span(start + two * 2 * HEAD_DIM, 2 * HEAD_DIM)] = value.astype(BF16)


def gelu_parts(gate):
    root, cubic = 0.7978845608028654, 0.044715
    square = gate * gate
    bent = jnp.tanh(root * gate * (1.0 + cubic * square))
    half = 0.5 * (1.0 + bent)
    slope = half + 0.5 * gate * (1.0 - bent * bent) * root * (1.0 + 3.0 * cubic * square)
    return gate * half, slope


FF_TILE = 512


def mlp_forward(a_ref, w_in, w_down, into_ref, hidden_ref=None, slopes_ref=None):
    ff = w_in.shape[1] // 2

    @pl.loop(0, ff // FF_TILE)
    def _(n):
        gates, uppers = span(n * FF_TILE, FF_TILE), span(ff + n * FF_TILE, FF_TILE)
        gate, upper = dot(a_ref[...], w_in[:, gates]), dot(a_ref[...], w_in[:, uppers])
        active, slope = gelu_parts(gate)
        hidden = (active * upper).astype(BF16)
        if hidden_ref is not None:
            hidden_ref[:, gates] = hidden
            slopes_ref[:, gates] = (slope * upper).astype(BF16)
            slopes_ref[:, uppers] = active.astype(BF16)
        if w_down is not None:
            into_ref[...] += dot(hidden, w_down[gates, :])


def mlp_back(d_low, w_in, w_down, slopes_ref, dn_ref):
    ff = w_in.shape[1] // 2
    dn_ref[...] = jnp.zeros(dn_ref.shape, F32)

    @pl.loop(0, ff // FF_TILE)
    def _(n):
        gates, uppers = span(n * FF_TILE, FF_TILE), span(ff + n * FF_TILE, FF_TILE)
        d_hidden = dot(d_low[...], w_down[gates, :], 1, 1)
        d_gate = (d_hidden * slopes_ref[:, gates]).astype(BF16)
        d_upper = (d_hidden * slopes_ref[:, uppers]).astype(BF16)
        slopes_ref[:, gates], slopes_ref[:, uppers] = d_gate, d_upper
        dn_ref[...] += dot(d_gate, w_in[:, gates], 1, 1) + dot(d_upper, w_in[:, uppers], 1, 1)


def product_into(a_ref, w_ref, out_ref, tile, w_at=0, transposed=False):
    width = out_ref.shape[1]

    @pl.loop(0, width // tile)
    def _(n):
        if transposed:
            value = dot(a_ref[...], w_ref[span(w_at + n * tile, tile), :], 1, 1)
        else:
            value = dot(a_ref[...], w_ref[:, span(w_at + n * tile, tile)])
        out_ref[:, span(n * tile, tile)] = value.astype(out_ref.dtype)


def add_product(base_ref, a_ref, w, out_ref):
    out_ref[...] = base_ref[...].astype(F32) + dot(a_ref[...], w)


class Moves:
    def __init__(self, sems):
        self.sems, self.used = sems, 0

    def start(self, src, dst):
        copy = pltpu.make_async_copy(src, dst, self.sems.at[self.used])
        self.used += 1
        copy.start()
        return copy


def weight_grad(a_ref, y_ref, grad, tile_rows, tile_columns, column_at=0):
    @pl.loop(0, a_ref.shape[1] // tile_rows)
    def _(i):
        @pl.loop(0, y_ref.shape[1] // tile_columns)
        def _(j):
            rows, columns = span(i * tile_rows, tile_rows), span(j * tile_columns, tile_columns)
            value = dot(a_ref[:, rows], y_ref[:, columns], 0, 0).astype(BF16)
            grad[rows, pl.ds(pl.multiple_of(column_at + j * tile_columns, 256), tile_columns)] = value


GATHER_NAMES = ("small", "qkv", "out", "crossE", "crossD", "in", "down")
SCATTER_NAMES = ("down", "in", "crossD", "crossE", "out", "qkv", "gains")
BLOCK = (8, 128)


def spread_gains(small, own, width):
    lane = lax.broadcasted_iota(jnp.int32, BLOCK, 1)
    total = jnp.zeros((BLOCK[0], width), F32)
    for n in range(width // own):
        part = jnp.where(lane < own, small[n * BLOCK[0] : (n + 1) * BLOCK[0], :], 0.0)
        wide = jnp.concatenate([part, jnp.zeros((BLOCK[0], width - BLOCK[1]), F32)], axis=1)
        total += wide if n == 0 else pltpu.roll(wide, n * own, 1)
    return total


def gather_blocks(gains_grad, own, out_ref):
    width = gains_grad.shape[1]
    lane = lax.broadcasted_iota(jnp.int32, BLOCK, 1)
    for n in range(width // own):
        turned = gains_grad if n == 0 else pltpu.roll(gains_grad, width - n * own, 1)
        out_ref[n * BLOCK[0] : (n + 1) * BLOCK[0], :] = jnp.where(lane < own, turned[:, : BLOCK[1]], 0.0)


def step_kernel(
    wide, seq, lengths, sources, loss_weight, gains_in, x_in, cot_in, qkv_in, out_in, cross_in, in_in, down_in,
    small_full, qkv_full, out_full, enc_full, dec_full, in_full, down_full,
    joined_kept, attended_kept, middle_kept, final_kept,
    block_out, input_out, down_sum, in_sum, cross_sum, out_sum, qkv_sum, gains_sum,
    small_own, gains, factors, gain_sum, landing, back, passed_out, passed_in, g_gains, g_down, *refs,
):
    count = len(SCATTER_NAMES)
    twins, arrived = dict(zip(SCATTER_NAMES, refs[:count])), dict(zip(SCATTER_NAMES, refs[count : 2 * count]))
    load_sem, send_sem, recv_sem = refs[2 * count : 2 * count + 3]
    gather_sems, scatter_sems = refs[2 * count + 3 : 2 * count + 8], refs[2 * count + 8 :]
    at = Place(wide)
    rows, width = x_in.shape
    pairs, own = rows // seq, gains_in.shape[1]
    vmem = pltpu.VMEM
    broad, slim = vmem((rows, width), F32), vmem((rows, width), BF16)
    lane = lax.broadcasted_iota(jnp.int32, (1, BLOCK[1]), 1)
    counted = jnp.zeros((1, BLOCK[1]), F32)
    for pair in range(pairs):
        counted += jnp.where(lane == sources[pair], lengths[pair].astype(F32), 0.0)
    small_own[...] = jnp.zeros(BLOCK, F32)
    small_own[0:3, 0:own] = gains_in[...].astype(F32)
    small_own[3:4, :] = counted
    entry_barrier((at.ahead, at.behind, at.twin, at.across))

    fulls = dict(zip(GATHER_NAMES, (small_full, qkv_full, out_full, enc_full, dec_full, in_full, down_full)))
    full_rows = {n: f.shape[0] // wide for n, f in fulls.items()}
    w_qkv_shape, w_out_shape, w_cross_shape = qkv_full.shape, out_full.shape, dec_full.shape
    w_in_shape, w_down_shape = in_full.shape, down_full.shape
    ff = w_down_shape[0]
    shapes = dict(zip(SCATTER_NAMES, (w_down_shape, w_in_shape, w_cross_shape, w_cross_shape, w_out_shape, w_qkv_shape)))
    shapes["gains"] = g_gains.shape
    share = {n: s[0] // wide for n, s in shapes.items()}
    grads = {"down": g_down, "gains": g_gains}
    scatter = Scatter(at, SCATTER_NAMES, grads, share, LONG_WAY, twins, arrived, scatter_sems)
    sums = {"down": down_sum, "in": in_sum, "out": out_sum, "qkv": qkv_sum, "gains": gains_sum}
    sums.update(crossD=cross_sum, crossE=passed_out)
    passed_weight = remote(
        cross_in, block_rows(enc_full, full_rows["crossE"], at.chip, at.core), send_sem.at[0], recv_sem.at[0], at.across
    )
    passed_sum = remote(passed_out, passed_in, send_sem.at[1], recv_sem.at[1], at.across)

    def grad_space(*names):
        return [vmem(shapes[n], BF16) for n in names]

    def to_dec(pair):
        part = span(pair * seq, seq)
        return remote(back.at[part], landing.at[part], send_sem.at[2 + pair], recv_sem.at[2 + pair], at.across)

    def to_enc(pair):
        part, i = span(pair * seq, seq), 2 + pairs + pair
        return remote(back.at[part], landing.at[part], send_sem.at[i], recv_sem.at[i], at.across)

    class Hops:
        def __init__(self):
            self.done = {}

        def hop(self, *names):
            for name in names:
                for way in range(2):
                    scatter.step(name, way, self.done.get(name, 0))
                self.done[name] = self.done.get(name, 0) + 1

        def ready(self, name):
            scatter.start(name)
            self.hop(name)

        def rest(self, names):
            for step in range(at.chips // 2 + 1):
                for name in names:
                    if self.done[name] == step < at.chips // 2:
                        self.hop(name)
                    elif self.done[name] == step:
                        scatter.finish(name, sums[name])
                        self.done[name] += 1
                        if name == "crossE":
                            passed_sum.start()

    def first_part(moves, gather, names, lengths, x, small, w_qkv, w_out, normed, joined, attended, middle, between):
        load_x = moves.start(x_in, x)
        for name in names:
            if name == "crossE":
                passed_weight.wait_recv()
            gather.start(name)
        for hop in range(at.chips // 2 - 1):
            for name in names:
                gather.step(name, hop)

        def load(name, into):
            gather.complete(name)
            return moves.start(fulls[name], into)

        gather.step("small", at.chips // 2 - 1)
        load("small", small).wait()
        gains[...] = spread_gains(small, own, width)
        totals = jnp.zeros((1, BLOCK[1]), F32)
        for n in range(wide):
            totals += small[n * BLOCK[0] + 3 : n * BLOCK[0] + 4, :]
        factors[...] = jnp.zeros(factors.shape, F32)
        for pair in range(pairs):
            source = sources[pair]
            weight = jnp.where(source == 0, loss_weight[0], jnp.where(source == 1, loss_weight[1], loss_weight[2]))
            total = jnp.sum(jnp.where(lane == source, totals, 0.0), axis=1, keepdims=True)
            factor = jnp.full((1, 1), weight.astype(F32) * (pairs * wide * seq / 3.0), F32) / total
            factors[pair : pair + 1, :] = jnp.broadcast_to(factor, (1, BLOCK[1]))
        load_x.wait()
        norm_into(x, gains[0:1], normed)
        gather.step("qkv", at.chips // 2 - 1)
        gather.step("out", at.chips // 2 - 1)
        load_qkv = load("qkv", w_qkv)
        load_out = load("out", w_out)
        load_qkv.wait()
        product_into(normed, w_qkv, joined, width)
        for name in names[3:]:
            gather.step(name, at.chips // 2 - 1)
        between()
        attend(joined, 0, joined, width, joined, 2 * width, attended, seq, lengths)
        load_out.wait()
        add_product(x, attended, w_out[...], middle)
        return [moves.start(a, b) for a, b in ((middle, middle_kept), (joined, joined_kept), (attended, attended_kept))]

    def self_back(hops, lengths, d_middle, x, normed, d_low, w_qkv, w_out, joined, attended, d_attended, dn, loads, first, second):
        each(rows, ROWS, lambda part: d_low.__setitem__(part, d_middle[part].astype(BF16)))
        weight_grad(attended, d_low, grads["out"], width // 3, width)
        hops.ready("out")
        product_into(d_low, w_out, d_attended, width, transposed=True)
        hops.hop(*first)
        for load in loads:
            load.wait()
        attend_back(
            joined, 0, joined, width, joined, 2 * width, d_attended,
            (joined, 0), (joined, width), (joined, 2 * width), seq, lengths,
        )
        hops.hop(*second)
        norm_into(x, gains[0:1], normed)
        weight_grad(normed, joined, grads["qkv"], width // 3, width)
        hops.ready("qkv")
        product_into(joined, w_qkv, dn, width, transposed=True)

        def finish(part, d_input):
            d_middle[part] = d_middle[part] + d_input

        norm_back(dn, x, gains[0:1], gain_sum, 0, finish)

    def gains_ready(hops):
        lines = [jnp.sum(gain_sum[row], axis=0, keepdims=True) for row in range(3)]
        gather_blocks(jnp.concatenate(lines + [jnp.zeros((BLOCK[0] - 3, width), F32)], axis=0), own, g_gains)
        hops.ready("gains")

    @pl.when(at.section == 0)
    def _():
        moves, hops = Moves(load_sem), Hops()
        passed_weight.start()
        names = ("small", "qkv", "out", "in", "down")
        shards = dict(zip(names, (small_own, qkv_in, out_in, in_in, down_in)))
        gather = Gather(at, GATHER_NAMES, shards, fulls, full_rows, LONG_WAY, gather_sems)

        def ahead(x, small, w_qkv, w_out, normed, joined, attended, middle, w_in, w_down):
            loads = []

            def between():
                for name, into in (("in", w_in), ("down", w_down)):
                    gather.complete(name)
                    loads.append(moves.start(fulls[name], into))

            stores = first_part(
                moves, gather, names, None, x, small, w_qkv, w_out, normed, joined, attended, middle, between
            )
            norm_into(middle, gains[1:2], normed)
            for copy in loads + stores[:1]:
                copy.wait()
            mlp_forward(normed, w_in, w_down, middle)
            stores.append(moves.start(middle, final_kept))
            for pair in range(pairs):
                part = pl.ds(pair * seq, seq)
                norm_into(middle.at[part], gains[2:3], back.at[part])
                to_dec(pair).start()
            stores.append(moves.start(back, block_out))
            for copy in stores[1:]:
                copy.wait()

        pl.run_scoped(
            ahead,
            slim, vmem(small_full.shape, F32), vmem(w_qkv_shape, BF16), vmem(w_out_shape, BF16),
            slim, vmem((rows, 3 * width), BF16), slim, broad, vmem(w_in_shape, BF16), vmem(w_down_shape, BF16),
        )

        def backward(final, normed, w_out, attended, g_in, g_out, g_qkv):
            grads.update({"in": g_in, "out": g_out, "qkv": g_qkv})
            early = [moves.start(a, b) for a, b in ((out_full, w_out), (attended_kept, attended))]

            def feed(w_in, w_down, middle, hidden, slopes, d_low, dn):
                loads = [
                    moves.start(a, b)
                    for a, b in ((middle_kept, middle), (in_full, w_in), (final_kept, final), (down_full, w_down))
                ]
                for load in loads:
                    load.wait()
                norm_into(middle, gains[1:2], normed)
                mlp_forward(normed, w_in, None, None, hidden, slopes)

                def finish_final(part, d_input):
                    final[part] = d_input
                    d_low[part] = d_input.astype(BF16)

                for pair in range(pairs):
                    to_enc(pair).wait_recv()
                    norm_back(landing, final, gains[2:3], gain_sum, 2, finish_final, pair * seq, seq)
                weight_grad(hidden, d_low, g_down, ff // 4, width)
                hops.ready("down")
                mlp_back(d_low, w_in, w_down, slopes, dn)
                hops.hop("down")
                weight_grad(normed, slopes, g_in, width // 3, ff // 2)
                hops.ready("in")
                hops.hop("down")

                def finish_middle(part, d_input):
                    final[part] = final[part] + d_input

                norm_back(dn, middle, gains[1:2], gain_sum, 1, finish_middle)

            pl.run_scoped(
                feed,
                vmem(w_in_shape, BF16), vmem(w_down_shape, BF16), broad, vmem((rows, ff), BF16), vmem((rows, 2 * ff), BF16),
                slim, broad,
            )

            def attention(w_qkv, x, joined, d_low, d_attended, dn):
                loads = [moves.start(a, b) for a, b in ((joined_kept, joined), (x_in, x), (qkv_full, w_qkv))]
                for load in early:
                    load.wait()
                self_back(
                    hops, None, final, x, normed, d_low, w_qkv, w_out, joined, attended, d_attended, dn, loads, ("in",), ("out", "in")
                )
                store = moves.start(final, input_out)
                gains_ready(hops)
                hops.rest(("down", "in", "out", "qkv", "gains"))
                store.wait()

            pl.run_scoped(
                attention,
                vmem(w_qkv_shape, BF16), slim, vmem((rows, 3 * width), BF16), slim, slim, broad,
            )
            for name in ("down", "in", "out", "qkv", "gains"):
                scatter.drain(name)

        pl.run_scoped(backward, broad, slim, vmem(w_out_shape, BF16), slim, *grad_space("in", "out", "qkv"))
        gather.drain(names)
        passed_weight.wait_send()
        for pair in range(pairs):
            to_dec(pair).wait_send()
        passed_sum.wait_recv()
        cross_sum[...] = passed_in[...]

    @pl.when(at.section == 1)
    def _():
        moves, hops = Moves(load_sem), Hops()
        names = ("small", "qkv", "out", "crossD", "crossE", "in", "down")
        shards = {"small": small_own, "qkv": qkv_in, "out": out_in, "crossD": cross_in, "in": in_in, "down": down_in}
        gather = Gather(at, GATHER_NAMES, shards, fulls, full_rows, LONG_WAY, gather_sems)

        def ahead(x, small, w_qkv, w_out, normed, joined, attended, middle):
            stores = first_part(
                moves, gather, names, lengths, x, small, w_qkv, w_out, normed, joined, attended, middle, lambda: None
            )
            for store in stores:
                store.wait()

        pl.run_scoped(
            ahead,
            slim, vmem(small_full.shape, F32), vmem(w_qkv_shape, BF16), vmem(w_out_shape, BF16),
            slim, vmem((rows, 3 * width), BF16), slim, broad,
        )

        def rest(cot, normed_a, keyval, crossed, normed_b, slopes, d_low2, d_after):
            d_queries, d_keyval, memory = cot, keyval, landing

            def to_memory(w_enc, w_dec, w_in, w_down, queries, after, hidden, d_low, dn, d_crossed, middle):
                load_middle = moves.start(middle_kept, middle)
                load_cot = moves.start(cot_in, cot)
                loads = []
                for name, into in (("crossD", w_dec), ("crossE", w_enc)):
                    gather.complete(name)
                    loads.append(moves.start(fulls[name], into))
                load_middle.wait()
                norm_into(middle, gains[1:2], normed_a)
                loads[0].wait()
                product_into(normed_a, w_dec, queries, width)
                loads[1].wait()
                for name, into in (("in", w_in), ("down", w_down)):
                    gather.complete(name)
                    loads.append(moves.start(fulls[name], into))

                @pl.loop(0, pairs)
                def _(pair):
                    part = span(pair * seq, seq)
                    to_dec(pair).wait_recv()
                    product_into(memory.at[part], w_enc, keyval.at[part], width)
                    attend(queries, 0, keyval, 0, keyval, width, crossed, seq, None, (pair, pair + 1))

                add_product(middle, crossed, w_dec[:, width:], after)
                norm_into(after, gains[2:3], normed_b)
                for load in loads[2:] + [load_cot]:
                    load.wait()
                dn[...] = after[...]
                mlp_forward(normed_b, w_in, w_down, dn, hidden, slopes)

                for pair in range(pairs):

                    @pl.loop(0, seq // ROWS)
                    def _(n):
                        part = span(pair * seq + n * ROWS, ROWS)
                        position = n * ROWS + lax.broadcasted_iota(jnp.int32, (ROWS, 1), 0)
                        d_low2[part] = dn[part].astype(BF16)
                        factor = factors[pair : pair + 1, 0:1]
                        d_final = jnp.where(position < lengths[pair], cot[part].astype(F32) * factor, 0.0)
                        d_after[part] = d_final
                        d_low[part] = d_final.astype(BF16)

                store = moves.start(d_low2, block_out)
                weight_grad(hidden, d_low, g_down, ff // 4, width)
                hops.ready("down")
                mlp_back(d_low, w_in, w_down, slopes, dn)
                hops.hop("down")
                store.wait()

                def finish_after(part, d_input):
                    total = d_after[part] + d_input
                    d_after[part] = total
                    d_low2[part] = total.astype(BF16)

                norm_back(dn, after, gains[2:3], gain_sum, 2, finish_after)
                d_crossed[...] = dot(d_low2[...], w_dec[:, width:], 1, 1).astype(BF16)

                @pl.loop(0, pairs)
                def _(pair):
                    part = span(pair * seq, seq)
                    attend_back(
                        queries, 0, keyval, 0, keyval, width, d_crossed,
                        (d_queries, 0), (d_keyval, 0), (d_keyval, width), seq, None, (pair, pair + 1),
                    )
                    back[part] = dot(d_keyval[part], w_enc[...], 1, 1).astype(BF16)
                    to_enc(pair).start()

                hops.hop("down")
                dn[...] = dot(d_queries[...], w_dec[:, :width], 1, 1)

                def finish_middle(part, d_input):
                    d_after[part] = d_after[part] + d_input

                norm_back(dn, middle, gains[1:2], gain_sum, 1, finish_middle)

            pl.run_scoped(
                to_memory,
                vmem(w_cross_shape, BF16), vmem(w_cross_shape, BF16), vmem(w_in_shape, BF16), vmem(w_down_shape, BF16),
                slim, broad, vmem((rows, ff), BF16), slim, broad, slim, broad,
            )

            def to_input(w_qkv, w_out, d_low, d_attended, dn, g_in, g_dec, g_enc, g_out, g_qkv):
                grads.update({"in": g_in, "crossD": g_dec, "crossE": g_enc, "out": g_out, "qkv": g_qkv})
                load_out = moves.start(out_full, w_out)
                loads = [moves.start(qkv_full, w_qkv)]
                weight_grad(normed_b, slopes, g_in, width // 3, ff // 2)
                hops.ready("in")
                joined = slopes.at[:, pl.ds(0, 3 * width)]
                loads.append(moves.start(joined_kept, joined))
                weight_grad(memory, d_keyval, g_enc, width // 3, width)
                hops.ready("crossE")
                loads.append(moves.start(x_in, memory))
                weight_grad(crossed, d_low2, g_dec, width // 3, width, column_at=width)
                load_attended = moves.start(attended_kept, crossed)
                weight_grad(normed_a, d_queries, g_dec, width // 3, width)
                hops.ready("crossD")
                load_out.wait()
                load_attended.wait()
                self_back(
                    hops, lengths, d_after, memory, normed_a, d_low, w_qkv, w_out, joined, crossed, d_attended, dn, loads,
                    ("down",), ("in", "crossE"),
                )
                store = moves.start(d_after, input_out)
                gains_ready(hops)
                hops.rest(("crossE", "down", "in", "crossD", "out", "qkv", "gains"))
                store.wait()
                for name in SCATTER_NAMES:
                    scatter.drain(name)

            pl.run_scoped(
                to_input,
                vmem(w_qkv_shape, BF16), vmem(w_out_shape, BF16), slim, slim, broad,
                *grad_space("in", "crossD", "crossE", "out", "qkv"),
            )

        pl.run_scoped(
            rest,
            slim, slim, vmem((rows, 2 * width), BF16), slim, slim, vmem((rows, 2 * ff), BF16), slim, broad,
        )
        gather.drain(names)
        for pair in range(pairs):
            to_enc(pair).wait_send()
        passed_sum.wait_send()


def run_step(wide, seq, lengths, sources, loss_weight, gains, x, cot, w_qkv, w_out, w_cross, w_in, w_down):
    (rows, width), chips, pairs = x.shape, wide // 2, x.shape[0] // seq
    vmem, shaped, dma = pltpu.VMEM, jax.ShapeDtypeStruct, pltpu.SemaphoreType.DMA
    fulls = [(wide * w.shape[0], w.shape[1]) for w in (w_qkv, w_out, w_cross, w_cross, w_in, w_down)]
    shares = [w.shape for w in (w_down, w_in, w_cross, w_cross, w_out, w_qkv)] + [BLOCK]
    types = [BF16] * 6 + [F32]
    gathered, scattered = len(GATHER_NAMES), len(SCATTER_NAMES)
    return pl.pallas_call(
        partial(step_kernel, wide, seq),
        out_shape=[shaped((wide * BLOCK[0], BLOCK[1]), F32)]
        + [shaped(f, BF16) for f in fulls]
        + [shaped((rows, 3 * width), BF16), shaped((rows, width), BF16)]
        + [shaped((rows, width), F32)] * 2
        + [shaped((rows, width), BF16), shaped((rows, width), F32)]
        + [shaped(shares[n], F32) for n in (0, 1, 2, 4, 5, 6)],
        in_specs=[SMEM] * 3 + [VMEM] + [ANY] * 7,
        out_specs=[ANY] * 13 + [VMEM] * 6,
        scratch_shapes=[
            vmem(BLOCK, F32),
            vmem((BLOCK[0], width), F32),
            vmem(BLOCK, F32),
            vmem((3, 8, width), F32),
            vmem((rows, width), BF16),
            vmem((rows, width), BF16),
            vmem(w_cross.shape, F32),
            vmem(w_cross.shape, F32),
            vmem((wide * BLOCK[0], BLOCK[1]), F32),
            vmem(fulls[5], BF16),
        ]
        + [vmem((chips,) + s, t) for s, t in zip(shares, types)]
        + [vmem((chips - 1,) + s, t) for s, t in zip(shares, types)]
        + [dma((64,)), dma((2 + 2 * pairs,)), dma((2 + 2 * pairs,))]
        + [dma((gathered,)), dma((gathered, 2, chips // 2)), dma((gathered, 2, chips // 2))]
        + [dma((gathered, chips)), dma((gathered, chips)), dma((scattered, chips)), dma((scattered, chips))]
        + [dma((scattered, 2, chips // 2)), dma((scattered, 2, chips // 2))],
        name="encoder_and_decoder",
        compiler_params=pltpu.CompilerParams(collective_id=0, has_side_effects=True, vmem_limit_bytes=VMEM_LIMIT),
    )(lengths, sources, loss_weight, gains, x, cot, w_qkv, w_out, w_cross, w_in, w_down)


def copy_kernel(count, *refs):
    blocks, gains, stored, gains_out = refs[:count], refs[count], refs[count + 1 : 2 * count + 1], refs[2 * count + 1]
    held, sems = refs[2 * count + 2 : -1], refs[-1]
    loads = [pltpu.make_async_copy(blocks[n], held[n], sems.at[n]) for n in range(count)]
    stores = [pltpu.make_async_copy(held[n], stored[n], sems.at[count + n]) for n in range(count)]
    for load in loads:
        load.start()
    gains_out[...] = gains[0 : gains_out.shape[0], 0 : gains_out.shape[1]]
    for load, store in zip(loads, stores):
        load.wait()
        store.start()
    for store in stores:
        store.wait()


def copied(arrays, gains, gains_shape):
    count = len(arrays)
    return pl.pallas_call(
        partial(copy_kernel, count),
        out_shape=[jax.ShapeDtypeStruct(a.shape, a.dtype) for a in arrays] + [jax.ShapeDtypeStruct(gains_shape, F32)],
        in_specs=[ANY] * count + [VMEM],
        out_specs=[ANY] * count + [VMEM],
        scratch_shapes=[pltpu.VMEM(a.shape, a.dtype) for a in arrays] + [pltpu.SemaphoreType.DMA((2 * count,))],
        name="outputs",
    )(*arrays, gains)


def shifted(block, axis, distance):
    devices = range(lax.axis_size(axis))
    route = [(i - distance, i) for i in devices if i - distance in devices]
    return lax.ppermute(block, axis, route)


def plain_product(a, b):
    return jnp.dot(a, b, preferred_element_type=jnp.float32)


def plain_split_heads(v):
    return v.reshape(v.shape[0], HEADS, -1)


def plain_norm_forward(h, norm_gain):
    inv_root = lax.rsqrt(jnp.mean(h * h, axis=-1, keepdims=True) + EPS)
    return (h * inv_root * norm_gain.astype(jnp.float32), inv_root)


def plain_norm_back(d_normed, h, inv_root, norm_gain):
    scaled = h * inv_root
    d_gain = jnp.sum(d_normed * scaled, axis=0)
    inner = d_normed * norm_gain.astype(jnp.float32)
    d_input = inv_root * (inner - scaled * jnp.mean(inner * scaled, axis=-1, keepdims=True))
    return (d_input, d_gain)


def plain_score_block(q, k, key_mask):
    scores = jnp.einsum(
        "qhd,khd->hqk", plain_split_heads(q), plain_split_heads(k), preferred_element_type=jnp.float32
    ) * HEAD_DIM ** (-0.5)
    if key_mask is not None:
        scores = jnp.where(key_mask[None], scores, NEG)
    return scores


def plain_attend_forward(q, k, v, key_mask):
    scores = plain_score_block(q, k, key_mask)
    highest = jnp.max(scores, axis=-1, keepdims=True)
    expo = jnp.exp(scores - highest)
    total = jnp.sum(expo, axis=-1, keepdims=True)
    weights = (expo / total).astype(jnp.bfloat16)
    output = jnp.einsum("hqk,khd->qhd", weights, plain_split_heads(v), preferred_element_type=jnp.float32)
    return (output.reshape(q.shape[0], -1), highest + jnp.log(total))


def plain_attend_back(q, k, v, key_mask, log_total, d_out):
    scores = plain_score_block(q, k, key_mask)
    probs = jnp.exp(scores - log_total)
    heads_dout = plain_split_heads(d_out)
    d_value = jnp.einsum(
        "hqk,qhd->khd", probs.astype(jnp.bfloat16), heads_dout, preferred_element_type=jnp.float32
    )
    d_probs = jnp.einsum(
        "qhd,khd->hqk", heads_dout, plain_split_heads(v), preferred_element_type=jnp.float32
    )
    centre = jnp.sum(probs * d_probs, axis=-1, keepdims=True)
    d_scores = (probs * (d_probs - centre)).astype(jnp.bfloat16)
    d_query = jnp.einsum(
        "hqk,khd->qhd", d_scores, plain_split_heads(k), preferred_element_type=jnp.float32
    ) * HEAD_DIM ** (-0.5)
    d_key = jnp.einsum(
        "hqk,qhd->khd", d_scores, plain_split_heads(q), preferred_element_type=jnp.float32
    ) * HEAD_DIM ** (-0.5)
    rows_query = q.shape[0]
    rows_key = k.shape[0]
    return (
        d_query.reshape(rows_query, -1),
        d_key.reshape(rows_key, -1),
        d_value.reshape(rows_key, -1),
    )


def plain_attention_forward(h, norm_gain, w_qkv, w_out, key_mask):
    normed, inv_root = plain_norm_forward(h, norm_gain)
    normed_low = normed.astype(jnp.bfloat16)
    joined = plain_product(normed_low, w_qkv).astype(jnp.bfloat16)
    q, k, v = jnp.split(joined, 3, axis=1)
    output, log_total = plain_attend_forward(q, k, v, key_mask)
    output_low = output.astype(jnp.bfloat16)
    return (normed_low, inv_root, joined, output_low, log_total, plain_product(output_low, w_out))


def plain_attention_back(d_h, h, saved, norm_gain, w_qkv, w_out, key_mask):
    normed_low, inv_root, joined, output_low, log_total, unused = saved
    d_low = d_h.astype(jnp.bfloat16)
    d_wout = plain_product(output_low.T, d_low)
    d_output = plain_product(d_low, w_out.T).astype(jnp.bfloat16)
    q, k, v = jnp.split(joined, 3, axis=1)
    d_query, d_key, d_value = plain_attend_back(q, k, v, key_mask, log_total, d_output)
    d_joined = jnp.concatenate([d_query, d_key, d_value], axis=1).astype(jnp.bfloat16)
    d_wqkv = plain_product(normed_low.T, d_joined)
    d_normed = plain_product(d_joined, w_qkv.T)
    d_input, d_gain = plain_norm_back(d_normed, h, inv_root, norm_gain)
    return (d_input, d_gain, d_wqkv, d_wout)


def plain_mlp_forward(h, norm_gain, w_in, w_down):
    normed, inv_root = plain_norm_forward(h, norm_gain)
    normed_low = normed.astype(jnp.bfloat16)
    joined = plain_product(normed_low, w_in)
    gate, upper = jnp.split(joined, 2, axis=1)
    hidden_low = (jax.nn.gelu(gate, approximate=True) * upper).astype(jnp.bfloat16)
    return (normed_low, inv_root, joined, hidden_low, plain_product(hidden_low, w_down))


def plain_mlp_back(d_h, h, saved, norm_gain, w_in, w_down):
    normed_low, inv_root, joined, hidden_low, unused = saved
    d_low = d_h.astype(jnp.bfloat16)
    d_wdown = plain_product(hidden_low.T, d_low)
    d_hidden = plain_product(d_low, w_down.T)
    gate, upper = jnp.split(joined, 2, axis=1)
    active, active_back = jax.vjp(partial(jax.nn.gelu, approximate=True), gate)
    d_gate = active_back(d_hidden * upper)[0]
    d_upper = d_hidden * active
    d_joined = jnp.concatenate([d_gate, d_upper], axis=1).astype(jnp.bfloat16)
    d_win = plain_product(normed_low.T, d_joined)
    d_normed = plain_product(d_joined, w_in.T)
    d_input, d_gain = plain_norm_back(d_normed, h, inv_root, norm_gain)
    return (d_input, d_gain, d_win, d_wdown)


def encoder_forward(weights, source):
    gains, w_qkv, w_out, w_cross, w_in, w_down = weights
    inputs = source.astype(jnp.float32)
    attn_saved = plain_attention_forward(inputs, gains[0], w_qkv, w_out, None)
    middle = inputs + attn_saved[-1]
    mlp_saved = plain_mlp_forward(middle, gains[1], w_in, w_down)
    final = middle + mlp_saved[-1]
    normed, inv_root = plain_norm_forward(final, gains[2])
    memory = normed.astype(jnp.bfloat16)
    key_value = plain_product(memory, w_cross).astype(jnp.bfloat16)
    return (inputs, attn_saved, middle, mlp_saved, final, inv_root, memory, key_value)


def encoder_front(weights, source):
    saved = encoder_forward(weights, source)
    return (saved[7], saved[6])


def encoder_back_saved(weights, saved, d_keyvalue):
    gains, w_qkv, w_out, w_cross, w_in, w_down = weights
    inputs, attn_saved, middle, mlp_saved, final, inv_root, memory, key_value = saved
    d_wcross = plain_product(memory.T, d_keyvalue)
    d_memory = plain_product(d_keyvalue, w_cross.T)
    d_final, gain_last = plain_norm_back(d_memory, final, inv_root, gains[2])
    d_part, gain_mlp, d_win, d_wdown = plain_mlp_back(d_final, middle, mlp_saved, gains[1], w_in, w_down)
    d_middle = d_final + d_part
    d_first, gain_attn, d_wqkv, d_wout = plain_attention_back(
        d_middle, inputs, attn_saved, gains[0], w_qkv, w_out, None
    )
    grads = (jnp.stack([gain_attn, gain_mlp, gain_last]), d_wqkv, d_wout, d_wcross, d_win, d_wdown)
    return (d_middle + d_first, grads)


def encoder_back(weights, source, d_keyvalue):
    return encoder_back_saved(weights, encoder_forward(weights, source), d_keyvalue)


def decoder_pass(weights, source, key_value, weight_cot, length, factor):
    gains, w_qkv, w_out, w_cross, w_in, w_down = weights
    width = source.shape[1]
    inputs = source.astype(jnp.float32)
    position = jnp.arange(inputs.shape[0], dtype=jnp.int32)
    is_valid = position < length
    key_mask = (position[None, :] <= position[:, None]) & is_valid[None, :]
    attn_saved = plain_attention_forward(inputs, gains[0], w_qkv, w_out, key_mask)
    middle = inputs + attn_saved[-1]
    normed, inv_root = plain_norm_forward(middle, gains[1])
    normed_low = normed.astype(jnp.bfloat16)
    w_query = w_cross[:, :width]
    w_back = w_cross[:, width:]
    queries = plain_product(normed_low, w_query).astype(jnp.bfloat16)
    mem_keys = key_value[:, :width]
    mem_values = key_value[:, width:]
    cross_out, cross_total = plain_attend_forward(queries, mem_keys, mem_values, None)
    cross_low = cross_out.astype(jnp.bfloat16)
    after = middle + plain_product(cross_low, w_back)
    mlp_saved = plain_mlp_forward(after, gains[2], w_in, w_down)
    final = after + mlp_saved[-1]
    d_final = jnp.where(is_valid[:, None], weight_cot.astype(jnp.float32) * factor, 0.0)
    d_part, gain_mlp, d_win, d_wdown = plain_mlp_back(d_final, after, mlp_saved, gains[2], w_in, w_down)
    d_after = d_final + d_part
    d_low = d_after.astype(jnp.bfloat16)
    d_wback = plain_product(cross_low.T, d_low)
    d_cross = plain_product(d_low, w_back.T).astype(jnp.bfloat16)
    d_query, d_key, d_value = plain_attend_back(queries, mem_keys, mem_values, None, cross_total, d_cross)
    d_query_low = d_query.astype(jnp.bfloat16)
    d_wquery = plain_product(normed_low.T, d_query_low)
    d_normed = plain_product(d_query_low, w_query.T)
    d_norm_in, gain_cross = plain_norm_back(d_normed, middle, inv_root, gains[1])
    d_middle = d_after + d_norm_in
    d_keyvalue = jnp.concatenate([d_key, d_value], axis=1).astype(jnp.bfloat16)
    d_first, gain_attn, d_wqkv, d_wout = plain_attention_back(
        d_middle, inputs, attn_saved, gains[0], w_qkv, w_out, key_mask
    )
    grads = (
        jnp.stack([gain_attn, gain_cross, gain_mlp]),
        d_wqkv,
        d_wout,
        jnp.concatenate([d_wquery, d_wback], axis=1),
        d_win,
        d_wdown,
    )
    return (final.astype(jnp.bfloat16), d_middle + d_first, d_keyvalue, grads)


def on_section(flag, work, operands):

    def run_work(values):
        return work(*values)

    def skip_work(values):
        return jax.tree.map(jnp.zeros_like, work(*values))

    return lax.cond(flag, run_work, skip_work, operands)


def plain_body(
    block_in,
    cotangent,
    lengths,
    sources,
    loss_weight,
    gains,
    qkv_weight,
    out_weight,
    cross_weight,
    in_weight,
    down_weight,
):
    is_encoder = lax.axis_index("section") == 0
    is_decoder = jnp.logical_not(is_encoder)
    wide = lax.axis_size("dp")
    gathered = (
        lax.all_gather(gains, "dp", axis=2, tiled=True),
        lax.all_gather(qkv_weight, "dp", axis=1, tiled=True),
        lax.all_gather(out_weight, "dp", axis=1, tiled=True),
        lax.all_gather(cross_weight, "dp", axis=1, tiled=True),
        lax.all_gather(in_weight, "dp", axis=1, tiled=True),
        lax.all_gather(down_weight, "dp", axis=1, tiled=True),
    )
    weights = tuple((w[0] for w in gathered))
    onehot = (sources[:, None] == jnp.arange(3, dtype=jnp.int32)[None, :]).astype(jnp.float32)
    counts = lax.psum(jnp.sum(onehot * lengths[:, None].astype(jnp.float32), axis=0), "dp")
    own_count = jnp.sum(onehot * counts[None, :], axis=1)
    own_weight = jnp.sum(onehot * loss_weight[None, :].astype(jnp.float32), axis=1)
    scale = own_weight * (lengths.shape[0] * wide * block_in.shape[2] / 3.0) / own_count

    def step(carry, item):
        source, weight_cot, length, factor = item
        key_value, memory = on_section(is_encoder, encoder_front, (weights, source))
        received = shifted(key_value, "section", 1)
        decoded, table_grad, d_keyvalue, dec_grads = on_section(
            is_decoder, decoder_pass, (weights, source, received, weight_cot, length, factor)
        )
        returned = shifted(d_keyvalue, "section", -1)
        plot_grad, enc_grads = on_section(is_encoder, encoder_back, (weights, source, returned))
        grads = tuple((a + b for a, b in zip(dec_grads, enc_grads)))
        carry = tuple((a + b for a, b in zip(carry, grads)))
        return (carry, (memory + decoded, plot_grad + table_grad))

    start = tuple((jnp.zeros(w.shape, jnp.float32) for w in weights))
    carry, (outputs, input_grads) = lax.scan(step, start, (block_in[0], cotangent, lengths, scale))
    gain_total, qkv_total, out_total, cross_sum, in_total, down_total = carry
    reduced = (
        lax.psum_scatter(gain_total[None], "dp", scatter_dimension=2, tiled=True),
        lax.psum_scatter(qkv_total[None], "dp", scatter_dimension=1, tiled=True),
        lax.psum_scatter(out_total[None], "dp", scatter_dimension=1, tiled=True),
        lax.psum_scatter(cross_sum[None], "dp", scatter_dimension=1, tiled=True),
        lax.psum_scatter(in_total[None], "dp", scatter_dimension=1, tiled=True),
        lax.psum_scatter(down_total[None], "dp", scatter_dimension=1, tiled=True),
    )
    return (
        outputs[None],
        input_grads[None],
        reduced[0],
        reduced[1],
        reduced[2],
        reduced[3],
        reduced[4],
        reduced[5],
    )


def tiled_body(
    block_in, cotangent, lengths, sources, loss_weight, gains, qkv_weight, out_weight, cross_weight, in_weight, down_weight
):
    wide = lax.axis_size("dp")
    pairs, seq, width = block_in.shape[1:]
    x, cot = block_in.reshape(pairs * seq, width), cotangent.reshape(pairs * seq, width)
    results = run_step(
        wide, seq, lengths, sources, loss_weight, gains[0], x, cot,
        qkv_weight[0], out_weight[0], cross_weight[0], in_weight[0], down_weight[0],
    )
    block_out, input_grad, down, inner, cross, out, qkv, gains_sum = copied(results[-8:-1], results[-1], gains.shape[1:])
    return (
        block_out.reshape(block_in.shape),
        input_grad.reshape(block_in.shape),
        gains_sum[None],
        qkv[None],
        out[None],
        cross[None],
        inner[None],
        down[None],
    )


def solution(mesh):
    in_specs = (
        P("section", "dp", None, None),
        P("dp", None, None),
        P("dp"),
        P("dp"),
        P(),
        P("section", None, "dp"),
        P("section", "dp", None),
        P("section", "dp", None),
        P("section", "dp", None),
        P("section", "dp", None),
        P("section", "dp", None),
    )
    out_specs = (
        P("section", "dp", None, None),
        P("section", "dp", None, None),
        P("section", None, "dp"),
        P("section", "dp", None),
        P("section", "dp", None),
        P("section", "dp", None),
        P("section", "dp", None),
        P("section", "dp", None),
    )

    def body(*args):
        shards = args[6:]
        tiled = args[5].shape[2] <= 128 and all(w.shape[1] % 16 == 0 for w in shards)
        return (tiled_body if tiled else plain_body)(*args)

    return jax.shard_map(body, mesh=mesh, in_specs=in_specs, out_specs=out_specs, check_vma=False)
```

```python
from functools import partial

import jax
import jax.numpy as jnp
from jax import lax
from jax.experimental import pallas as pl
from jax.experimental.pallas import tpu as pltpu
from jax.sharding import PartitionSpec as P

HEADS = 12
HEAD_DIM = 64


EPS = 1e-06
NEG = -1000000000.0


MESH = pl.DeviceIdType.MESH
VMEM_LIMIT = 62 * 2**20
F32, BF16 = jnp.float32, jnp.bfloat16
ANY = pl.BlockSpec(memory_space=pl.ANY)
SMEM = pl.BlockSpec(memory_space=pltpu.SMEM)
VMEM = pl.BlockSpec(memory_space=pltpu.VMEM)


def ring_position(chip, chips):
    return jnp.where(chip % 2 == 0, chip // 2, chips - 1 - chip // 2)


def ring_chip(position, chips):
    position = lax.rem(position + 2 * chips, chips)
    return jnp.where(position < chips // 2, 2 * position, 2 * (chips - 1 - position) + 1)


def ring_hops(long_way, chips):
    long, short = chips // 2, chips - 1 - chips // 2
    return (long, short) if long_way == 0 else (short, long)


def slot_of(long_way, way, distance, chips):
    return distance if distance == 0 or way == long_way else chips // 2 + distance


def entry_barrier(partners):
    barrier = pltpu.get_barrier_semaphore()
    for partner in partners:
        pl.semaphore_signal(barrier, inc=1, device_id=partner, device_id_type=MESH)
    pl.semaphore_wait(barrier, len(partners))


def remote(src, dst, send_sem, recv_sem, target):
    return pltpu.make_async_remote_copy(
        src_ref=src,
        dst_ref=dst,
        send_sem=send_sem,
        recv_sem=recv_sem,
        device_id=target,
        device_id_type=MESH,
    )


class Place:
    def __init__(self, wide):
        self.chips = wide // 2
        self.section, self.me = lax.axis_index("section"), lax.axis_index("dp")
        self.chip, self.core = self.me // 2, lax.rem(self.me, 2)
        self.spot = ring_position(self.chip, self.chips)
        self.ahead = (self.section, 2 * ring_chip(self.spot + 1, self.chips) + self.core)
        self.behind = (self.section, 2 * ring_chip(self.spot - 1, self.chips) + self.core)
        self.twin = (self.section, 2 * self.chip + 1 - self.core)
        self.across = (1 - self.section, self.me)

    def next_of(self, way):
        return self.ahead if way == 0 else self.behind

    def chip_at(self, way, distance):
        return ring_chip(self.spot + distance if way == 0 else self.spot - distance, self.chips)


def block_rows(ref, rows, chip, core):
    return ref.at[pl.ds(pl.multiple_of((2 * chip + core) * rows, rows), rows)]


class Gather:
    def __init__(self, place, names, shards, fulls, rows, long_way, sems):
        self.place, self.names = place, names
        self.shards, self.fulls, self.rows, self.long_way = shards, fulls, rows, long_way
        self.own_sem, self.ring_send, self.ring_recv, self.twin_send, self.twin_recv = sems

    def hops(self, name, way):
        return ring_hops(self.long_way[name], self.place.chips)[way]

    def pieces(self, name, way, hop):
        at = self.place
        origin = at.chip_at(way, -hop)
        target = block_rows(self.fulls[name], self.rows[name], origin, at.core)
        own = self.shards.get(name)
        return (own if hop == 0 and own is not None else target), target

    def ring(self, name, way, hop):
        source, target = self.pieces(name, way, hop)
        i = self.names.index(name)
        return remote(
            source, target, self.ring_send.at[i, way, hop], self.ring_recv.at[i, way, hop], self.place.next_of(way)
        )

    def pair(self, name, way, hop):
        source, target = self.pieces(name, way, hop)
        i, slot = self.names.index(name), slot_of(self.long_way[name], way, hop, self.place.chips)
        return remote(source, target, self.twin_send.at[i, slot], self.twin_recv.at[i, slot], self.place.twin)

    def own(self, name):
        source, target = self.pieces(name, 0, 0)
        return pltpu.make_async_copy(source, target, self.own_sem.at[self.names.index(name)])

    def start(self, name):
        for way in range(2):
            self.ring(name, way, 0).start()
        self.pair(name, 0, 0).start()
        if name in self.shards:
            self.own(name).start()

    def step(self, name, hop):
        for way in range(2):
            hops = self.hops(name, way)
            if hop < hops:
                self.ring(name, way, hop).wait_recv()
                if hop + 1 < hops:
                    self.ring(name, way, hop + 1).start()
                self.pair(name, way, hop + 1).start()

    def complete(self, name):
        if name in self.shards:
            self.own(name).wait()
        self.pair(name, 0, 0).wait_recv()
        for way in range(2):
            for hop in range(self.hops(name, way)):
                self.pair(name, way, hop + 1).wait_recv()

    def drain(self, names):
        for name in names:
            self.pair(name, 0, 0).wait_send()
            for way in range(2):
                for hop in range(self.hops(name, way)):
                    self.pair(name, way, hop + 1).wait_send()
                    self.ring(name, way, hop).wait_send()


LONG_WAY = {"small": 0, "qkv": 0, "out": 1, "crossE": 0, "crossD": 1, "in": 1, "down": 0, "gains": 0}


class Scatter:
    def __init__(self, place, names, grads, rows, long_way, twins, arrived, sems):
        self.place, self.names, self.grads, self.rows, self.long_way = place, names, grads, rows, long_way
        self.twins, self.arrived = twins, arrived
        self.twin_send, self.twin_recv, self.ring_send, self.ring_recv = sems

    def hops(self, name, way):
        return ring_hops(self.long_way[name], self.place.chips)[way]

    def landing(self, name, way, hop):
        return self.arrived[name].at[hop if way == self.long_way[name] else self.place.chips // 2 + hop]

    def block(self, name, way, distance, core):
        return block_rows(self.grads[name], self.rows[name], self.place.chip_at(way, distance), core)

    def pair(self, name, way, distance):
        at, i = self.place, self.names.index(name)
        slot = slot_of(self.long_way[name], way, distance, at.chips)
        source = self.block(name, way, distance, 1 - at.core)
        return remote(source, self.twins[name].at[slot], self.twin_send.at[i, slot], self.twin_recv.at[i, slot], at.twin)

    def ring(self, name, way, hop):
        at, i = self.place, self.names.index(name)
        return remote(
            self.block(name, way, self.hops(name, way) - hop, at.core),
            self.landing(name, way, hop),
            self.ring_send.at[i, way, hop],
            self.ring_recv.at[i, way, hop],
            at.next_of(way),
        )

    def slots(self, name):
        found = []
        for hop in range(self.place.chips // 2 + 1):
            for way in range(2):
                distance = self.hops(name, way) - hop
                if distance > 0 or (distance == 0 and way == self.long_way[name]):
                    found.append((way, distance))
        return found

    def start(self, name):
        for way, distance in self.slots(name):
            self.pair(name, way, distance).start()

    def add(self, name, way, distance, terms, out=None):
        at, rows, grad = self.place, self.rows[name], self.grads[name]
        group = 16 if rows % 16 == 0 else rows
        tile = next(t for t in (1024, 768, 128) if grad.shape[1] % t == 0)
        first = (2 * at.chip_at(way, distance) + at.core) * rows
        slot = slot_of(self.long_way[name], way, distance, at.chips)

        @pl.loop(0, rows // group)
        def _(n):
            part = span(n * group, group)
            own = pl.ds(pl.multiple_of(first + n * group, group), group)

            @pl.loop(0, grad.shape[1] // tile)
            def _(m):
                columns = span(m * tile, tile)
                total = grad[own, columns].astype(F32) + self.twins[name][slot, part, columns].astype(F32)
                for term in terms:
                    total += term[part, columns].astype(F32)
                if out is None:
                    grad[own, columns] = total.astype(grad.dtype)
                else:
                    out[part, columns] = total

    def step(self, name, way, hop):
        distance = self.hops(name, way) - hop
        if distance <= 0:
            return
        self.pair(name, way, distance).wait_recv()
        terms = []
        if hop > 0:
            self.ring(name, way, hop - 1).wait_recv()
            terms.append(self.landing(name, way, hop - 1))
        self.add(name, way, distance, terms)
        self.ring(name, way, hop).start()

    def finish(self, name, out):
        self.pair(name, self.long_way[name], 0).wait_recv()
        terms = []
        for way in range(2):
            last = self.hops(name, way) - 1
            self.ring(name, way, last).wait_recv()
            terms.append(self.landing(name, way, last))
        self.add(name, self.long_way[name], 0, terms, out)

    def drain(self, name):
        for way, distance in self.slots(name):
            self.pair(name, way, distance).wait_send()
        for way in range(2):
            for hop in range(self.hops(name, way)):
                self.ring(name, way, hop).wait_send()


def dot(a, b, over_a=1, over_b=0):
    return lax.dot_general(a, b, (((over_a,), (over_b,)), ((), ())), preferred_element_type=F32)


def span(start, size):
    return pl.ds(start, size) if isinstance(start, int) else pl.ds(pl.multiple_of(start, size), size)


def each(total, tile, work):
    @pl.loop(0, total // tile)
    def _(n):
        work(span(n * tile, tile))


ROWS = 64


def norm_into(h_ref, gain, out_ref):
    def work(at):
        h = h_ref[at].astype(F32)
        inv_root = lax.rsqrt(jnp.mean(h * h, axis=-1, keepdims=True) + EPS)
        out_ref[at] = (h * inv_root * gain).astype(out_ref.dtype)

    each(h_ref.shape[0], ROWS, work)


def norm_back(dn_ref, h_ref, gain, gain_sum, row, finish, start=0, size=None):
    if start == 0:
        gain_sum[row] = jnp.zeros(gain_sum.shape[1:], F32)

    def work(part):
        at = span(start + part.start, ROWS)
        h, dn = h_ref[at].astype(F32), dn_ref[at].astype(F32)
        inv_root = lax.rsqrt(jnp.mean(h * h, axis=-1, keepdims=True) + EPS)
        scaled = h * inv_root
        product = dn * scaled
        gain_sum[row] += jnp.sum(product.reshape(-1, 8, product.shape[1]), axis=0)
        inner = dn * gain
        finish(at, inv_root * (inner - scaled * jnp.mean(product * gain, axis=-1, keepdims=True)))

    each(size or h_ref.shape[0], ROWS, work)


def pair_columns(ref, rows, start, two):
    return ref[rows, span(start + two * 2 * HEAD_DIM, 2 * HEAD_DIM)]


def side_masks():
    lane = lax.broadcasted_iota(jnp.int32, (1, 2 * HEAD_DIM), 1)
    first = lane < HEAD_DIM
    return first, (first.astype(F32).astype(BF16), (1 - first.astype(F32)).astype(BF16))


def expo_columns(q, k, seq, length):
    scores = dot(k, q, 1, 1) * HEAD_DIM ** (-0.5)
    if length is not None:
        key = lax.broadcasted_iota(jnp.int32, (seq, seq), 0)
        query = lax.broadcasted_iota(jnp.int32, (seq, seq), 1)
        scores = jnp.where((key <= query) & (key < length), scores, NEG)
    expo = jnp.exp(scores - jnp.max(scores, axis=0, keepdims=True))
    return expo, jnp.sum(expo, axis=0, keepdims=True)


def attend(q_ref, q_at, k_ref, k_at, v_ref, v_at, out_ref, seq, lengths, chosen=None):
    start, stop = chosen or (0, q_ref.shape[0] // seq)
    first, keeps = side_masks()
    each_time = HEADS // 4

    @pl.loop(start * (HEADS // 2 // each_time), stop * (HEADS // 2 // each_time))
    def _(m):
        work = []
        for g in range(each_time):
            n = m * each_time + g
            pair, two = n // (HEADS // 2), lax.rem(n, HEADS // 2)
            rows = span(pair * seq, seq)
            length = None if lengths is None else lengths[pair]
            q, k, v = (pair_columns(r, rows, a, two) for r, a in ((q_ref, q_at), (k_ref, k_at), (v_ref, v_at)))
            for side in range(2):
                work.append((rows, two, length, q, k, v, side))
        expos = [expo_columns(q * keeps[side], k, seq, length) for rows, two, length, q, k, v, side in work]
        outs = [dot((e * (1.0 / t)).astype(BF16), w[5], 0, 0) for (e, t), w in zip(expos, work)]
        for g in range(each_time):
            rows, two = work[2 * g][:2]
            value = jnp.where(first, outs[2 * g], outs[2 * g + 1])
            out_ref[rows, span(two * 2 * HEAD_DIM, 2 * HEAD_DIM)] = value.astype(BF16)


def attend_back(q_ref, q_at, k_ref, k_at, v_ref, v_at, do_ref, dq, dk, dv, seq, lengths, chosen=None):
    start, stop = chosen or (0, q_ref.shape[0] // seq)
    first, keeps = side_masks()
    root = HEAD_DIM ** (-0.5)
    each_time = HEADS // 6

    @pl.loop(start * (HEADS // 2 // each_time), stop * (HEADS // 2 // each_time))
    def _(m):
        work = []
        for g in range(each_time):
            n = m * each_time + g
            pair, two = n // (HEADS // 2), lax.rem(n, HEADS // 2)
            rows = span(pair * seq, seq)
            length = None if lengths is None else lengths[pair]
            q, k, v = (pair_columns(r, rows, a, two) for r, a in ((q_ref, q_at), (k_ref, k_at), (v_ref, v_at)))
            d_out = pair_columns(do_ref, rows, 0, two)
            for side in range(2):
                work.append((rows, two, length, q, k, v, d_out, side))
        expos = [expo_columns(q * keeps[side], k, seq, length) for rows, two, length, q, k, v, d_out, side in work]
        d_probs = [dot(v, d_out * keeps[side], 1, 1) for rows, two, length, q, k, v, d_out, side in work]
        probs = [e * (1.0 / t) for e, t in expos]
        d_scores = [(p * (d - jnp.sum(p * d, axis=0, keepdims=True))).astype(BF16) for p, d in zip(probs, d_probs)]
        dvs = [dot(p.astype(BF16), w[6]) for p, w in zip(probs, work)]
        dqs = [dot(d, w[4], 0, 0) for d, w in zip(d_scores, work)]
        dks = [dot(d, w[3]) for d, w in zip(d_scores, work)]
        for g in range(each_time):
            rows, two = work[2 * g][:2]
            for (ref, start), both, factor in ((dq, dqs, root), (dk, dks, root), (dv, dvs, 1.0)):
                value = jnp.where(first, both[2 * g], both[2 * g + 1]) * factor
                ref[rows, span(start + two * 2 * HEAD_DIM, 2 * HEAD_DIM)] = value.astype(BF16)


def gelu_parts(gate):
    root, cubic = 0.7978845608028654, 0.044715
    square = gate * gate
    bent = jnp.tanh(root * gate * (1.0 + cubic * square))
    half = 0.5 * (1.0 + bent)
    slope = half + 0.5 * gate * (1.0 - bent * bent) * root * (1.0 + 3.0 * cubic * square)
    return gate * half, slope


FF_TILE = 512


def mlp_forward(a_ref, w_in, w_down, into_ref, hidden_ref=None, slopes_ref=None):
    ff = w_in.shape[1] // 2

    @pl.loop(0, ff // FF_TILE)
    def _(n):
        gates, uppers = span(n * FF_TILE, FF_TILE), span(ff + n * FF_TILE, FF_TILE)
        gate, upper = dot(a_ref[...], w_in[:, gates]), dot(a_ref[...], w_in[:, uppers])
        active, slope = gelu_parts(gate)
        hidden = (active * upper).astype(BF16)
        if hidden_ref is not None:
            hidden_ref[:, gates] = hidden
            slopes_ref[:, gates] = (slope * upper).astype(BF16)
            slopes_ref[:, uppers] = active.astype(BF16)
        if w_down is not None:
            into_ref[...] += dot(hidden, w_down[gates, :])


def mlp_back(d_low, w_in, w_down, slopes_ref, dn_ref):
    ff = w_in.shape[1] // 2
    dn_ref[...] = jnp.zeros(dn_ref.shape, F32)

    @pl.loop(0, ff // FF_TILE)
    def _(n):
        gates, uppers = span(n * FF_TILE, FF_TILE), span(ff + n * FF_TILE, FF_TILE)
        d_hidden = dot(d_low[...], w_down[gates, :], 1, 1)
        d_gate = (d_hidden * slopes_ref[:, gates]).astype(BF16)
        d_upper = (d_hidden * slopes_ref[:, uppers]).astype(BF16)
        slopes_ref[:, gates], slopes_ref[:, uppers] = d_gate, d_upper
        dn_ref[...] += dot(d_gate, w_in[:, gates], 1, 1) + dot(d_upper, w_in[:, uppers], 1, 1)


def product_into(a_ref, w_ref, out_ref, tile, w_at=0, transposed=False):
    width = out_ref.shape[1]

    @pl.loop(0, width // tile)
    def _(n):
        if transposed:
            value = dot(a_ref[...], w_ref[span(w_at + n * tile, tile), :], 1, 1)
        else:
            value = dot(a_ref[...], w_ref[:, span(w_at + n * tile, tile)])
        out_ref[:, span(n * tile, tile)] = value.astype(out_ref.dtype)


def add_product(base_ref, a_ref, w, out_ref):
    out_ref[...] = base_ref[...].astype(F32) + dot(a_ref[...], w)


class Moves:
    def __init__(self, sems):
        self.sems, self.used = sems, 0

    def start(self, src, dst):
        copy = pltpu.make_async_copy(src, dst, self.sems.at[self.used])
        self.used += 1
        copy.start()
        return copy


def weight_grad(a_ref, y_ref, grad, tile_rows, tile_columns, column_at=0):
    @pl.loop(0, a_ref.shape[1] // tile_rows)
    def _(i):
        @pl.loop(0, y_ref.shape[1] // tile_columns)
        def _(j):
            rows, columns = span(i * tile_rows, tile_rows), span(j * tile_columns, tile_columns)
            value = dot(a_ref[:, rows], y_ref[:, columns], 0, 0).astype(BF16)
            grad[rows, pl.ds(pl.multiple_of(column_at + j * tile_columns, 256), tile_columns)] = value


GATHER_NAMES = ("small", "qkv", "out", "crossE", "crossD", "in", "down")
SCATTER_NAMES = ("down", "in", "crossD", "crossE", "out", "qkv", "gains")
BLOCK = (8, 128)


def spread_gains(small, own, width):
    lane = lax.broadcasted_iota(jnp.int32, BLOCK, 1)
    total = jnp.zeros((BLOCK[0], width), F32)
    for n in range(width // own):
        part = jnp.where(lane < own, small[n * BLOCK[0] : (n + 1) * BLOCK[0], :], 0.0)
        wide = jnp.concatenate([part, jnp.zeros((BLOCK[0], width - BLOCK[1]), F32)], axis=1)
        total += wide if n == 0 else pltpu.roll(wide, n * own, 1)
    return total


def gather_blocks(gains_grad, own, out_ref):
    width = gains_grad.shape[1]
    lane = lax.broadcasted_iota(jnp.int32, BLOCK, 1)
    for n in range(width // own):
        turned = gains_grad if n == 0 else pltpu.roll(gains_grad, width - n * own, 1)
        out_ref[n * BLOCK[0] : (n + 1) * BLOCK[0], :] = jnp.where(lane < own, turned[:, : BLOCK[1]], 0.0)


def step_kernel(
    wide, seq, lengths, sources, loss_weight, gains_in, x_in, cot_in, qkv_in, out_in, cross_in, in_in, down_in,
    small_full, qkv_full, out_full, enc_full, dec_full, in_full, down_full,
    joined_kept, attended_kept, middle_kept, final_kept,
    block_out, input_out, down_sum, in_sum, cross_sum, out_sum, qkv_sum, gains_sum,
    small_own, gains, factors, gain_sum, landing, back, passed_out, passed_in, g_gains, g_down, *refs,
):
    count = len(SCATTER_NAMES)
    twins, arrived = dict(zip(SCATTER_NAMES, refs[:count])), dict(zip(SCATTER_NAMES, refs[count : 2 * count]))
    load_sem, send_sem, recv_sem = refs[2 * count : 2 * count + 3]
    gather_sems, scatter_sems = refs[2 * count + 3 : 2 * count + 8], refs[2 * count + 8 :]
    at = Place(wide)
    rows, width = x_in.shape
    pairs, own = rows // seq, gains_in.shape[1]
    vmem = pltpu.VMEM
    broad, slim = vmem((rows, width), F32), vmem((rows, width), BF16)
    lane = lax.broadcasted_iota(jnp.int32, (1, BLOCK[1]), 1)
    counted = jnp.zeros((1, BLOCK[1]), F32)
    for pair in range(pairs):
        counted += jnp.where(lane == sources[pair], lengths[pair].astype(F32), 0.0)
    small_own[...] = jnp.zeros(BLOCK, F32)
    small_own[0:3, 0:own] = gains_in[...].astype(F32)
    small_own[3:4, :] = counted
    entry_barrier((at.ahead, at.behind, at.twin, at.across))

    fulls = dict(zip(GATHER_NAMES, (small_full, qkv_full, out_full, enc_full, dec_full, in_full, down_full)))
    full_rows = {n: f.shape[0] // wide for n, f in fulls.items()}
    w_qkv_shape, w_out_shape, w_cross_shape = qkv_full.shape, out_full.shape, dec_full.shape
    w_in_shape, w_down_shape = in_full.shape, down_full.shape
    ff = w_down_shape[0]
    shapes = dict(zip(SCATTER_NAMES, (w_down_shape, w_in_shape, w_cross_shape, w_cross_shape, w_out_shape, w_qkv_shape)))
    shapes["gains"] = g_gains.shape
    share = {n: s[0] // wide for n, s in shapes.items()}
    grads = {"down": g_down, "gains": g_gains}
    scatter = Scatter(at, SCATTER_NAMES, grads, share, LONG_WAY, twins, arrived, scatter_sems)
    sums = {"down": down_sum, "in": in_sum, "out": out_sum, "qkv": qkv_sum, "gains": gains_sum}
    sums.update(crossD=cross_sum, crossE=passed_out)
    passed_weight = remote(
        cross_in, block_rows(enc_full, full_rows["crossE"], at.chip, at.core), send_sem.at[0], recv_sem.at[0], at.across
    )
    passed_sum = remote(passed_out, passed_in, send_sem.at[1], recv_sem.at[1], at.across)

    def grad_space(*names):
        return [vmem(shapes[n], BF16) for n in names]

    def to_dec(pair):
        part = span(pair * seq, seq)
        return remote(back.at[part], landing.at[part], send_sem.at[2 + pair], recv_sem.at[2 + pair], at.across)

    def to_enc(pair):
        part, i = span(pair * seq, seq), 2 + pairs + pair
        return remote(back.at[part], landing.at[part], send_sem.at[i], recv_sem.at[i], at.across)

    class Hops:
        def __init__(self):
            self.done = {}

        def hop(self, *names):
            for name in names:
                for way in range(2):
                    scatter.step(name, way, self.done.get(name, 0))
                self.done[name] = self.done.get(name, 0) + 1

        def ready(self, name):
            scatter.start(name)
            self.hop(name)

        def rest(self, names):
            for step in range(at.chips // 2 + 1):
                for name in names:
                    if self.done[name] == step < at.chips // 2:
                        self.hop(name)
                    elif self.done[name] == step:
                        scatter.finish(name, sums[name])
                        self.done[name] += 1
                        if name == "crossE":
                            passed_sum.start()

    def first_part(moves, gather, names, lengths, x, small, w_qkv, w_out, normed, joined, attended, middle, between):
        load_x = moves.start(x_in, x)
        for name in names:
            if name == "crossE":
                passed_weight.wait_recv()
            gather.start(name)
        for hop in range(at.chips // 2 - 1):
            for name in names:
                gather.step(name, hop)

        def load(name, into):
            gather.complete(name)
            return moves.start(fulls[name], into)

        gather.step("small", at.chips // 2 - 1)
        load("small", small).wait()
        gains[...] = spread_gains(small, own, width)
        totals = jnp.zeros((1, BLOCK[1]), F32)
        for n in range(wide):
            totals += small[n * BLOCK[0] + 3 : n * BLOCK[0] + 4, :]
        factors[...] = jnp.zeros(factors.shape, F32)
        for pair in range(pairs):
            source = sources[pair]
            weight = jnp.where(source == 0, loss_weight[0], jnp.where(source == 1, loss_weight[1], loss_weight[2]))
            total = jnp.sum(jnp.where(lane == source, totals, 0.0), axis=1, keepdims=True)
            factor = jnp.full((1, 1), weight.astype(F32) * (pairs * wide * seq / 3.0), F32) / total
            factors[pair : pair + 1, :] = jnp.broadcast_to(factor, (1, BLOCK[1]))
        load_x.wait()
        norm_into(x, gains[0:1], normed)
        gather.step("qkv", at.chips // 2 - 1)
        gather.step("out", at.chips // 2 - 1)
        load_qkv = load("qkv", w_qkv)
        load_out = load("out", w_out)
        load_qkv.wait()
        product_into(normed, w_qkv, joined, width)
        for name in names[3:]:
            gather.step(name, at.chips // 2 - 1)
        between()
        attend(joined, 0, joined, width, joined, 2 * width, attended, seq, lengths)
        load_out.wait()
        add_product(x, attended, w_out[...], middle)
        return [moves.start(a, b) for a, b in ((middle, middle_kept), (joined, joined_kept), (attended, attended_kept))]

    def self_back(hops, lengths, d_middle, x, normed, d_low, w_qkv, w_out, joined, attended, d_attended, dn, loads, first, second):
        each(rows, ROWS, lambda part: d_low.__setitem__(part, d_middle[part].astype(BF16)))
        weight_grad(attended, d_low, grads["out"], width // 3, width)
        hops.ready("out")
        product_into(d_low, w_out, d_attended, width, transposed=True)
        hops.hop(*first)
        for load in loads:
            load.wait()
        attend_back(
            joined, 0, joined, width, joined, 2 * width, d_attended,
            (joined, 0), (joined, width), (joined, 2 * width), seq, lengths,
        )
        hops.hop(*second)
        norm_into(x, gains[0:1], normed)
        weight_grad(normed, joined, grads["qkv"], width // 3, width)
        hops.ready("qkv")
        product_into(joined, w_qkv, dn, width, transposed=True)

        def finish(part, d_input):
            d_middle[part] = d_middle[part] + d_input

        norm_back(dn, x, gains[0:1], gain_sum, 0, finish)

    def gains_ready(hops):
        lines = [jnp.sum(gain_sum[row], axis=0, keepdims=True) for row in range(3)]
        gather_blocks(jnp.concatenate(lines + [jnp.zeros((BLOCK[0] - 3, width), F32)], axis=0), own, g_gains)
        hops.ready("gains")

    @pl.when(at.section == 0)
    def _():
        moves, hops = Moves(load_sem), Hops()
        passed_weight.start()
        names = ("small", "qkv", "out", "in", "down")
        shards = dict(zip(names, (small_own, qkv_in, out_in, in_in, down_in)))
        gather = Gather(at, GATHER_NAMES, shards, fulls, full_rows, LONG_WAY, gather_sems)

        def ahead(x, small, w_qkv, w_out, normed, joined, attended, middle, w_in, w_down):
            loads = []

            def between():
                for name, into in (("in", w_in), ("down", w_down)):
                    gather.complete(name)
                    loads.append(moves.start(fulls[name], into))

            stores = first_part(
                moves, gather, names, None, x, small, w_qkv, w_out, normed, joined, attended, middle, between
            )
            norm_into(middle, gains[1:2], normed)
            for copy in loads + stores[:1]:
                copy.wait()
            mlp_forward(normed, w_in, w_down, middle)
            stores.append(moves.start(middle, final_kept))
            for pair in range(pairs):
                part = pl.ds(pair * seq, seq)
                norm_into(middle.at[part], gains[2:3], back.at[part])
                to_dec(pair).start()
            stores.append(moves.start(back, block_out))
            for copy in stores[1:]:
                copy.wait()

        pl.run_scoped(
            ahead,
            slim, vmem(small_full.shape, F32), vmem(w_qkv_shape, BF16), vmem(w_out_shape, BF16),
            slim, vmem((rows, 3 * width), BF16), slim, broad, vmem(w_in_shape, BF16), vmem(w_down_shape, BF16),
        )

        def backward(final, normed, w_out, attended, g_in, g_out, g_qkv):
            grads.update({"in": g_in, "out": g_out, "qkv": g_qkv})
            early = [moves.start(a, b) for a, b in ((out_full, w_out), (attended_kept, attended))]

            def feed(w_in, w_down, middle, hidden, slopes, d_low, dn):
                loads = [
                    moves.start(a, b)
                    for a, b in ((middle_kept, middle), (in_full, w_in), (final_kept, final), (down_full, w_down))
                ]
                for load in loads:
                    load.wait()
                norm_into(middle, gains[1:2], normed)
                mlp_forward(normed, w_in, None, None, hidden, slopes)

                def finish_final(part, d_input):
                    final[part] = d_input
                    d_low[part] = d_input.astype(BF16)

                for pair in range(pairs):
                    to_enc(pair).wait_recv()
                    norm_back(landing, final, gains[2:3], gain_sum, 2, finish_final, pair * seq, seq)
                weight_grad(hidden, d_low, g_down, ff // 4, width)
                hops.ready("down")
                mlp_back(d_low, w_in, w_down, slopes, dn)
                hops.hop("down")
                weight_grad(normed, slopes, g_in, width // 3, ff // 2)
                hops.ready("in")
                hops.hop("down")

                def finish_middle(part, d_input):
                    final[part] = final[part] + d_input

                norm_back(dn, middle, gains[1:2], gain_sum, 1, finish_middle)

            pl.run_scoped(
                feed,
                vmem(w_in_shape, BF16), vmem(w_down_shape, BF16), broad, vmem((rows, ff), BF16), vmem((rows, 2 * ff), BF16),
                slim, broad,
            )

            def attention(w_qkv, x, joined, d_low, d_attended, dn):
                loads = [moves.start(a, b) for a, b in ((joined_kept, joined), (x_in, x), (qkv_full, w_qkv))]
                for load in early:
                    load.wait()
                self_back(
                    hops, None, final, x, normed, d_low, w_qkv, w_out, joined, attended, d_attended, dn, loads, ("in",), ("out", "in")
                )
                store = moves.start(final, input_out)
                gains_ready(hops)
                hops.rest(("down", "in", "out", "qkv", "gains"))
                store.wait()

            pl.run_scoped(
                attention,
                vmem(w_qkv_shape, BF16), slim, vmem((rows, 3 * width), BF16), slim, slim, broad,
            )
            for name in ("down", "in", "out", "qkv", "gains"):
                scatter.drain(name)

        pl.run_scoped(backward, broad, slim, vmem(w_out_shape, BF16), slim, *grad_space("in", "out", "qkv"))
        gather.drain(names)
        passed_weight.wait_send()
        for pair in range(pairs):
            to_dec(pair).wait_send()
        passed_sum.wait_recv()
        cross_sum[...] = passed_in[...]

    @pl.when(at.section == 1)
    def _():
        moves, hops = Moves(load_sem), Hops()
        names = ("small", "qkv", "out", "crossD", "crossE", "in", "down")
        shards = {"small": small_own, "qkv": qkv_in, "out": out_in, "crossD": cross_in, "in": in_in, "down": down_in}
        gather = Gather(at, GATHER_NAMES, shards, fulls, full_rows, LONG_WAY, gather_sems)

        def ahead(x, small, w_qkv, w_out, normed, joined, attended, middle):
            stores = first_part(
                moves, gather, names, lengths, x, small, w_qkv, w_out, normed, joined, attended, middle, lambda: None
            )
            for store in stores:
                store.wait()

        pl.run_scoped(
            ahead,
            slim, vmem(small_full.shape, F32), vmem(w_qkv_shape, BF16), vmem(w_out_shape, BF16),
            slim, vmem((rows, 3 * width), BF16), slim, broad,
        )

        def rest(cot, normed_a, keyval, crossed, normed_b, slopes, d_low2, d_after):
            d_queries, d_keyval, memory = cot, keyval, landing

            def to_memory(w_enc, w_dec, w_in, w_down, queries, after, hidden, d_low, dn, d_crossed, middle):
                load_middle = moves.start(middle_kept, middle)
                load_cot = moves.start(cot_in, cot)
                loads = []
                for name, into in (("crossD", w_dec), ("crossE", w_enc)):
                    gather.complete(name)
                    loads.append(moves.start(fulls[name], into))
                load_middle.wait()
                norm_into(middle, gains[1:2], normed_a)
                loads[0].wait()
                product_into(normed_a, w_dec, queries, width)
                loads[1].wait()
                for name, into in (("in", w_in), ("down", w_down)):
                    gather.complete(name)
                    loads.append(moves.start(fulls[name], into))

                @pl.loop(0, pairs)
                def _(pair):
                    part = span(pair * seq, seq)
                    to_dec(pair).wait_recv()
                    product_into(memory.at[part], w_enc, keyval.at[part], width)
                    attend(queries, 0, keyval, 0, keyval, width, crossed, seq, None, (pair, pair + 1))

                add_product(middle, crossed, w_dec[:, width:], after)
                norm_into(after, gains[2:3], normed_b)
                for load in loads[2:] + [load_cot]:
                    load.wait()
                dn[...] = after[...]
                mlp_forward(normed_b, w_in, w_down, dn, hidden, slopes)

                for pair in range(pairs):

                    @pl.loop(0, seq // ROWS)
                    def _(n):
                        part = span(pair * seq + n * ROWS, ROWS)
                        position = n * ROWS + lax.broadcasted_iota(jnp.int32, (ROWS, 1), 0)
                        d_low2[part] = dn[part].astype(BF16)
                        factor = factors[pair : pair + 1, 0:1]
                        d_final = jnp.where(position < lengths[pair], cot[part].astype(F32) * factor, 0.0)
                        d_after[part] = d_final
                        d_low[part] = d_final.astype(BF16)

                store = moves.start(d_low2, block_out)
                weight_grad(hidden, d_low, g_down, ff // 4, width)
                hops.ready("down")
                mlp_back(d_low, w_in, w_down, slopes, dn)
                hops.hop("down")
                store.wait()

                def finish_after(part, d_input):
                    total = d_after[part] + d_input
                    d_after[part] = total
                    d_low2[part] = total.astype(BF16)

                norm_back(dn, after, gains[2:3], gain_sum, 2, finish_after)
                d_crossed[...] = dot(d_low2[...], w_dec[:, width:], 1, 1).astype(BF16)

                @pl.loop(0, pairs)
                def _(pair):
                    part = span(pair * seq, seq)
                    attend_back(
                        queries, 0, keyval, 0, keyval, width, d_crossed,
                        (d_queries, 0), (d_keyval, 0), (d_keyval, width), seq, None, (pair, pair + 1),
                    )
                    back[part] = dot(d_keyval[part], w_enc[...], 1, 1).astype(BF16)
                    to_enc(pair).start()

                hops.hop("down")
                dn[...] = dot(d_queries[...], w_dec[:, :width], 1, 1)

                def finish_middle(part, d_input):
                    d_after[part] = d_after[part] + d_input

                norm_back(dn, middle, gains[1:2], gain_sum, 1, finish_middle)

            pl.run_scoped(
                to_memory,
                vmem(w_cross_shape, BF16), vmem(w_cross_shape, BF16), vmem(w_in_shape, BF16), vmem(w_down_shape, BF16),
                slim, broad, vmem((rows, ff), BF16), slim, broad, slim, broad,
            )

            def to_input(w_qkv, w_out, d_low, d_attended, dn, g_in, g_dec, g_enc, g_out, g_qkv):
                grads.update({"in": g_in, "crossD": g_dec, "crossE": g_enc, "out": g_out, "qkv": g_qkv})
                load_out = moves.start(out_full, w_out)
                loads = [moves.start(qkv_full, w_qkv)]
                weight_grad(normed_b, slopes, g_in, width // 3, ff // 2)
                hops.ready("in")
                joined = slopes.at[:, pl.ds(0, 3 * width)]
                loads.append(moves.start(joined_kept, joined))
                weight_grad(memory, d_keyval, g_enc, width // 3, width)
                hops.ready("crossE")
                loads.append(moves.start(x_in, memory))
                weight_grad(crossed, d_low2, g_dec, width // 3, width, column_at=width)
                load_attended = moves.start(attended_kept, crossed)
                weight_grad(normed_a, d_queries, g_dec, width // 3, width)
                hops.ready("crossD")
                load_out.wait()
                load_attended.wait()
                self_back(
                    hops, lengths, d_after, memory, normed_a, d_low, w_qkv, w_out, joined, crossed, d_attended, dn, loads,
                    ("down",), ("in", "crossE"),
                )
                store = moves.start(d_after, input_out)
                gains_ready(hops)
                hops.rest(("crossE", "down", "in", "crossD", "out", "qkv", "gains"))
                store.wait()
                for name in SCATTER_NAMES:
                    scatter.drain(name)

            pl.run_scoped(
                to_input,
                vmem(w_qkv_shape, BF16), vmem(w_out_shape, BF16), slim, slim, broad,
                *grad_space("in", "crossD", "crossE", "out", "qkv"),
            )

        pl.run_scoped(
            rest,
            slim, slim, vmem((rows, 2 * width), BF16), slim, slim, vmem((rows, 2 * ff), BF16), slim, broad,
        )
        gather.drain(names)
        for pair in range(pairs):
            to_enc(pair).wait_send()
        passed_sum.wait_send()


def run_step(wide, seq, lengths, sources, loss_weight, gains, x, cot, w_qkv, w_out, w_cross, w_in, w_down):
    (rows, width), chips, pairs = x.shape, wide // 2, x.shape[0] // seq
    vmem, shaped, dma = pltpu.VMEM, jax.ShapeDtypeStruct, pltpu.SemaphoreType.DMA
    fulls = [(wide * w.shape[0], w.shape[1]) for w in (w_qkv, w_out, w_cross, w_cross, w_in, w_down)]
    shares = [w.shape for w in (w_down, w_in, w_cross, w_cross, w_out, w_qkv)] + [BLOCK]
    types = [BF16] * 6 + [F32]
    gathered, scattered = len(GATHER_NAMES), len(SCATTER_NAMES)
    return pl.pallas_call(
        partial(step_kernel, wide, seq),
        out_shape=[shaped((wide * BLOCK[0], BLOCK[1]), F32)]
        + [shaped(f, BF16) for f in fulls]
        + [shaped((rows, 3 * width), BF16), shaped((rows, width), BF16)]
        + [shaped((rows, width), F32)] * 2
        + [shaped((rows, width), BF16), shaped((rows, width), F32)]
        + [shaped(shares[n], F32) for n in (0, 1, 2, 4, 5, 6)],
        in_specs=[SMEM] * 3 + [VMEM] + [ANY] * 7,
        out_specs=[ANY] * 13 + [VMEM] * 6,
        scratch_shapes=[
            vmem(BLOCK, F32),
            vmem((BLOCK[0], width), F32),
            vmem(BLOCK, F32),
            vmem((3, 8, width), F32),
            vmem((rows, width), BF16),
            vmem((rows, width), BF16),
            vmem(w_cross.shape, F32),
            vmem(w_cross.shape, F32),
            vmem((wide * BLOCK[0], BLOCK[1]), F32),
            vmem(fulls[5], BF16),
        ]
        + [vmem((chips,) + s, t) for s, t in zip(shares, types)]
        + [vmem((chips - 1,) + s, t) for s, t in zip(shares, types)]
        + [dma((64,)), dma((2 + 2 * pairs,)), dma((2 + 2 * pairs,))]
        + [dma((gathered,)), dma((gathered, 2, chips // 2)), dma((gathered, 2, chips // 2))]
        + [dma((gathered, chips)), dma((gathered, chips)), dma((scattered, chips)), dma((scattered, chips))]
        + [dma((scattered, 2, chips // 2)), dma((scattered, 2, chips // 2))],
        name="encoder_and_decoder",
        compiler_params=pltpu.CompilerParams(collective_id=0, has_side_effects=True, vmem_limit_bytes=VMEM_LIMIT),
    )(lengths, sources, loss_weight, gains, x, cot, w_qkv, w_out, w_cross, w_in, w_down)


def copy_kernel(count, *refs):
    sources, goals = refs[: count + 1], refs[count + 1 : 2 * count + 2]
    held, gains_own, sems = refs[2 * count + 2 : -2], refs[-2], refs[-1]
    loads = [pltpu.make_async_copy(a, b, sems.at[n]) for n, (a, b) in enumerate(zip(sources, held))]
    stores = [
        pltpu.make_async_copy(a, b, sems.at[count + 1 + n]) for n, (a, b) in enumerate(zip((*held[:count], gains_own), goals))
    ]
    order = [count, *range(count)]
    for n in order:
        loads[n].start()
    for n in order:
        loads[n].wait()
        if n == count:
            gains_own[0] = held[count][0 : gains_own.shape[1], 0 : gains_own.shape[2]]
        stores[n].start()
    for store in stores:
        store.wait()


def copied(arrays, gains, gains_shape):
    count = len(arrays)
    return pl.pallas_call(
        partial(copy_kernel, count),
        out_shape=[jax.ShapeDtypeStruct(a.shape, a.dtype) for a in arrays] + [jax.ShapeDtypeStruct(gains_shape, F32)],
        in_specs=[ANY] * (count + 1),
        out_specs=[ANY] * (count + 1),
        scratch_shapes=[pltpu.VMEM(a.shape, a.dtype) for a in (*arrays, gains)]
        + [pltpu.VMEM(gains_shape, F32), pltpu.SemaphoreType.DMA((2 * count + 2,))],
        name="outputs",
    )(*arrays, gains)


def shifted(block, axis, distance):
    devices = range(lax.axis_size(axis))
    route = [(i - distance, i) for i in devices if i - distance in devices]
    return lax.ppermute(block, axis, route)


def plain_product(a, b):
    return jnp.dot(a, b, preferred_element_type=jnp.float32)


def plain_split_heads(v):
    return v.reshape(v.shape[0], HEADS, -1)


def plain_norm_forward(h, norm_gain):
    inv_root = lax.rsqrt(jnp.mean(h * h, axis=-1, keepdims=True) + EPS)
    return (h * inv_root * norm_gain.astype(jnp.float32), inv_root)


def plain_norm_back(d_normed, h, inv_root, norm_gain):
    scaled = h * inv_root
    d_gain = jnp.sum(d_normed * scaled, axis=0)
    inner = d_normed * norm_gain.astype(jnp.float32)
    d_input = inv_root * (inner - scaled * jnp.mean(inner * scaled, axis=-1, keepdims=True))
    return (d_input, d_gain)


def plain_score_block(q, k, key_mask):
    scores = jnp.einsum(
        "qhd,khd->hqk", plain_split_heads(q), plain_split_heads(k), preferred_element_type=jnp.float32
    ) * HEAD_DIM ** (-0.5)
    if key_mask is not None:
        scores = jnp.where(key_mask[None], scores, NEG)
    return scores


def plain_attend_forward(q, k, v, key_mask):
    scores = plain_score_block(q, k, key_mask)
    highest = jnp.max(scores, axis=-1, keepdims=True)
    expo = jnp.exp(scores - highest)
    total = jnp.sum(expo, axis=-1, keepdims=True)
    weights = (expo / total).astype(jnp.bfloat16)
    output = jnp.einsum("hqk,khd->qhd", weights, plain_split_heads(v), preferred_element_type=jnp.float32)
    return (output.reshape(q.shape[0], -1), highest + jnp.log(total))


def plain_attend_back(q, k, v, key_mask, log_total, d_out):
    scores = plain_score_block(q, k, key_mask)
    probs = jnp.exp(scores - log_total)
    heads_dout = plain_split_heads(d_out)
    d_value = jnp.einsum(
        "hqk,qhd->khd", probs.astype(jnp.bfloat16), heads_dout, preferred_element_type=jnp.float32
    )
    d_probs = jnp.einsum(
        "qhd,khd->hqk", heads_dout, plain_split_heads(v), preferred_element_type=jnp.float32
    )
    centre = jnp.sum(probs * d_probs, axis=-1, keepdims=True)
    d_scores = (probs * (d_probs - centre)).astype(jnp.bfloat16)
    d_query = jnp.einsum(
        "hqk,khd->qhd", d_scores, plain_split_heads(k), preferred_element_type=jnp.float32
    ) * HEAD_DIM ** (-0.5)
    d_key = jnp.einsum(
        "hqk,qhd->khd", d_scores, plain_split_heads(q), preferred_element_type=jnp.float32
    ) * HEAD_DIM ** (-0.5)
    rows_query = q.shape[0]
    rows_key = k.shape[0]
    return (
        d_query.reshape(rows_query, -1),
        d_key.reshape(rows_key, -1),
        d_value.reshape(rows_key, -1),
    )


def plain_attention_forward(h, norm_gain, w_qkv, w_out, key_mask):
    normed, inv_root = plain_norm_forward(h, norm_gain)
    normed_low = normed.astype(jnp.bfloat16)
    joined = plain_product(normed_low, w_qkv).astype(jnp.bfloat16)
    q, k, v = jnp.split(joined, 3, axis=1)
    output, log_total = plain_attend_forward(q, k, v, key_mask)
    output_low = output.astype(jnp.bfloat16)
    return (normed_low, inv_root, joined, output_low, log_total, plain_product(output_low, w_out))


def plain_attention_back(d_h, h, saved, norm_gain, w_qkv, w_out, key_mask):
    normed_low, inv_root, joined, output_low, log_total, unused = saved
    d_low = d_h.astype(jnp.bfloat16)
    d_wout = plain_product(output_low.T, d_low)
    d_output = plain_product(d_low, w_out.T).astype(jnp.bfloat16)
    q, k, v = jnp.split(joined, 3, axis=1)
    d_query, d_key, d_value = plain_attend_back(q, k, v, key_mask, log_total, d_output)
    d_joined = jnp.concatenate([d_query, d_key, d_value], axis=1).astype(jnp.bfloat16)
    d_wqkv = plain_product(normed_low.T, d_joined)
    d_normed = plain_product(d_joined, w_qkv.T)
    d_input, d_gain = plain_norm_back(d_normed, h, inv_root, norm_gain)
    return (d_input, d_gain, d_wqkv, d_wout)


def plain_mlp_forward(h, norm_gain, w_in, w_down):
    normed, inv_root = plain_norm_forward(h, norm_gain)
    normed_low = normed.astype(jnp.bfloat16)
    joined = plain_product(normed_low, w_in)
    gate, upper = jnp.split(joined, 2, axis=1)
    hidden_low = (jax.nn.gelu(gate, approximate=True) * upper).astype(jnp.bfloat16)
    return (normed_low, inv_root, joined, hidden_low, plain_product(hidden_low, w_down))


def plain_mlp_back(d_h, h, saved, norm_gain, w_in, w_down):
    normed_low, inv_root, joined, hidden_low, unused = saved
    d_low = d_h.astype(jnp.bfloat16)
    d_wdown = plain_product(hidden_low.T, d_low)
    d_hidden = plain_product(d_low, w_down.T)
    gate, upper = jnp.split(joined, 2, axis=1)
    active, active_back = jax.vjp(partial(jax.nn.gelu, approximate=True), gate)
    d_gate = active_back(d_hidden * upper)[0]
    d_upper = d_hidden * active
    d_joined = jnp.concatenate([d_gate, d_upper], axis=1).astype(jnp.bfloat16)
    d_win = plain_product(normed_low.T, d_joined)
    d_normed = plain_product(d_joined, w_in.T)
    d_input, d_gain = plain_norm_back(d_normed, h, inv_root, norm_gain)
    return (d_input, d_gain, d_win, d_wdown)


def encoder_forward(weights, source):
    gains, w_qkv, w_out, w_cross, w_in, w_down = weights
    inputs = source.astype(jnp.float32)
    attn_saved = plain_attention_forward(inputs, gains[0], w_qkv, w_out, None)
    middle = inputs + attn_saved[-1]
    mlp_saved = plain_mlp_forward(middle, gains[1], w_in, w_down)
    final = middle + mlp_saved[-1]
    normed, inv_root = plain_norm_forward(final, gains[2])
    memory = normed.astype(jnp.bfloat16)
    key_value = plain_product(memory, w_cross).astype(jnp.bfloat16)
    return (inputs, attn_saved, middle, mlp_saved, final, inv_root, memory, key_value)


def encoder_front(weights, source):
    saved = encoder_forward(weights, source)
    return (saved[7], saved[6])


def encoder_back_saved(weights, saved, d_keyvalue):
    gains, w_qkv, w_out, w_cross, w_in, w_down = weights
    inputs, attn_saved, middle, mlp_saved, final, inv_root, memory, key_value = saved
    d_wcross = plain_product(memory.T, d_keyvalue)
    d_memory = plain_product(d_keyvalue, w_cross.T)
    d_final, gain_last = plain_norm_back(d_memory, final, inv_root, gains[2])
    d_part, gain_mlp, d_win, d_wdown = plain_mlp_back(d_final, middle, mlp_saved, gains[1], w_in, w_down)
    d_middle = d_final + d_part
    d_first, gain_attn, d_wqkv, d_wout = plain_attention_back(
        d_middle, inputs, attn_saved, gains[0], w_qkv, w_out, None
    )
    grads = (jnp.stack([gain_attn, gain_mlp, gain_last]), d_wqkv, d_wout, d_wcross, d_win, d_wdown)
    return (d_middle + d_first, grads)


def encoder_back(weights, source, d_keyvalue):
    return encoder_back_saved(weights, encoder_forward(weights, source), d_keyvalue)


def decoder_pass(weights, source, key_value, weight_cot, length, factor):
    gains, w_qkv, w_out, w_cross, w_in, w_down = weights
    width = source.shape[1]
    inputs = source.astype(jnp.float32)
    position = jnp.arange(inputs.shape[0], dtype=jnp.int32)
    is_valid = position < length
    key_mask = (position[None, :] <= position[:, None]) & is_valid[None, :]
    attn_saved = plain_attention_forward(inputs, gains[0], w_qkv, w_out, key_mask)
    middle = inputs + attn_saved[-1]
    normed, inv_root = plain_norm_forward(middle, gains[1])
    normed_low = normed.astype(jnp.bfloat16)
    w_query = w_cross[:, :width]
    w_back = w_cross[:, width:]
    queries = plain_product(normed_low, w_query).astype(jnp.bfloat16)
    mem_keys = key_value[:, :width]
    mem_values = key_value[:, width:]
    cross_out, cross_total = plain_attend_forward(queries, mem_keys, mem_values, None)
    cross_low = cross_out.astype(jnp.bfloat16)
    after = middle + plain_product(cross_low, w_back)
    mlp_saved = plain_mlp_forward(after, gains[2], w_in, w_down)
    final = after + mlp_saved[-1]
    d_final = jnp.where(is_valid[:, None], weight_cot.astype(jnp.float32) * factor, 0.0)
    d_part, gain_mlp, d_win, d_wdown = plain_mlp_back(d_final, after, mlp_saved, gains[2], w_in, w_down)
    d_after = d_final + d_part
    d_low = d_after.astype(jnp.bfloat16)
    d_wback = plain_product(cross_low.T, d_low)
    d_cross = plain_product(d_low, w_back.T).astype(jnp.bfloat16)
    d_query, d_key, d_value = plain_attend_back(queries, mem_keys, mem_values, None, cross_total, d_cross)
    d_query_low = d_query.astype(jnp.bfloat16)
    d_wquery = plain_product(normed_low.T, d_query_low)
    d_normed = plain_product(d_query_low, w_query.T)
    d_norm_in, gain_cross = plain_norm_back(d_normed, middle, inv_root, gains[1])
    d_middle = d_after + d_norm_in
    d_keyvalue = jnp.concatenate([d_key, d_value], axis=1).astype(jnp.bfloat16)
    d_first, gain_attn, d_wqkv, d_wout = plain_attention_back(
        d_middle, inputs, attn_saved, gains[0], w_qkv, w_out, key_mask
    )
    grads = (
        jnp.stack([gain_attn, gain_cross, gain_mlp]),
        d_wqkv,
        d_wout,
        jnp.concatenate([d_wquery, d_wback], axis=1),
        d_win,
        d_wdown,
    )
    return (final.astype(jnp.bfloat16), d_middle + d_first, d_keyvalue, grads)


def on_section(flag, work, operands):

    def run_work(values):
        return work(*values)

    def skip_work(values):
        return jax.tree.map(jnp.zeros_like, work(*values))

    return lax.cond(flag, run_work, skip_work, operands)


def plain_body(
    block_in,
    cotangent,
    lengths,
    sources,
    loss_weight,
    gains,
    qkv_weight,
    out_weight,
    cross_weight,
    in_weight,
    down_weight,
):
    is_encoder = lax.axis_index("section") == 0
    is_decoder = jnp.logical_not(is_encoder)
    wide = lax.axis_size("dp")
    gathered = (
        lax.all_gather(gains, "dp", axis=2, tiled=True),
        lax.all_gather(qkv_weight, "dp", axis=1, tiled=True),
        lax.all_gather(out_weight, "dp", axis=1, tiled=True),
        lax.all_gather(cross_weight, "dp", axis=1, tiled=True),
        lax.all_gather(in_weight, "dp", axis=1, tiled=True),
        lax.all_gather(down_weight, "dp", axis=1, tiled=True),
    )
    weights = tuple((w[0] for w in gathered))
    onehot = (sources[:, None] == jnp.arange(3, dtype=jnp.int32)[None, :]).astype(jnp.float32)
    counts = lax.psum(jnp.sum(onehot * lengths[:, None].astype(jnp.float32), axis=0), "dp")
    own_count = jnp.sum(onehot * counts[None, :], axis=1)
    own_weight = jnp.sum(onehot * loss_weight[None, :].astype(jnp.float32), axis=1)
    scale = own_weight * (lengths.shape[0] * wide * block_in.shape[2] / 3.0) / own_count

    def step(carry, item):
        source, weight_cot, length, factor = item
        key_value, memory = on_section(is_encoder, encoder_front, (weights, source))
        received = shifted(key_value, "section", 1)
        decoded, table_grad, d_keyvalue, dec_grads = on_section(
            is_decoder, decoder_pass, (weights, source, received, weight_cot, length, factor)
        )
        returned = shifted(d_keyvalue, "section", -1)
        plot_grad, enc_grads = on_section(is_encoder, encoder_back, (weights, source, returned))
        grads = tuple((a + b for a, b in zip(dec_grads, enc_grads)))
        carry = tuple((a + b for a, b in zip(carry, grads)))
        return (carry, (memory + decoded, plot_grad + table_grad))

    start = tuple((jnp.zeros(w.shape, jnp.float32) for w in weights))
    carry, (outputs, input_grads) = lax.scan(step, start, (block_in[0], cotangent, lengths, scale))
    gain_total, qkv_total, out_total, cross_sum, in_total, down_total = carry
    reduced = (
        lax.psum_scatter(gain_total[None], "dp", scatter_dimension=2, tiled=True),
        lax.psum_scatter(qkv_total[None], "dp", scatter_dimension=1, tiled=True),
        lax.psum_scatter(out_total[None], "dp", scatter_dimension=1, tiled=True),
        lax.psum_scatter(cross_sum[None], "dp", scatter_dimension=1, tiled=True),
        lax.psum_scatter(in_total[None], "dp", scatter_dimension=1, tiled=True),
        lax.psum_scatter(down_total[None], "dp", scatter_dimension=1, tiled=True),
    )
    return (
        outputs[None],
        input_grads[None],
        reduced[0],
        reduced[1],
        reduced[2],
        reduced[3],
        reduced[4],
        reduced[5],
    )


def tiled_body(
    block_in, cotangent, lengths, sources, loss_weight, gains, qkv_weight, out_weight, cross_weight, in_weight, down_weight
):
    wide = lax.axis_size("dp")
    pairs, seq, width = block_in.shape[1:]
    x, cot = block_in.reshape(pairs * seq, width), cotangent.reshape(pairs * seq, width)
    results = run_step(
        wide, seq, lengths, sources, loss_weight, gains[0], x, cot,
        qkv_weight[0], out_weight[0], cross_weight[0], in_weight[0], down_weight[0],
    )
    block_out, input_grad, down, inner, cross, out, qkv, gains_sum = copied(results[-8:-1], results[-1], gains.shape)
    return (
        block_out.reshape(block_in.shape),
        input_grad.reshape(block_in.shape),
        gains_sum,
        qkv[None],
        out[None],
        cross[None],
        inner[None],
        down[None],
    )


def solution(mesh):
    in_specs = (
        P("section", "dp", None, None),
        P("dp", None, None),
        P("dp"),
        P("dp"),
        P(),
        P("section", None, "dp"),
        P("section", "dp", None),
        P("section", "dp", None),
        P("section", "dp", None),
        P("section", "dp", None),
        P("section", "dp", None),
    )
    out_specs = (
        P("section", "dp", None, None),
        P("section", "dp", None, None),
        P("section", None, "dp"),
        P("section", "dp", None),
        P("section", "dp", None),
        P("section", "dp", None),
        P("section", "dp", None),
        P("section", "dp", None),
    )

    def body(*args):
        shards = args[6:]
        tiled = args[5].shape[2] <= 128 and all(w.shape[1] % 16 == 0 for w in shards)
        return (tiled_body if tiled else plain_body)(*args)

    return jax.shard_map(body, mesh=mesh, in_specs=in_specs, out_specs=out_specs, check_vma=False)
```
